32 devices in a mesh: dp: 8 (over z, x), tensor: 4 (over y, core).
Axes of the slice: x: 2, y: 2, z: 4, core: 2. Of those that a mesh axis runs over, the one named last changes fastest.
Arguments:
- tokens: bfloat16 [32, 512, 512], P('dp', 'tensor'), may hold values from -6 to 6
- valid: int32 [32], P('dp'), may hold values from 2 to 8, as said below
- w_qkv: bfloat16 [512, 1536], P(None, ('dp', 'tensor')), may hold values from -0.25 to 0.25
- w_out: bfloat16 [512, 512], P(None, ('dp', 'tensor')), may hold values from -1 to 1
- vectors: bfloat16 [12, 512], P(None, ('dp', 'tensor')), may hold values from -1.5 to 1.5, as said below
- w_up: bfloat16 [512, 2048], P('dp', 'tensor'), may hold values from -0.25 to 0.25
- w_down: bfloat16 [2048, 512], P('tensor', 'dp'), may hold values from -0.25 to 0.25
- cotangent: bfloat16 [32, 512, 512], P('dp', 'tensor'), may hold values from -6 to 6
Outputs:
- output: bfloat16 [32, 512, 512], P('dp', 'tensor')
- grad_tokens: float32 [32, 512, 512], P('dp', 'tensor')
- grad_w_qkv: float32 [512, 1536], P(None, ('dp', 'tensor'))
- grad_w_out: float32 [512, 512], P(None, ('dp', 'tensor'))
- grad_vectors: float32 [12, 512], P(None, ('dp', 'tensor'))
- grad_w_up: float32 [512, 2048], P('dp', 'tensor')
- grad_w_down: float32 [2048, 512], P('tensor', 'dp')
The draws below stay inside these ranges and needn't reach their ends.
Inputs may be any that keep to these rules, and one draw needn't show every extreme that they name: In every group of 4 consecutive clips one clip is valid over all 64 time rows. `vectors`: rows 0 and 5 lie near one, the others about zero.
All inputs are finite; a program needn't handle non-finite values.
Results may differ from the reference program's by a relative error of at most 0.014.
Values may be sent and summed in bfloat16 or wider, within the bound.
No kernel may reach another device: no remote copies, remote signals or barrier semaphores. Data moves between devices by JAX's collectives and lax.ppermute only.
A program may use at most 128 MiB of HBM per device.

```python
import jax
import jax.numpy as jnp
from jax import lax

D = 512
FF = 2048
HEADS = 16
TIME_ROWS = 64
FREQ = 8
WINDOW = 4
SHIFT = 2
ROW_UNIT = 8
PATCHES = 512
CLIPS_DEV = 4
CLIPS = 32


def draw_vectors(key, part):
    key = jax.random.fold_in(key, 11)
    gain_key, bias_key = jax.random.split(key)
    row_total = 8 + FF // D
    gains = 1.0 + 0.3 * jax.random.uniform(gain_key, (row_total, D), jnp.float32, -1.0, 1.0)
    biases = jnp.clip(0.3 * jax.random.normal(bias_key, (row_total, D), jnp.float32), -1.5, 1.5)
    row_index = jnp.arange(row_total)[:, None]
    is_gain = (row_index == 0) | (row_index == 5)
    return jnp.where(is_gain, gains, biases).astype(jnp.bfloat16)


def draw_valid(key, part):
    key = jax.random.fold_in(key, 12)
    count_key, place_key = jax.random.split(key)
    most_count = TIME_ROWS // ROW_UNIT
    counts = jax.random.randint(count_key, (CLIPS,), 2, most_count + 1)
    groups = CLIPS // CLIPS_DEV
    places = jax.random.randint(place_key, (groups,), 0, CLIPS_DEV)
    clip_index = jnp.arange(CLIPS)
    full_clip = clip_index % CLIPS_DEV == jnp.repeat(places, CLIPS_DEV)
    return jnp.where(full_clip, most_count, counts).astype(jnp.int32)


def block_levels(key, shape, cuts, smallest, top_value):
    def one(position, blocks):
        heights = jax.random.uniform(jax.random.fold_in(jax.random.fold_in(key, 6), position), (blocks,), jnp.float32, smallest / len(cuts), top_value / len(cuts))
        return jnp.repeat(jnp.exp(heights), shape[position] // blocks).reshape((-1,) + (1,) * (len(shape) - position - 1))

    factor_of = one(*cuts[0])
    for cut in cuts[1:]:
        factor_of = factor_of * one(*cut)
    return factor_of


def gaussian(own_key, dims, scale, reach, cuts=(), dtype=jnp.bfloat16):
    values = scale * jax.random.normal(own_key, dims, jnp.float32)
    if cuts:
        values = values * block_levels(own_key, dims, cuts, -0.22, 0.18)
    return jnp.clip(values, -reach, reach).astype(dtype)


def setup_inputs(seed: int = 0) -> dict:
    keys = jax.random.split(jax.random.key(seed), 9)
    tokens = gaussian(keys[0], (CLIPS, PATCHES, D), 1.0, 6.0, ((0, 8), (1, 4)))
    valid = draw_valid(jax.random.fold_in(keys[8], 71), 0)
    w_qkv = gaussian(keys[2], (D, 3 * D), D ** -0.5, 0.25, ((1, 32),))
    w_out = gaussian(keys[3], (D, D), (D // 16) ** -0.5, 1.0, ((1, 32),))
    vectors = draw_vectors(jax.random.fold_in(keys[8], 71), 0)
    w_up = gaussian(keys[5], (D, FF), D ** -0.5, 0.25, ((0, 8), (1, 4)))
    w_down = gaussian(keys[6], (FF, D), (FF // 4) ** -0.5, 0.25, ((0, 4), (1, 8)))
    cotangent = gaussian(keys[7], (CLIPS, PATCHES, D), 1.0, 6.0, ((0, 8), (1, 4)))
    return {"tokens": tokens, "valid": valid, "w_qkv": w_qkv, "w_out": w_out, "vectors": vectors, "w_up": w_up, "w_down": w_down, "cotangent": cotangent}


@jax.custom_vjp
def low(v):
    return lax.optimization_barrier(v.astype(jnp.bfloat16)).astype(jnp.float32)

@jax.custom_vjp
def low_back(v):
    return v

def low_keep(v):
    return (low(v), None)

def low_pass(kept, grad):
    return (grad,)

def back_keep(v):
    return (v, None)

def back_low(kept, grad):
    return (low(grad),)
low.defvjp(low_keep, low_pass)
low_back.defvjp(back_keep, back_low)
highest = lax.Precision.HIGHEST
norm_eps = 1e-06
masked_score = -1000000000.0

def layer_norm(values, gain, shift_row):
    row_mean = lax.optimization_barrier(jnp.mean(values, axis=-1, keepdims=True))
    centred = values - row_mean
    variance = lax.optimization_barrier(jnp.mean(centred * centred, axis=-1, keepdims=True))
    return centred * lax.rsqrt(variance + norm_eps) * gain + shift_row

def split_windows(values):
    group_count, row_count, col_count, channels = values.shape
    shaped = values.reshape(group_count, row_count // WINDOW, WINDOW, col_count // WINDOW, WINDOW, channels)
    shaped = shaped.transpose(0, 1, 3, 2, 4, 5)
    return shaped.reshape(group_count, row_count // WINDOW * (col_count // WINDOW), WINDOW * WINDOW, channels)

def join_windows(values, row_count, col_count):
    group_count = values.shape[0]
    channels = values.shape[-1]
    shaped = values.reshape(group_count, row_count // WINDOW, col_count // WINDOW, WINDOW, WINDOW, channels)
    shaped = shaped.transpose(0, 1, 3, 2, 4, 5)
    return shaped.reshape(group_count, row_count, col_count, channels)

def window_attention(projected, rows_valid):
    group_count = projected.shape[0]
    head_size = D // HEADS
    clip_grid = projected.reshape(group_count, TIME_ROWS, FREQ, 3 * D)
    padded = jnp.pad(clip_grid, ((0, 0), (SHIFT, SHIFT), (SHIFT, SHIFT), (0, 0)))
    time_index = jnp.arange(TIME_ROWS + 2 * SHIFT) - SHIFT
    freq_index = jnp.arange(FREQ + 2 * SHIFT) - SHIFT
    time_ok = (time_index[None, :] >= 0) & (time_index[None, :] < rows_valid[:, None] * ROW_UNIT)
    freq_ok = (freq_index >= 0) & (freq_index < FREQ)
    key_ok = (time_ok[:, :, None] & freq_ok[None, None, :]).astype(jnp.int32)[..., None]
    key_windows = split_windows(key_ok)[..., 0] == 1
    windows = split_windows(padded)
    head_shape = windows.shape[:3] + (HEADS, head_size)
    query_heads = windows[..., :D].reshape(head_shape)
    key_heads = windows[..., D:2 * D].reshape(head_shape)
    value_heads = windows[..., 2 * D:].reshape(head_shape)
    scores = low_back(jnp.einsum('gwqhe,gwkhe->gwhqk', query_heads, key_heads, precision=highest) * head_size ** (-0.5))
    scores = jnp.where(key_windows[:, :, None, None, :], scores, masked_score)
    attention_weights = low(jax.nn.softmax(scores, axis=-1))
    mixed_heads = jnp.einsum('gwhqk,gwkhe->gwqhe', attention_weights, value_heads, precision=highest)
    mixed_heads = mixed_heads.reshape(windows.shape[:3] + (D,))
    joined = join_windows(mixed_heads, TIME_ROWS + 2 * SHIFT, FREQ + 2 * SHIFT)
    return joined[:, SHIFT:SHIFT + TIME_ROWS, SHIFT:SHIFT + FREQ].reshape(group_count, PATCHES, D)

def forward(tokens, w_qkv, w_out, vectors, w_up, w_down, rows_valid):
    normed = low(layer_norm(tokens, vectors[0], vectors[1]))
    qkv_bias = jnp.concatenate([vectors[2], jnp.zeros_like(vectors[2]), vectors[3]])
    projected = low(low_back(jnp.dot(normed, w_qkv, precision=highest) + qkv_bias))
    mixed_heads = low(low_back(window_attention(projected, rows_valid)))
    attended = low_back(jnp.dot(mixed_heads, w_out, precision=highest) + vectors[4])
    residual = tokens + attended
    second = low(layer_norm(residual, vectors[5], vectors[6]))
    up_bias = vectors[8:].reshape(FF)
    pre_act = low_back(jnp.dot(second, w_up, precision=highest) + up_bias)
    hidden = low(jax.nn.gelu(pre_act, approximate=False))
    branch = low_back(jnp.dot(hidden, w_down, precision=highest) + vectors[7])
    time_row = jnp.arange(PATCHES) // FREQ
    keep = (time_row[None, :] < rows_valid[:, None] * ROW_UNIT).astype(jnp.float32)
    return (residual + branch) * keep[:, :, None]

def reference(tokens, valid, w_qkv, w_out, vectors, w_up, w_down, cotangent):
    weights = (w_qkv.astype(jnp.float32), w_out.astype(jnp.float32), vectors.astype(jnp.float32), w_up.astype(jnp.float32), w_down.astype(jnp.float32))
    group_size = 8 if CLIPS % 8 == 0 else 1
    group_count = CLIPS // group_size
    token_groups = tokens.astype(jnp.float32).reshape(group_count, group_size, PATCHES, D)
    cot_groups = cotangent.astype(jnp.float32).reshape(group_count, group_size, PATCHES, D)
    valid_groups = valid.reshape(group_count, group_size)

    def one_group(totals, scan_items):
        token_part, cot_part, valid_part = scan_items

        def local_forward(token_in, *params):
            return forward(token_in, *params, valid_part)
        result, pullback = jax.vjp(local_forward, token_part, *weights)
        gradients = pullback(cot_part)
        summed = tuple((total_arr + grad_arr for total_arr, grad_arr in zip(totals, gradients[1:])))
        return (summed, (result.astype(jnp.bfloat16), gradients[0]))
    initial = tuple((jnp.zeros_like(weight_arr) for weight_arr in weights))
    totals, (outputs, token_grads) = lax.scan(one_group, initial, (token_groups, cot_groups, valid_groups))
    return (outputs.reshape(CLIPS, PATCHES, D), token_grads.reshape(CLIPS, PATCHES, D), totals[0], totals[1], totals[2], totals[3], totals[4])
```

```python
import functools

import jax
import jax.numpy as jnp
from jax import lax
from jax.experimental import pallas as pl
from jax.experimental.pallas import tpu as pltpu
from jax.sharding import PartitionSpec as P

D = 512
FF = 2048
HEADS = 16
HEAD = D // HEADS
FREQ = 8
WINDOW = 4
SHIFT = 2
ROW_UNIT = 8

EPS = 1e-06
MASKED = -1000000000.0
SCALE = HEAD ** (-0.5)
INV_ROOT_TWO = 0.7071067811865476
INV_ROOT_TAU = 0.3989422804014327

BOTH = ("dp", "tensor")
SLOTS = 32
NEAR = SLOTS // 2
PIECE = 4
QKV_ROWS = 3 * D // SLOTS
OUT_ROWS = D // SLOTS
A_ROWS = QKV_ROWS + OUT_ROWS
CHUNKS = FF // D
UP_ROWS = D * CHUNKS // SLOTS
B_ROWS = OUT_ROWS + UP_ROWS

CLIPS = 4
OWN = 128
EDGE = 16
OWN_ALL = CLIPS * OWN
ROWS = OWN_ALL + CLIPS * 2 * EDGE
BAND = 2 * EDGE
BANDS = OWN // BAND + 1
HALF = D // 2
HALF_HEADS = HALF // HEAD
STEP = 128
SUB = 32

bf16 = jnp.bfloat16
f32 = jnp.float32


def nn(a, b):
    return lax.dot_general(a, b, (((1,), (0,)), ((), ())), preferred_element_type=f32)


def nt(a, b):
    return lax.dot_general(a, b, (((1,), (1,)), ((), ())), preferred_element_type=f32)


def tn(a, b):
    return lax.dot_general(a, b, (((0,), (0,)), ((), ())), preferred_element_type=f32)


def rows_at(start, size):
    return pl.ds(pl.multiple_of(start, size), size)


def norm_parts(values):
    mean = jnp.mean(values, axis=-1, keepdims=True)
    centred = values - mean
    variance = jnp.mean(centred * centred, axis=-1, keepdims=True)
    inverse = lax.rsqrt(variance + EPS)
    return centred * inverse, inverse


def norm_back(grad, scaled, inverse, gain):
    grad_hat = grad * gain
    centre = jnp.mean(grad_hat, axis=-1, keepdims=True)
    slope = jnp.mean(grad_hat * scaled, axis=-1, keepdims=True)
    return inverse * (grad_hat - centre - scaled * slope)


def band_rows(band):
    clip = band // BANDS
    place = band % BANDS
    first = jnp.where(place == 0, OWN_ALL + clip * BAND, clip * OWN + place * BAND - EDGE)
    last = jnp.where(place == BANDS - 1, OWN_ALL + clip * BAND + EDGE, clip * OWN + place * BAND)
    return rows_at(first, EDGE), rows_at(last, EDGE)


def load_band(ref, places, columns):
    return jnp.concatenate([ref[places[0], columns], ref[places[1], columns]], axis=0)


def find(pieces, slot):
    size = pieces[0].shape[0]
    return pieces[slot // size], slot % size


def weight_block(owner):
    return rows_at(owner // CHUNKS * UP_ROWS, UP_ROWS), rows_at(owner % CHUNKS * D, D)


def pack_kernel(qkv_ref, vec_ref, out_ref, up_ref, block_ref):
    block_ref[:QKV_ROWS, :] = qkv_ref[...]
    block_ref[QKV_ROWS:A_ROWS, :] = jnp.zeros((OUT_ROWS, D), bf16)
    block_ref[QKV_ROWS:A_ROWS, : vec_ref.shape[1]] = vec_ref[...]
    block_ref[A_ROWS : A_ROWS + OUT_ROWS, :] = out_ref[...]
    block_ref[A_ROWS + OUT_ROWS :, :] = up_ref[...]


def head_lanes():
    row = lax.broadcasted_iota(jnp.int32, (HALF, HALF), 0) // HEAD
    lane = lax.broadcasted_iota(jnp.int32, (HALF, HALF), 1) // HEAD
    return jnp.where(row == lane, 1.0, 0.0)


def by_head(rows, lanes):
    return jnp.concatenate([rows] * HALF_HEADS, axis=0) * lanes


def flip_heads(wide):
    turned = wide.T
    return jnp.concatenate([turned[head * BAND : (head + 1) * BAND] for head in range(HALF_HEADS)], axis=1)


def attend_kernel(
    own_ref, keep_ref, x_ref, *refs,
):
    a_refs, refs = refs[:-10], refs[-10:]
    proj_ref, prob_ref, mixed_ref, scaled_ref, wqkv_ref, vec_ref, column_vec, lanes_ref, pair_ref, normed_ref = refs
    for slot in range(SLOTS):
        owner = own_ref[slot]
        a_ref, held = find(a_refs, slot)
        wqkv_ref[rows_at(owner * QKV_ROWS, QKV_ROWS), :] = a_ref[held, :QKV_ROWS, :]
        column_vec[rows_at(owner * OUT_ROWS, OUT_ROWS), :] = a_ref[held, QKV_ROWS:A_ROWS, :128].astype(f32)
    vec_ref[...] = column_vec[...].T[:16, :]
    lanes_ref[...] = head_lanes().astype(bf16)
    key_group = (lax.broadcasted_iota(jnp.int32, (BAND, HALF), 0) % FREQ + SHIFT) // WINDOW
    query_group = (lax.broadcasted_iota(jnp.int32, (BAND, HALF), 1) % FREQ + SHIFT) // WINDOW
    pair_ref[...] = jnp.where(key_group == query_group, 1.0, 0.0)

    def scale(step, carry):
        here = rows_at(step * SUB, SUB)
        scaled, _ = norm_parts(x_ref[here, :].astype(f32))
        scaled_ref[here, :] = scaled.astype(bf16)
        normed_ref[here, :] = (scaled * vec_ref[0:1, :] + vec_ref[1:2, :]).astype(bf16)
        return carry

    lax.fori_loop(0, ROWS // SUB, scale, 0, unroll=4)
    for part in range(3):
        columns = slice(part * D, (part + 1) * D)
        part_out = nt(normed_ref[...], wqkv_ref[columns, :])
        if part != 1:
            bias = 2 if part == 0 else 3
            part_out = part_out + vec_ref[bias : bias + 1, :]
        proj_ref[:, columns] = part_out.astype(bf16)

    def score(band, carry):
        places = band_rows(band)
        key_ok = load_band(keep_ref, places, slice(None))
        key_ok = jnp.concatenate([key_ok, key_ok], axis=1) * pair_ref[...] > 0.5
        for half in range(2):
            low = half * HALF
            query = load_band(proj_ref, places, slice(low, low + HALF))
            key = load_band(proj_ref, places, slice(D + low, D + low + HALF))
            scores = nt(key, by_head(query, lanes_ref[...])) * SCALE
            scores = jnp.where(key_ok, scores, MASKED)
            exponent = jnp.exp(scores - jnp.max(scores, axis=0, keepdims=True))
            prob_ref[band, half] = exponent / jnp.sum(exponent, axis=0, keepdims=True)
        return carry

    lax.fori_loop(0, CLIPS * BANDS, score, 0, unroll=10)

    def mix(band, carry):
        places = band_rows(band)
        for half in range(2):
            low = half * HALF
            value = load_band(proj_ref, places, slice(2 * D + low, 2 * D + low + HALF))
            probs = flip_heads(prob_ref[band, half].astype(bf16))
            mixed = nn(probs, by_head(value, lanes_ref[...])).astype(bf16)
            mixed_ref[places[0], low : low + HALF] = mixed[:EDGE]
            mixed_ref[places[1], low : low + HALF] = mixed[EDGE:]
        return carry

    lax.fori_loop(0, CLIPS * BANDS, mix, 0, unroll=10)


def together(*works):
    for _ in range(4):
        for work in works:
            next(work)


def write_grads(own_ref, pieces, block_ref):
    for slot in range(SLOTS):
        grads_ref, held = find(pieces, slot)
        grads_ref[held] = block_ref[weight_block(own_ref[slot])]


def up_kernel(
    own_ref, own_down_ref, keep_ref, cot_ref, x_ref, mixed_ref, vec_ref, *refs,
):
    b_refs, refs = refs[:-14], refs[-14:]
    (
        kept_ref, sent_ref, resid_ref, hid_ref, slope_ref, second_ref, branch_low, up_ref, wout_ref,
        gdown_ref, pre_ref, branch_t, attended_ref, normed_ref,
    ) = refs
    for slot in range(SLOTS):
        owner = own_ref[slot]
        b_ref, held = find(b_refs, slot)
        low = b_ref.shape[1] - B_ROWS
        wout_ref[rows_at(owner * OUT_ROWS, OUT_ROWS), :] = b_ref[held, low : low + OUT_ROWS, :]
        up_ref[weight_block(owner)] = b_ref[held, low + OUT_ROWS :, :]

    attended_ref[...] = nt(mixed_ref[...], wout_ref[...])

    def begin(step, carry):
        here = rows_at(step * SUB, SUB)
        residual = x_ref[here, :].astype(f32) + (attended_ref[here, :] + vec_ref[4:5, :])
        resid_ref[here, :] = residual
        scaled, _ = norm_parts(residual)
        second = (scaled * vec_ref[5:6, :] + vec_ref[6:7, :]).astype(bf16)
        second_ref[here, :] = second
        normed_ref[here, :] = second
        wide = jnp.concatenate([keep_ref[here, :]] * (D // 128), axis=1)
        branch_low[here, :] = (cot_ref[here, :].astype(f32) * wide).astype(bf16)
        return carry

    lax.fori_loop(0, ROWS // SUB, begin, 0, unroll=4)
    branch_t[...] = branch_low[:OWN_ALL, :].T

    def products(chunk):
        for quarter in range(4):
            columns = slice(chunk * D + quarter * 128, chunk * D + (quarter + 1) * 128)
            pre_ref[:, columns] = nn(normed_ref[...], up_ref[:, columns])
            yield

    def slopes(chunk):
        columns = slice(chunk * D, (chunk + 1) * D)
        for step in range(ROWS // 16):
            here = slice(step * 16, step * 16 + 16)
            pre = pre_ref[here, columns] + vec_ref[8 + chunk : 9 + chunk, :]
            phi = 0.5 + 0.5 * lax.erf(pre * INV_ROOT_TWO)
            slope_ref[here, columns] = (phi + pre * (jnp.exp(-0.5 * pre * pre) * INV_ROOT_TAU)).astype(bf16)
            hid_ref[here, columns] = (pre * phi).astype(bf16)
            if step % 10 == 9:
                yield

    def weights(chunk):
        for half in range(2):
            columns = slice(chunk * D + half * HALF, chunk * D + (half + 1) * HALF)
            gdown_ref[:, columns] = nn(branch_t[...], hid_ref[:OWN_ALL, columns]).astype(bf16)
            yield
            yield

    together(products(0))
    together(products(1), slopes(0))
    for chunk in range(2, CHUNKS):
        together(products(chunk), slopes(chunk - 1), weights(chunk - 2))
    together(slopes(CHUNKS - 1), weights(CHUNKS - 2))
    together(weights(CHUNKS - 1))
    write_grads(own_down_ref, (kept_ref, sent_ref), gdown_ref)


def down_kernel(
    own_ref, own_down_ref, hid_ref, slope_ref, second_ref, branch_low, up_ref, *refs,
):
    c_refs, refs = refs[:-10], refs[-10:]
    (
        kept_ref, sent_ref, branch_ref, gsec_ref, colsum_ref,
        down_ref, gup_ref, ghid_ref, gpre_ref, second_t,
    ) = refs
    for slot in range(SLOTS):
        c_ref, held = find(c_refs, slot)
        down_ref[weight_block(own_down_ref[slot])] = c_ref[held]
    second_t[:D, :] = second_ref[:OWN_ALL, :].T
    second_t[D:, :] = jnp.ones((16, OWN_ALL), bf16)

    def products(chunk):
        for half in range(2):
            columns = slice(chunk * D + half * HALF, chunk * D + (half + 1) * HALF)
            ghid_ref[:, columns] = nn(branch_low[...], down_ref[:, columns])
            yield
            yield

    def slopes(chunk):
        columns = slice(chunk * D, (chunk + 1) * D)
        for step in range(ROWS // 16):
            here = slice(step * 16, step * 16 + 16)
            gpre_ref[here, columns] = (ghid_ref[here, columns] * slope_ref[here, columns].astype(f32)).astype(bf16)
            if step % 10 == 9:
                yield

    def weights(chunk):
        for half in range(2):
            columns = slice(chunk * D + half * HALF, chunk * D + (half + 1) * HALF)
            gup = nn(second_t[...], gpre_ref[:OWN_ALL, columns])
            gup_ref[:, columns] = gup[:D].astype(bf16)
            colsum_ref[chunk : chunk + 1, half * HALF : (half + 1) * HALF] = gup[D : D + 1]
            yield
            yield

    together(products(0))
    together(products(1), slopes(0))
    for chunk in range(2, CHUNKS):
        together(products(chunk), slopes(chunk - 1), weights(chunk - 2))
    together(slopes(CHUNKS - 1), weights(CHUNKS - 2))
    together(weights(CHUNKS - 1))
    branch_ref[...] = nt(hid_ref[:OWN_ALL, :], down_ref[...])
    gsec_ref[...] = nt(gpre_ref[...], up_ref[...])
    write_grads(own_ref, (kept_ref, sent_ref), gup_ref)


def finish_kernel(
    own_ref, keep_ref, cot_ref, mixed_ref, resid_ref, branch_ref, gsec_ref, wout_ref, vec_ref,
    out_ref, gres_ref, kept_ref, sent_ref, gmix_ref, sums_ref,
    gatt_ref, gout_ref,
):
    def rows(step, totals):
        here = rows_at(step * SUB, SUB)
        own = jnp.where(step < OWN_ALL // SUB, 1.0, 0.0)
        wide = jnp.concatenate([keep_ref[here, :]] * (D // 128), axis=1)
        scaled, inverse = norm_parts(resid_ref[here, :])
        grad_out = cot_ref[here, :].astype(f32) * wide
        gsec = gsec_ref[here, :]
        gres = grad_out + norm_back(gsec, scaled, inverse, vec_ref[5:6, :])
        gres_ref[here, :] = gres
        gatt = gres.astype(bf16)
        gatt_ref[here, :] = gatt
        parts = (gatt.astype(f32), gsec * scaled, gsec, grad_out.astype(bf16).astype(f32))
        return tuple(t + own * p.reshape(SUB // 8, 8, D).sum(axis=0) for t, p in zip(totals, parts))

    totals = lax.fori_loop(0, ROWS // SUB, rows, (jnp.zeros((8, D), f32),) * 4, unroll=4)
    for place, total in enumerate(totals):
        sums_ref[place : place + 1, :] = jnp.sum(total, axis=0, keepdims=True)
    gmix_ref[...] = nn(gatt_ref[...], wout_ref[...]).astype(bf16)
    gout_ref[...] = nn(gatt_ref[:OWN_ALL, :].T, mixed_ref[:OWN_ALL, :]).astype(bf16)
    for slot in range(SLOTS):
        grads_ref, held = find((kept_ref, sent_ref), slot)
        grads_ref[held] = gout_ref[rows_at(own_ref[slot] * OUT_ROWS, OUT_ROWS), :]

    def outputs(step, carry):
        here = rows_at(step * SUB, SUB)
        wide = jnp.concatenate([keep_ref[here, :]] * (D // 128), axis=1)
        out_ref[here, :] = (wide * (resid_ref[here, :] + (branch_ref[here, :] + vec_ref[7:8, :]))).astype(bf16)
        return carry

    lax.fori_loop(0, OWN_ALL // SUB, outputs, 0, unroll=4)


def back_kernel(
    own_ref, gmix_ref, proj_ref, prob_ref, scaled_ref, wqkv_ref, vec_ref, sums_ref, colsum_ref,
    gproj_ref, kept_ref, sent_ref,
    lanes_ref, gscore_ref, gqkv_ref, gvec_ref, column_vec,
):
    lanes_ref[...] = head_lanes().astype(bf16)

    def score(band, carry):
        places = band_rows(band)
        for half in range(2):
            low = half * HALF
            value = load_band(proj_ref, places, slice(2 * D + low, 2 * D + low + HALF))
            grad = load_band(gmix_ref, places, slice(low, low + HALF))
            probs = prob_ref[band, half]
            grad_probs = nt(value, by_head(grad, lanes_ref[...]))
            row_dot = jnp.sum(probs * grad_probs, axis=0, keepdims=True)
            gscore_ref[band, half] = (probs * (grad_probs - row_dot)).astype(bf16)
        return carry

    lax.fori_loop(0, CLIPS * BANDS, score, 0, unroll=10)

    def mix(band, carry):
        places = band_rows(band)
        for half in range(2):
            low = half * HALF
            query = load_band(proj_ref, places, slice(low, low + HALF))
            key = load_band(proj_ref, places, slice(D + low, D + low + HALF))
            grad = load_band(gmix_ref, places, slice(low, low + HALF))
            grad_scores = gscore_ref[band, half]
            grad_key = nn(grad_scores, by_head(query, lanes_ref[...])) * SCALE
            grad_value = nn(prob_ref[band, half].astype(bf16), by_head(grad, lanes_ref[...]))
            grad_query = nn(flip_heads(grad_scores), by_head(key, lanes_ref[...])) * SCALE
            for part, values in enumerate((grad_query, grad_key, grad_value)):
                values = values.astype(bf16)
                gproj_ref[places[0], part * D + low : part * D + low + HALF] = values[:EDGE]
                gproj_ref[places[1], part * D + low : part * D + low + HALF] = values[EDGE:]
        return carry

    lax.fori_loop(0, CLIPS * BANDS, mix, 0, unroll=10)

    def add_rows(step, totals):
        here = rows_at(step * SUB, SUB)
        return totals + gproj_ref[here, :].astype(f32).reshape(SUB // 8, 8, 3 * D).sum(axis=0)

    totals = lax.fori_loop(0, OWN_ALL // SUB, add_rows, jnp.zeros((8, 3 * D), f32))
    totals = jnp.sum(totals, axis=0, keepdims=True)
    gvec_ref[...] = jnp.zeros_like(gvec_ref)
    gain_grad = jnp.zeros((8, D), f32)
    shift_grad = jnp.zeros((1, D), f32)
    for part in range(3):
        gproj_t = gproj_ref[:OWN_ALL, part * D : (part + 1) * D].T
        product = nn(gproj_t, scaled_ref[:OWN_ALL, :])
        total = totals[:, part * D : (part + 1) * D]
        weight = wqkv_ref[part * D : (part + 1) * D, :]
        both = product * weight.astype(f32)
        gain_grad = gain_grad + both.reshape(D // 8, 8, D).sum(axis=0)
        high = total.astype(bf16)
        rest = (total - high.astype(f32)).astype(bf16)
        shift_grad = shift_grad + nn(high, weight) + nn(rest, weight)
        column = jnp.broadcast_to(total, (8, D)).T[:, 0:1]
        gqkv = product * vec_ref[0:1, :] + column * vec_ref[1:2, :]
        gqkv_ref[part * D : (part + 1) * D, :] = gqkv.astype(bf16)
    gvec_ref[0:1, :] = jnp.sum(gain_grad, axis=0, keepdims=True)
    gvec_ref[1:2, :] = shift_grad
    gvec_ref[2:3, :] = totals[:, :D]
    gvec_ref[3:4, :] = totals[:, 2 * D :]
    gvec_ref[4:8, :] = sums_ref[0:4, :]
    gvec_ref[8:12, :] = colsum_ref[0:4, :]
    column_vec[...] = gvec_ref[...].T.astype(bf16)
    for slot in range(SLOTS):
        owner = own_ref[slot]
        grads_ref, held = find((kept_ref, sent_ref), slot)
        grads_ref[held, :QKV_ROWS, :] = gqkv_ref[rows_at(owner * QKV_ROWS, QKV_ROWS), :]
        grads_ref[held, QKV_ROWS:, :128] = column_vec[rows_at(owner * OUT_ROWS, OUT_ROWS), :]
        grads_ref[held, QKV_ROWS:, 128:] = jnp.zeros((OUT_ROWS, D - 128), bf16)


def token_kernel( gproj_ref, x_ref, gres_ref, wqkv_ref, vec_ref, gtok_ref):
    def rows(step, carry):
        here = rows_at(step * STEP, STEP)
        gnormed = nn(gproj_ref[here, :D], wqkv_ref[:D, :])
        for part in range(1, 3):
            gnormed += nn(gproj_ref[here, part * D : (part + 1) * D], wqkv_ref[part * D : (part + 1) * D, :])
        scaled, inverse = norm_parts(x_ref[here, :].astype(f32))
        gtok_ref[here, :] = gres_ref[here, :] + norm_back(gnormed, scaled, inverse, vec_ref[0:1, :])
        return carry

    lax.fori_loop(0, OWN_ALL // STEP, rows, 0)


def call(kernel, args, outs, scratch, micros, mib):
    smem, vmem = pl.BlockSpec(memory_space=pltpu.SMEM), pl.BlockSpec(memory_space=pltpu.VMEM)
    return pl.pallas_call(
        kernel,
        out_shape=[jax.ShapeDtypeStruct(s, t) for s, t in outs],
        in_specs=[smem if a.dtype == jnp.int32 else vmem for a in args],
        out_specs=[vmem] * len(outs),
        scratch_shapes=[pltpu.VMEM(s, t) for s, t in scratch],
        compiler_params=pltpu.CompilerParams(vmem_limit_bytes=mib * 1024 * 1024),
        cost_estimate=pl.CostEstimate(flops=int(micros * 1.1e9), bytes_accessed=2**20, transcendentals=0),
    )(*args)


def swap(array, mask, other=None):
    count = lax.axis_size("dp") * lax.axis_size("tensor")
    masks = (mask, mask if other is None else other)
    return lax.ppermute(array, BOTH, [(device, device ^ masks[device % 2]) for device in range(count)])


ALONG_Z, ALONG_Y, ALONG_X, CORES = (8, 16, 24), 2, 4, 1
ALONG_XY = (ALONG_Y, ALONG_X, ALONG_Y ^ ALONG_X)


def owners(device, swapped, line_first=True):
    def one(second_core):
        first = ALONG_X if second_core and swapped else ALONG_Y
        plane = [0, first, first ^ ALONG_XY[2], ALONG_XY[2]]
        if line_first:
            return [m ^ o for o in plane for m in (0, *ALONG_Z)]
        line = [0, ALONG_Z[second_core], ALONG_Z[1 - second_core], ALONG_Z[2]]
        return [m ^ o for o in line for m in plane]

    core = device % 2
    first = jnp.where(core == 0, jnp.array(one(0)), jnp.array(one(1)))
    second = jnp.where(core == 0, jnp.array(one(1)), jnp.array(one(0))) ^ CORES
    return (device ^ jnp.concatenate([first, second])).astype(jnp.int32)


def gather(held, phase):
    return [held] + [swap(held, mask) for mask in phase]


def both_cores(pieces):
    return pieces + [swap(piece, CORES) for piece in pieces]


def wide(array):
    return array.astype(f32)


def scatter_sum(pieces, phase):
    total = pieces[0]
    for piece, mask in zip(pieces[1:], phase):
        total = total + wide(swap(piece.astype(bf16), mask))
    return total


def singles(piece):
    return [piece[i : i + 1] for i in range(PIECE)]


def after(array, *others):
    return lax.optimization_barrier((array,) + others)[0]


def neighbours(array, axis_name, width):
    count = lax.axis_size(axis_name)
    up = [(i, i + 1) for i in range(count - 1)]
    low = lax.ppermute(array[..., -width:, :], axis_name, up)
    high = lax.ppermute(array[..., :width, :], axis_name, [(b, a) for a, b in up])
    return low, high


def shards(tokens, valid, w_qkv, w_out, vectors, w_up, w_down, cotangent):
    devices_dp, devices_t = lax.axis_size("dp"), lax.axis_size("tensor")
    near = devices_dp == 8 and devices_t == 4
    rank = lax.axis_index("tensor")

    own_time = jnp.broadcast_to((jnp.arange(OWN) // FREQ)[None], (CLIPS, OWN)).reshape(-1)
    edge_time = jnp.arange(BAND) // FREQ + jnp.where(jnp.arange(BAND) < EDGE, -SHIFT, OWN // FREQ - SHIFT)
    edge_time = jnp.broadcast_to(edge_time[None], (CLIPS, BAND)).reshape(-1)
    time = jnp.concatenate([own_time, edge_time]) + rank * (OWN // FREQ)
    limit = valid * ROW_UNIT
    limit = jnp.concatenate([jnp.repeat(limit, OWN), jnp.repeat(limit, BAND)])
    keep = jnp.where((time >= 0) & (time < limit), 1.0, 0.0).astype(f32)
    keep = jnp.broadcast_to(keep[:, None], (ROWS, 128))

    if near:
        device = lax.axis_index("dp") * devices_t + rank
        own_near, own_far, own_down = owners(device, False), owners(device, True), owners(device, True, False)
        (block,) = call(
            pack_kernel, [w_qkv.T, vectors.T, w_out.T, w_up], [((A_ROWS + B_ROWS, D), bf16)], [], 1, 4,
        )
        edges = neighbours(jnp.stack([tokens, cotangent]), "tensor", EDGE)
        line = gather(block[None], ALONG_Z)
        down = w_down.T[None]
        down = jnp.concatenate([down, swap(down, ALONG_Y, ALONG_X)], axis=0)
        down = [down, swap(down, ALONG_X, ALONG_Y)]
        line, down, edges = lax.optimization_barrier((line, down, edges))
        line, down = jnp.concatenate(line, axis=0), jnp.concatenate(down, axis=0)
        near_pieces = swap(line, ALONG_Y, ALONG_X)
        down = [down, swap(down, ALONG_Z[0], ALONG_Z[1])]
        near_pieces, down = lax.optimization_barrier((near_pieces, down))
        down = jnp.concatenate(down, axis=0)
        near_pieces = jnp.concatenate([line, near_pieces], axis=0)
        a_far = swap(near_pieces[:, :A_ROWS], ALONG_X, ALONG_Y)
        b_far = swap(near_pieces[:, A_ROWS:], ALONG_X, ALONG_Y)
        pieces = both_cores([near_pieces])
        a_pieces = [pieces[0], a_far, pieces[1], swap(a_far, CORES)]
        c_pieces = [down, swap(down, ALONG_Z[1], ALONG_Z[0])]
    else:
        own_near = own_far = own_down = jnp.arange(SLOTS, dtype=jnp.int32)
        edges = neighbours(jnp.stack([tokens, cotangent]), "tensor", EDGE)
        qkv, out, vec = (lax.all_gather(a, BOTH, axis=1, tiled=True).T for a in (w_qkv, w_out, vectors))
        vec = jnp.pad(vec, ((0, 0), (0, D - vec.shape[1])))
        up = lax.all_gather(lax.all_gather(w_up, "dp", axis=0, tiled=True), "tensor", axis=1, tiled=True)
        down = lax.all_gather(lax.all_gather(w_down, "dp", axis=1, tiled=True), "tensor", axis=0, tiled=True).T
        up, down = (
            a.reshape(SLOTS // CHUNKS, UP_ROWS, CHUNKS, D).transpose(0, 2, 1, 3).reshape(SLOTS, UP_ROWS, D)
            for a in (up, down)
        )
        a_slots = jnp.concatenate([a.reshape(SLOTS, -1, D) for a in (qkv, vec)], axis=1)
        b_slots = jnp.concatenate([out.reshape(SLOTS, -1, D), up], axis=1)
        a_pieces, b_pieces, c_pieces = (
            [a[i : i + PIECE] for i in range(0, SLOTS, PIECE)] for a in (a_slots, b_slots, down)
        )

    edges = jnp.concatenate(edges, axis=2).reshape(2, CLIPS * BAND, D)
    x = jnp.concatenate([tokens.reshape(OWN_ALL, D), edges[0]], axis=0)
    cot = jnp.concatenate([cotangent.reshape(OWN_ALL, D), edges[1]], axis=0)
    if near:
        x, *c_pieces = lax.optimization_barrier((x, *c_pieces))
    proj, probs, mixed, scaled, wqkv, vec = call(
        attend_kernel, [own_far, keep, x, *a_pieces],
        [
            ((ROWS, 3 * D), bf16), ((CLIPS * BANDS, 2, BAND, HALF), f32), ((ROWS, D), bf16), ((ROWS, D), bf16),
            ((3 * D, D), bf16), ((16, D), f32),
        ],
        [((D, 128), f32), ((HALF, HALF), bf16), ((BAND, HALF), f32), ((ROWS, D), bf16)],
        6, 20,
    )
    if near:
        b_far = after(b_far, proj)
        b_pieces = [pieces[0], b_far, pieces[1], swap(b_far, CORES)]
    dn_kept, dn_sent, resid, hid, slope, second, branch_low, up_all, wout = call(
        up_kernel, [own_far, own_down, keep, cot, x, mixed, vec, *b_pieces],
        [
            ((NEAR, UP_ROWS, D), bf16), ((NEAR, UP_ROWS, D), bf16), ((ROWS, D), f32), ((ROWS, FF), bf16),
            ((ROWS, FF), bf16), ((ROWS, D), bf16), ((ROWS, D), bf16), ((D, FF), bf16), ((D, D), bf16),
        ],
        [
            ((D, FF), bf16), ((ROWS, FF), f32), ((D, OWN_ALL), bf16), ((ROWS, D), f32), ((ROWS, D), bf16),
        ],
        8, 30,
    )
    if near:
        c_pieces = both_cores(c_pieces)
    up_kept, up_sent, branch, gsec, colsum = call(
        down_kernel, [own_far, own_down, hid, slope, second, branch_low, up_all, *c_pieces],
        [
            ((NEAR, UP_ROWS, D), bf16), ((NEAR, UP_ROWS, D), bf16), ((OWN_ALL, D), f32), ((ROWS, D), f32),
            ((8, D), f32),
        ],
        [
            ((D, FF), bf16), ((D, FF), bf16), ((ROWS, FF), f32), ((ROWS, FF), bf16), ((D + 16, OWN_ALL), bf16),
        ],
        8, 30,
    )
    if near:
        dn_sum = wide(dn_kept) + wide(after(swap(dn_sent, CORES), gsec))
        dn_far = dn_sum[NEAR // 2 :].astype(bf16)
        up_sum = wide(up_kept) + wide(swap(up_sent, CORES))
        up_far = up_sum[NEAR // 2 :].astype(bf16)
        gsec, up_far, dn_far = lax.optimization_barrier((gsec, up_far, dn_far))
    out, gres, go_kept, go_sent, gmix, sums = call(
        finish_kernel, [own_far, keep, cot, mixed, resid, branch, gsec, wout, vec],
        [
            ((OWN_ALL, D), bf16), ((ROWS, D), f32), ((NEAR, OUT_ROWS, D), bf16), ((NEAR, OUT_ROWS, D), bf16),
            ((ROWS, D), bf16), ((8, D), f32),
        ],
        [((ROWS, D), bf16), ((D, D), bf16)],
        5, 16,
    )
    if near:
        go_sum = wide(go_kept) + wide(swap(go_sent, CORES))
        go_far = go_sum[NEAR // 2 :].astype(bf16)
        gmix = after(gmix, go_far)
    gproj, at_kept, at_sent = call(
        back_kernel, [own_near, gmix, proj, probs, scaled, wqkv, vec, sums, colsum],
        [((ROWS, 3 * D), bf16), ((NEAR, A_ROWS, D), bf16), ((NEAR, A_ROWS, D), bf16)],
        [
            ((HALF, HALF), bf16), ((CLIPS * BANDS, 2, BAND, HALF), bf16), ((3 * D, D), bf16),
            ((128, D), f32), ((D, 128), bf16),
        ],
        20, 20,
    )
    if near:
        dn_arrived = swap(dn_far, ALONG_Z[1], ALONG_Z[0])
        ff_arrived = [swap(far, ALONG_X, ALONG_Y) for far in (up_far, go_far)]
        dn_arrived, ff_arrived, gproj, at_sent = lax.optimization_barrier((dn_arrived, ff_arrived, gproj, at_sent))
        dn_sum = dn_sum[: NEAR // 2] + wide(dn_arrived)
        dn_sum = dn_sum[:PIECE] + wide(swap(dn_sum[PIECE:].astype(bf16), ALONG_Z[0], ALONG_Z[1]))
        dn_sum = dn_sum[:2] + wide(swap(dn_sum[2:].astype(bf16), ALONG_X, ALONG_Y))
        dn_sum = dn_sum[0] + wide(swap(dn_sum[1:].astype(bf16), ALONG_Y, ALONG_X))[0]
        up_sum = up_sum[: NEAR // 2] + wide(ff_arrived[0])
        go_sum = go_sum[: NEAR // 2] + wide(ff_arrived[1])
        ff_sum = jnp.concatenate([up_sum, go_sum], axis=1)
        ff_arrived = swap(ff_sum[PIECE:].astype(bf16), ALONG_Y, ALONG_X)
        at_sum = wide(at_kept) + wide(swap(at_sent, CORES))
        at_rest = [at_sum[i : i + PIECE].astype(bf16) for i in range(PIECE, NEAR, PIECE)]
        gproj = after(gproj, ff_arrived)
    (gtok,) = call(
        token_kernel, [gproj, x, gres, wqkv, vec], [((OWN_ALL, D), f32)], [], 5, 12,
    )
    if near:
        ff_sum = ff_sum[:PIECE] + wide(ff_arrived)
        at_sum = at_sum[:PIECE]
        for piece, mask in zip(at_rest, ALONG_XY):
            at_sum = at_sum + wide(after(swap(piece, mask), gtok))
        ff_sum = scatter_sum(singles(ff_sum), ALONG_Z)[0]
        at_sum = scatter_sum(singles(at_sum), ALONG_Z)[0]
    if near:
        g_up, g_down = ff_sum[:UP_ROWS], dn_sum.T
        g_out = ff_sum[UP_ROWS:].T
        g_qkv = at_sum[:QKV_ROWS].T
        g_vec = at_sum[QKV_ROWS:, : vectors.shape[0]].T
    else:
        at_grads = jnp.concatenate([at_kept, at_sent], axis=0)

        def whole(array):
            blocks = array.reshape(SLOTS // CHUNKS, CHUNKS, UP_ROWS, D).transpose(0, 2, 1, 3)
            return blocks.reshape(D, FF)

        g_up = lax.psum_scatter(whole(jnp.concatenate([up_kept, up_sent], axis=0)), "dp", scatter_dimension=0, tiled=True)
        g_up = lax.psum_scatter(g_up, "tensor", scatter_dimension=1, tiled=True).astype(f32)
        g_down = lax.psum_scatter(whole(jnp.concatenate([dn_kept, dn_sent], axis=0)).T, "dp", scatter_dimension=1, tiled=True)
        g_down = lax.psum_scatter(g_down, "tensor", scatter_dimension=0, tiled=True).astype(f32)

        def owned(array, columns):
            array = array.astype(f32).reshape(-1, D)[:, :columns].T
            return lax.psum_scatter(array, BOTH, scatter_dimension=1, tiled=True)

        g_qkv = owned(at_grads[:, :QKV_ROWS], D)
        g_out = owned(jnp.concatenate([go_kept, go_sent], axis=0), D)
        g_vec = owned(at_grads[:, QKV_ROWS:], vectors.shape[0])
    shape = tokens.shape
    return (out.reshape(shape), gtok.reshape(shape), g_qkv, g_out, g_vec, g_up, g_down)


def solution(mesh):
    placed = (
        P("dp", "tensor", None),
        P("dp"),
        P(None, BOTH),
        P(None, BOTH),
        P(None, BOTH),
        P("dp", "tensor"),
        P("tensor", "dp"),
        P("dp", "tensor", None),
    )
    return jax.shard_map(
        shards,
        mesh=mesh,
        in_specs=placed,
        out_specs=(
            P("dp", "tensor", None),
            P("dp", "tensor", None),
            P(None, BOTH),
            P(None, BOTH),
            P(None, BOTH),
            P("dp", "tensor"),
            P("tensor", "dp"),
        ),
        check_vma=False,
    )
```

```python
import functools

import jax
import jax.numpy as jnp
from jax import lax
from jax.experimental import pallas as pl
from jax.experimental.pallas import tpu as pltpu
from jax.sharding import PartitionSpec as P

D = 512
FF = 2048
HEADS = 16
HEAD = D // HEADS
FREQ = 8
WINDOW = 4
SHIFT = 2
ROW_UNIT = 8

EPS = 1e-06
MASKED = -1000000000.0
SCALE = HEAD ** (-0.5)
INV_ROOT_TWO = 0.7071067811865476
INV_ROOT_TAU = 0.3989422804014327

BOTH = ("dp", "tensor")
SLOTS = 32
NEAR = SLOTS // 2
PIECE = 4
QKV_ROWS = 3 * D // SLOTS
OUT_ROWS = D // SLOTS
A_ROWS = QKV_ROWS + OUT_ROWS
CHUNKS = FF // D
UP_ROWS = D * CHUNKS // SLOTS
B_ROWS = OUT_ROWS + UP_ROWS
G_ROWS = QKV_ROWS + OUT_ROWS
V_ROWS = 16

CLIPS = 4
OWN = 128
EDGE = 16
OWN_ALL = CLIPS * OWN
ROWS = OWN_ALL + CLIPS * 2 * EDGE
BAND = 2 * EDGE
BANDS = OWN // BAND + 1
HALF = D // 2
HALF_HEADS = HALF // HEAD
STEP = 128
SUB = 32

bf16 = jnp.bfloat16
f32 = jnp.float32


def nn(a, b):
    return lax.dot_general(a, b, (((1,), (0,)), ((), ())), preferred_element_type=f32)


def nt(a, b):
    return lax.dot_general(a, b, (((1,), (1,)), ((), ())), preferred_element_type=f32)


def tn(a, b):
    return lax.dot_general(a, b, (((0,), (0,)), ((), ())), preferred_element_type=f32)


def rows_at(start, size):
    return pl.ds(pl.multiple_of(start, size), size)


def norm_parts(values):
    mean = jnp.mean(values, axis=-1, keepdims=True)
    centred = values - mean
    variance = jnp.mean(centred * centred, axis=-1, keepdims=True)
    inverse = lax.rsqrt(variance + EPS)
    return centred * inverse, inverse


def norm_back(grad, scaled, inverse, gain):
    grad_hat = grad * gain
    centre = jnp.mean(grad_hat, axis=-1, keepdims=True)
    slope = jnp.mean(grad_hat * scaled, axis=-1, keepdims=True)
    return inverse * (grad_hat - centre - scaled * slope)


def band_rows(band):
    clip = band // BANDS
    place = band % BANDS
    first = jnp.where(place == 0, OWN_ALL + clip * BAND, clip * OWN + place * BAND - EDGE)
    last = jnp.where(place == BANDS - 1, OWN_ALL + clip * BAND + EDGE, clip * OWN + place * BAND)
    return rows_at(first, EDGE), rows_at(last, EDGE)


def load_band(ref, places, columns):
    return jnp.concatenate([ref[places[0], columns], ref[places[1], columns]], axis=0)


def find(pieces, slot):
    size = pieces[0].shape[0]
    return pieces[slot // size], slot % size


def weight_block(owner):
    return rows_at(owner // CHUNKS * UP_ROWS, UP_ROWS), rows_at(owner % CHUNKS * D, D)


def pack_kernel(qkv_ref, vec_ref, out_ref, up_ref, block_ref):
    block_ref[:QKV_ROWS, :] = qkv_ref[...]
    block_ref[QKV_ROWS:A_ROWS, :] = jnp.zeros((OUT_ROWS, D), bf16)
    block_ref[QKV_ROWS:A_ROWS, : vec_ref.shape[1]] = vec_ref[...]
    block_ref[A_ROWS : A_ROWS + OUT_ROWS, :] = out_ref[...]
    block_ref[A_ROWS + OUT_ROWS :, :] = up_ref[...]


def head_lanes():
    row = lax.broadcasted_iota(jnp.int32, (HALF, HALF), 0) // HEAD
    lane = lax.broadcasted_iota(jnp.int32, (HALF, HALF), 1) // HEAD
    return jnp.where(row == lane, 1.0, 0.0)


def by_head(rows, lanes):
    return jnp.concatenate([rows] * HALF_HEADS, axis=0) * lanes


def flip_heads(wide):
    turned = wide.T
    return jnp.concatenate([turned[head * BAND : (head + 1) * BAND] for head in range(HALF_HEADS)], axis=1)


def attend_kernel(
    own_ref, keep_ref, x_ref, *refs,
):
    a_refs, refs = refs[:-10], refs[-10:]
    proj_ref, prob_ref, mixed_ref, scaled_ref, wqkv_ref, vec_ref, column_vec, lanes_ref, pair_ref, normed_ref = refs
    for slot in range(SLOTS):
        owner = own_ref[slot]
        a_ref, held = find(a_refs, slot)
        wqkv_ref[rows_at(owner * QKV_ROWS, QKV_ROWS), :] = a_ref[held, :QKV_ROWS, :]
        column_vec[rows_at(owner * OUT_ROWS, OUT_ROWS), :] = a_ref[held, QKV_ROWS:A_ROWS, :128].astype(f32)
    vec_ref[...] = column_vec[...].T[:16, :]
    lanes_ref[...] = head_lanes().astype(bf16)
    key_group = (lax.broadcasted_iota(jnp.int32, (BAND, HALF), 0) % FREQ + SHIFT) // WINDOW
    query_group = (lax.broadcasted_iota(jnp.int32, (BAND, HALF), 1) % FREQ + SHIFT) // WINDOW
    pair_ref[...] = jnp.where(key_group == query_group, 1.0, 0.0)

    def scale(step, carry):
        here = rows_at(step * SUB, SUB)
        scaled, _ = norm_parts(x_ref[here, :].astype(f32))
        scaled_ref[here, :] = scaled.astype(bf16)
        normed_ref[here, :] = (scaled * vec_ref[0:1, :] + vec_ref[1:2, :]).astype(bf16)
        return carry

    lax.fori_loop(0, ROWS // SUB, scale, 0, unroll=4)
    for part in range(3):
        columns = slice(part * D, (part + 1) * D)
        part_out = nt(normed_ref[...], wqkv_ref[columns, :])
        if part != 1:
            bias = 2 if part == 0 else 3
            part_out = part_out + vec_ref[bias : bias + 1, :]
        proj_ref[:, columns] = part_out.astype(bf16)

    def score(band, carry):
        places = band_rows(band)
        key_ok = load_band(keep_ref, places, slice(None))
        key_ok = jnp.concatenate([key_ok, key_ok], axis=1) * pair_ref[...] > 0.5
        for half in range(2):
            low = half * HALF
            query = load_band(proj_ref, places, slice(low, low + HALF))
            key = load_band(proj_ref, places, slice(D + low, D + low + HALF))
            scores = nt(key, by_head(query, lanes_ref[...])) * SCALE
            scores = jnp.where(key_ok, scores, MASKED)
            exponent = jnp.exp(scores - jnp.max(scores, axis=0, keepdims=True))
            prob_ref[band, half] = exponent / jnp.sum(exponent, axis=0, keepdims=True)
        return carry

    lax.fori_loop(0, CLIPS * BANDS, score, 0, unroll=10)

    def mix(band, carry):
        places = band_rows(band)
        for half in range(2):
            low = half * HALF
            value = load_band(proj_ref, places, slice(2 * D + low, 2 * D + low + HALF))
            probs = flip_heads(prob_ref[band, half].astype(bf16))
            mixed = nn(probs, by_head(value, lanes_ref[...])).astype(bf16)
            mixed_ref[places[0], low : low + HALF] = mixed[:EDGE]
            mixed_ref[places[1], low : low + HALF] = mixed[EDGE:]
        return carry

    lax.fori_loop(0, CLIPS * BANDS, mix, 0, unroll=10)


def together(*works):
    for _ in range(4):
        for work in works:
            next(work)


def write_grads(own_ref, pieces, block_ref):
    for slot in range(SLOTS):
        grads_ref, held = find(pieces, slot)
        owner = own_ref[slot]
        grads_ref[held] = block_ref[owner % CHUNKS, rows_at(owner // CHUNKS * UP_ROWS, UP_ROWS), :]


def up_kernel(
    own_ref, own_down_ref, keep_ref, cot_ref, x_ref, mixed_ref, vec_ref, *refs,
):
    b_refs, refs = refs[:-14], refs[-14:]
    (
        kept_ref, sent_ref, resid_ref, hid_ref, slope_ref, second_ref, branch_low, up_ref, wout_ref,
        gdown_ref, pre_ref, branch_t, attended_ref, normed_ref,
    ) = refs
    for slot in range(SLOTS):
        owner = own_ref[slot]
        b_ref, held = find(b_refs, slot)
        low = b_ref.shape[1] - B_ROWS
        wout_ref[rows_at(owner * OUT_ROWS, OUT_ROWS), :] = b_ref[held, low : low + OUT_ROWS, :]
        up_ref[weight_block(owner)] = b_ref[held, low + OUT_ROWS :, :]

    attended_ref[...] = nt(mixed_ref[...], wout_ref[...])

    def begin(step, carry):
        here = rows_at(step * SUB, SUB)
        residual = x_ref[here, :].astype(f32) + (attended_ref[here, :] + vec_ref[4:5, :])
        resid_ref[here, :] = residual
        scaled, _ = norm_parts(residual)
        second = (scaled * vec_ref[5:6, :] + vec_ref[6:7, :]).astype(bf16)
        second_ref[here, :] = second
        normed_ref[here, :] = second
        wide = jnp.concatenate([keep_ref[here, :]] * (D // 128), axis=1)
        branch_low[here, :] = (cot_ref[here, :].astype(f32) * wide).astype(bf16)
        return carry

    lax.fori_loop(0, ROWS // SUB, begin, 0, unroll=4)
    branch_t[...] = branch_low[:OWN_ALL, :].T

    def products(chunk):
        for half in range(2):
            columns = slice(chunk * D + half * HALF, chunk * D + (half + 1) * HALF)
            pre_ref[:, columns] = nn(normed_ref[...], up_ref[:, columns])
            yield
            yield

    def slopes(chunk):
        columns = slice(chunk * D, (chunk + 1) * D)
        for step in range(ROWS // 16):
            here = slice(step * 16, step * 16 + 16)
            pre = pre_ref[here, columns] + vec_ref[8 + chunk : 9 + chunk, :]
            phi = 0.5 + 0.5 * lax.erf(pre * INV_ROOT_TWO)
            slope_ref[here, columns] = (phi + pre * (jnp.exp(-0.5 * pre * pre) * INV_ROOT_TAU)).astype(bf16)
            hid_ref[here, columns] = (pre * phi).astype(bf16)
            if step % 10 == 9:
                yield

    def weights(chunk):
        for half in range(2):
            columns = slice(chunk * D + half * HALF, chunk * D + (half + 1) * HALF)
            gdown = nn(branch_t[...], hid_ref[:OWN_ALL, columns])
            gdown_ref[chunk, :, half * HALF : (half + 1) * HALF] = gdown.astype(bf16)
            yield
            yield

    together(products(0))
    together(products(1), slopes(0))
    for chunk in range(2, CHUNKS):
        together(products(chunk), slopes(chunk - 1), weights(chunk - 2))
    together(slopes(CHUNKS - 1), weights(CHUNKS - 2))
    together(weights(CHUNKS - 1))
    write_grads(own_down_ref, (kept_ref, sent_ref), gdown_ref)


def down_kernel(
    own_ref, own_down_ref, hid_ref, slope_ref, second_ref, branch_low, up_ref, *refs,
):
    c_refs, refs = refs[:-10], refs[-10:]
    (
        kept_ref, sent_ref, branch_ref, gsec_ref, colsum_ref,
        down_ref, gup_ref, ghid_ref, gpre_ref, second_t,
    ) = refs
    for slot in range(SLOTS):
        c_ref, held = find(c_refs, slot)
        down_ref[weight_block(own_down_ref[slot])] = c_ref[held]
    second_t[:D, :] = second_ref[:OWN_ALL, :].T
    second_t[D:, :] = jnp.ones((16, OWN_ALL), bf16)

    def products(chunk):
        for half in range(2):
            columns = slice(chunk * D + half * HALF, chunk * D + (half + 1) * HALF)
            ghid_ref[:, columns] = nn(branch_low[...], down_ref[:, columns])
            yield
            yield

    def slopes(chunk):
        columns = slice(chunk * D, (chunk + 1) * D)
        for step in range(ROWS // 16):
            here = slice(step * 16, step * 16 + 16)
            gpre_ref[here, columns] = (ghid_ref[here, columns] * slope_ref[here, columns].astype(f32)).astype(bf16)
            if step % 10 == 9:
                yield

    def weights(chunk):
        for half in range(2):
            columns = slice(chunk * D + half * HALF, chunk * D + (half + 1) * HALF)
            gup = nn(second_t[...], gpre_ref[:OWN_ALL, columns])
            gup_ref[chunk, :, half * HALF : (half + 1) * HALF] = gup[:D].astype(bf16)
            colsum_ref[chunk : chunk + 1, half * HALF : (half + 1) * HALF] = gup[D : D + 1]
            yield
            yield

    together(products(0))
    together(products(1), slopes(0))
    for chunk in range(2, CHUNKS):
        together(products(chunk), slopes(chunk - 1), weights(chunk - 2))
    together(slopes(CHUNKS - 1), weights(CHUNKS - 2))
    together(weights(CHUNKS - 1))
    branch_ref[...] = nt(hid_ref[:OWN_ALL, :], down_ref[...])
    gsec_ref[...] = nt(gpre_ref[...], up_ref[...])
    write_grads(own_ref, (kept_ref, sent_ref), gup_ref)


def finish_kernel(
    keep_ref, cot_ref, mixed_ref, resid_ref, branch_ref, gsec_ref, wout_ref, vec_ref,
    out_ref, gres_ref, gout_ref, gmix_ref, sums_ref,
    gatt_ref,
):
    def rows(step, totals):
        here = rows_at(step * SUB, SUB)
        own = jnp.where(step < OWN_ALL // SUB, 1.0, 0.0)
        wide = jnp.concatenate([keep_ref[here, :]] * (D // 128), axis=1)
        scaled, inverse = norm_parts(resid_ref[here, :])
        grad_out = cot_ref[here, :].astype(f32) * wide
        gsec = gsec_ref[here, :]
        gres = grad_out + norm_back(gsec, scaled, inverse, vec_ref[5:6, :])
        gres_ref[here, :] = gres
        gatt = gres.astype(bf16)
        gatt_ref[here, :] = gatt
        parts = (gatt.astype(f32), gsec * scaled, gsec, grad_out.astype(bf16).astype(f32))
        return tuple(t + own * p.reshape(SUB // 8, 8, D).sum(axis=0) for t, p in zip(totals, parts))

    totals = lax.fori_loop(0, ROWS // SUB, rows, (jnp.zeros((8, D), f32),) * 4, unroll=4)
    for place, total in enumerate(totals):
        sums_ref[place : place + 1, :] = jnp.sum(total, axis=0, keepdims=True)
    gmix_ref[...] = nn(gatt_ref[...], wout_ref[...]).astype(bf16)
    gout_ref[...] = nn(gatt_ref[:OWN_ALL, :].T, mixed_ref[:OWN_ALL, :]).astype(bf16)

    def outputs(step, carry):
        here = rows_at(step * SUB, SUB)
        wide = jnp.concatenate([keep_ref[here, :]] * (D // 128), axis=1)
        out_ref[here, :] = (wide * (resid_ref[here, :] + (branch_ref[here, :] + vec_ref[7:8, :]))).astype(bf16)
        return carry

    lax.fori_loop(0, OWN_ALL // SUB, outputs, 0, unroll=4)


def back_kernel(gmix_ref, proj_ref, prob_ref, gproj_ref, lanes_ref, gscore_ref):
    lanes_ref[...] = head_lanes().astype(bf16)

    def score(band, carry):
        places = band_rows(band)
        for half in range(2):
            low = half * HALF
            value = load_band(proj_ref, places, slice(2 * D + low, 2 * D + low + HALF))
            grad = load_band(gmix_ref, places, slice(low, low + HALF))
            probs = prob_ref[band, half]
            grad_probs = nt(value, by_head(grad, lanes_ref[...]))
            row_dot = jnp.sum(probs * grad_probs, axis=0, keepdims=True)
            gscore_ref[band, half] = (probs * (grad_probs - row_dot)).astype(bf16)
        return carry

    lax.fori_loop(0, CLIPS * BANDS, score, 0, unroll=10)

    def mix(band, carry):
        places = band_rows(band)
        for half in range(2):
            low = half * HALF
            query = load_band(proj_ref, places, slice(low, low + HALF))
            key = load_band(proj_ref, places, slice(D + low, D + low + HALF))
            grad = load_band(gmix_ref, places, slice(low, low + HALF))
            grad_scores = gscore_ref[band, half]
            grad_key = nn(grad_scores, by_head(query, lanes_ref[...])) * SCALE
            grad_value = nn(prob_ref[band, half].astype(bf16), by_head(grad, lanes_ref[...]))
            grad_query = nn(flip_heads(grad_scores), by_head(key, lanes_ref[...])) * SCALE
            for part, values in enumerate((grad_query, grad_key, grad_value)):
                values = values.astype(bf16)
                gproj_ref[places[0], part * D + low : part * D + low + HALF] = values[:EDGE]
                gproj_ref[places[1], part * D + low : part * D + low + HALF] = values[EDGE:]
        return carry

    lax.fori_loop(0, CLIPS * BANDS, mix, 0, unroll=10)


def project_kernel(
    own_ref, gproj_ref, gout_ref, scaled_ref, wqkv_ref, vec_ref, sums_ref, colsum_ref,
    kept_ref, sent_ref,
    gqkv_ref, gvec_ref,
):
    def add_rows(step, totals):
        here = rows_at(step * SUB, SUB)
        return totals + gproj_ref[here, :].astype(f32).reshape(SUB // 8, 8, 3 * D).sum(axis=0)

    totals = lax.fori_loop(0, OWN_ALL // SUB, add_rows, jnp.zeros((8, 3 * D), f32))
    totals = jnp.sum(totals, axis=0, keepdims=True)
    gvec_ref[...] = jnp.zeros_like(gvec_ref)
    gain_grad = jnp.zeros((8, D), f32)
    shift_grad = jnp.zeros((1, D), f32)
    for part in range(3):
        gproj_t = gproj_ref[:OWN_ALL, part * D : (part + 1) * D].T
        product = nn(gproj_t, scaled_ref[:OWN_ALL, :])
        total = totals[:, part * D : (part + 1) * D]
        weight = wqkv_ref[part * D : (part + 1) * D, :]
        both = product * weight.astype(f32)
        gain_grad = gain_grad + both.reshape(D // 8, 8, D).sum(axis=0)
        high = total.astype(bf16)
        rest = (total - high.astype(f32)).astype(bf16)
        shift_grad = shift_grad + nn(high, weight) + nn(rest, weight)
        column = jnp.broadcast_to(total, (8, D)).T[:, 0:1]
        gqkv = product * vec_ref[0:1, :] + column * vec_ref[1:2, :]
        gqkv_ref[part * D : (part + 1) * D, :] = gqkv.astype(bf16)
    gvec_ref[0:1, :] = jnp.sum(gain_grad, axis=0, keepdims=True)
    gvec_ref[1:2, :] = shift_grad
    gvec_ref[2:3, :] = totals[:, :D]
    gvec_ref[3:4, :] = totals[:, 2 * D :]
    gvec_ref[4:8, :] = sums_ref[0:4, :]
    gvec_ref[8:12, :] = colsum_ref[0:4, :]
    for slot in range(SLOTS):
        owner = own_ref[slot]
        grads_ref, held = (kept_ref, sent_ref)[slot // NEAR], slot % NEAR * G_ROWS
        grads_ref[held : held + QKV_ROWS, :] = gqkv_ref[rows_at(owner * QKV_ROWS, QKV_ROWS), :]
        grads_ref[held + QKV_ROWS : held + G_ROWS, :] = gout_ref[rows_at(owner * OUT_ROWS, OUT_ROWS), :]
    for grads_ref in (kept_ref, sent_ref):
        grads_ref[NEAR * G_ROWS :, :] = gvec_ref[:V_ROWS, :].astype(bf16)


def share_kernel(*refs):
    *pieces, kept_ref, first_ref, second_ref, third_ref = refs
    size = kept_ref.shape[0] - V_ROWS

    def total(rows):
        result = pieces[0][rows, :].astype(f32)
        for piece in pieces[1:]:
            result = result + piece[rows, :].astype(f32)
        return result

    vectors = total(slice(4 * size, 4 * size + V_ROWS))
    for part, out_ref in enumerate((kept_ref, first_ref, second_ref, third_ref)):
        for low in range(0, size, 64):
            out_ref[low : low + 64, :] = total(slice(part * size + low, part * size + low + 64)).astype(out_ref.dtype)
        out_ref[size:, :] = vectors.astype(out_ref.dtype)


def token_kernel( gproj_ref, x_ref, gres_ref, wqkv_ref, vec_ref, gtok_ref):
    def rows(step, carry):
        here = rows_at(step * STEP, STEP)
        gnormed = nn(gproj_ref[here, :D], wqkv_ref[:D, :])
        for part in range(1, 3):
            gnormed += nn(gproj_ref[here, part * D : (part + 1) * D], wqkv_ref[part * D : (part + 1) * D, :])
        scaled, inverse = norm_parts(x_ref[here, :].astype(f32))
        gtok_ref[here, :] = gres_ref[here, :] + norm_back(gnormed, scaled, inverse, vec_ref[0:1, :])
        return carry

    lax.fori_loop(0, OWN_ALL // STEP, rows, 0)


def total_kernel(device_ref, *refs):
    *pieces, gqkv_ref, gout_ref, gvec_ref = refs
    total = pieces[0][...]
    for piece in pieces[1:]:
        total = total + piece[...].astype(f32)
    gqkv_ref[...] = total[:QKV_ROWS]
    gout_ref[...] = total[QKV_ROWS:G_ROWS]
    own = pltpu.roll(total[G_ROWS:], lax.rem(D - device_ref[0] * OUT_ROWS, D), 1)
    gvec_ref[...] = own[: gvec_ref.shape[0], : gvec_ref.shape[1]]


def call(kernel, args, outs, scratch, micros, mib):
    smem, vmem = pl.BlockSpec(memory_space=pltpu.SMEM), pl.BlockSpec(memory_space=pltpu.VMEM)
    return pl.pallas_call(
        kernel,
        out_shape=[jax.ShapeDtypeStruct(s, t) for s, t in outs],
        in_specs=[smem if a.dtype == jnp.int32 else vmem for a in args],
        out_specs=[vmem] * len(outs),
        scratch_shapes=[pltpu.VMEM(s, t) for s, t in scratch],
        compiler_params=pltpu.CompilerParams(vmem_limit_bytes=mib * 1024 * 1024),
        cost_estimate=pl.CostEstimate(flops=int(micros * 1.1e9), bytes_accessed=2**20, transcendentals=0),
    )(*args)


def swap(array, mask, other=None):
    count = lax.axis_size("dp") * lax.axis_size("tensor")
    masks = (mask, mask if other is None else other)
    return lax.ppermute(array, BOTH, [(device, device ^ masks[device % 2]) for device in range(count)])


ALONG_Z, ALONG_Y, ALONG_X, CORES = (8, 16, 24), 2, 4, 1
ALONG_XY = (ALONG_Y, ALONG_X, ALONG_Y ^ ALONG_X)


def owners(device, swapped, line_first=True, turn=None):
    def one(second_core):
        first = ALONG_X if second_core and swapped else ALONG_Y
        plane = [0, first, first ^ ALONG_XY[2], ALONG_XY[2]]
        line = [0, *ALONG_Z]
        if turn is not None and second_core != turn:
            line = [line[0], line[2], line[1], line[3]]
        return [m ^ o for o in plane for m in line] if line_first else [m ^ o for o in line for m in plane]

    core = device % 2
    first = jnp.where(core == 0, jnp.array(one(0)), jnp.array(one(1)))
    second = jnp.where(core == 0, jnp.array(one(1)), jnp.array(one(0))) ^ CORES
    return (device ^ jnp.concatenate([first, second])).astype(jnp.int32)


def gather(held, phase):
    return [held] + [swap(held, mask) for mask in phase]


def both_cores(pieces):
    return pieces + [swap(piece, CORES) for piece in pieces]


def wide(array):
    return array.astype(f32)


def add_all(total, others):
    for other in others:
        total = total + wide(other)
    return total


def after(array, *others):
    return lax.optimization_barrier((array,) + others)[0]


def neighbours(array, axis_name, width):
    count = lax.axis_size(axis_name)
    up = [(i, i + 1) for i in range(count - 1)]
    low = lax.ppermute(array[..., -width:, :], axis_name, up)
    high = lax.ppermute(array[..., :width, :], axis_name, [(b, a) for a, b in up])
    return low, high


def shards(tokens, valid, w_qkv, w_out, vectors, w_up, w_down, cotangent):
    devices_dp, devices_t = lax.axis_size("dp"), lax.axis_size("tensor")
    near = devices_dp == 8 and devices_t == 4
    rank = lax.axis_index("tensor")

    own_time = jnp.broadcast_to((jnp.arange(OWN) // FREQ)[None], (CLIPS, OWN)).reshape(-1)
    edge_time = jnp.arange(BAND) // FREQ + jnp.where(jnp.arange(BAND) < EDGE, -SHIFT, OWN // FREQ - SHIFT)
    edge_time = jnp.broadcast_to(edge_time[None], (CLIPS, BAND)).reshape(-1)
    time = jnp.concatenate([own_time, edge_time]) + rank * (OWN // FREQ)
    limit = valid * ROW_UNIT
    limit = jnp.concatenate([jnp.repeat(limit, OWN), jnp.repeat(limit, BAND)])
    keep = jnp.where((time >= 0) & (time < limit), 1.0, 0.0).astype(f32)
    keep = jnp.broadcast_to(keep[:, None], (ROWS, 128))

    if near:
        device = lax.axis_index("dp") * devices_t + rank
        own_near, own_far = owners(device, False), owners(device, True)
        own_down, own_up = owners(device, True, False, 0), owners(device, True, True, 1)
        (block,) = call(
            pack_kernel, [w_qkv.T, vectors.T, w_out.T, w_up], [((A_ROWS + B_ROWS, D), bf16)], [], 1, 4,
        )
        edges = neighbours(jnp.stack([tokens, cotangent]), "tensor", EDGE)
        line = gather(block[None], ALONG_Z)
        down = w_down.T[None]
        down = jnp.concatenate([down, swap(down, ALONG_Y, ALONG_X)], axis=0)
        down = [down, swap(down, ALONG_X, ALONG_Y)]
        line, down, edges, keep, own_near, own_far, own_down, own_up = lax.optimization_barrier(
            (line, down, edges, keep, own_near, own_far, own_down, own_up)
        )
        line, down = jnp.concatenate(line, axis=0), jnp.concatenate(down, axis=0)
        near_pieces = swap(line, ALONG_Y, ALONG_X)
        down = [down, swap(down, ALONG_Z[0], ALONG_Z[1])]
        near_pieces, down = lax.optimization_barrier((near_pieces, down))
        down = jnp.concatenate(down, axis=0)
        near_pieces = jnp.concatenate([line, near_pieces], axis=0)
        a_far = swap(near_pieces[:, :A_ROWS], ALONG_X, ALONG_Y)
        b_far = swap(near_pieces[:, A_ROWS:], ALONG_X, ALONG_Y)
        pieces = both_cores([near_pieces])
        a_pieces = [pieces[0], a_far, pieces[1], swap(a_far, CORES)]
        c_pieces = [down, swap(down, ALONG_Z[1], ALONG_Z[0])]
    else:
        own_near = own_far = own_down = own_up = jnp.arange(SLOTS, dtype=jnp.int32)
        edges = neighbours(jnp.stack([tokens, cotangent]), "tensor", EDGE)
        qkv, out, vec = (lax.all_gather(a, BOTH, axis=1, tiled=True).T for a in (w_qkv, w_out, vectors))
        vec = jnp.pad(vec, ((0, 0), (0, D - vec.shape[1])))
        up = lax.all_gather(lax.all_gather(w_up, "dp", axis=0, tiled=True), "tensor", axis=1, tiled=True)
        down = lax.all_gather(lax.all_gather(w_down, "dp", axis=1, tiled=True), "tensor", axis=0, tiled=True).T
        up, down = (
            a.reshape(SLOTS // CHUNKS, UP_ROWS, CHUNKS, D).transpose(0, 2, 1, 3).reshape(SLOTS, UP_ROWS, D)
            for a in (up, down)
        )
        a_slots = jnp.concatenate([a.reshape(SLOTS, -1, D) for a in (qkv, vec)], axis=1)
        b_slots = jnp.concatenate([out.reshape(SLOTS, -1, D), up], axis=1)
        a_pieces, b_pieces, c_pieces = (
            [a[i : i + PIECE] for i in range(0, SLOTS, PIECE)] for a in (a_slots, b_slots, down)
        )

    edges = jnp.concatenate(edges, axis=2).reshape(2, CLIPS * BAND, D)
    x = jnp.concatenate([tokens.reshape(OWN_ALL, D), edges[0]], axis=0)
    cot = jnp.concatenate([cotangent.reshape(OWN_ALL, D), edges[1]], axis=0)
    proj, probs, mixed, scaled, wqkv, vec = call(
        attend_kernel, [own_far, keep, x, *a_pieces],
        [
            ((ROWS, 3 * D), bf16), ((CLIPS * BANDS, 2, BAND, HALF), f32), ((ROWS, D), bf16), ((ROWS, D), bf16),
            ((3 * D, D), bf16), ((16, D), f32),
        ],
        [((D, 128), f32), ((HALF, HALF), bf16), ((BAND, HALF), f32), ((ROWS, D), bf16)],
        0.1, 20,
    )
    if near:
        b_far, c_pieces, proj = lax.optimization_barrier((b_far, c_pieces, proj))
        b_pieces = [pieces[0], b_far, pieces[1], swap(b_far, CORES)]
        c_pieces = both_cores(c_pieces)
    dn_kept, dn_sent, resid, hid, slope, second, branch_low, up_all, wout = call(
        up_kernel, [own_far, own_down, keep, cot, x, mixed, vec, *b_pieces],
        [
            ((NEAR, UP_ROWS, D), bf16), ((NEAR, UP_ROWS, D), bf16), ((ROWS, D), f32), ((ROWS, FF), bf16),
            ((ROWS, FF), bf16), ((ROWS, D), bf16), ((ROWS, D), bf16), ((D, FF), bf16), ((D, D), bf16),
        ],
        [
            ((CHUNKS, D, D), bf16), ((ROWS, FF), f32), ((D, OWN_ALL), bf16), ((ROWS, D), f32), ((ROWS, D), bf16),
        ],
        8, 30,
    )
    up_kept, up_sent, branch, gsec, colsum = call(
        down_kernel, [own_up, own_down, hid, slope, second, branch_low, up_all, *c_pieces],
        [
            ((NEAR, UP_ROWS, D), bf16), ((NEAR, UP_ROWS, D), bf16), ((OWN_ALL, D), f32), ((ROWS, D), f32),
            ((8, D), f32),
        ],
        [
            ((D, FF), bf16), ((CHUNKS, D, D), bf16), ((ROWS, FF), f32), ((ROWS, FF), bf16), ((D + 16, OWN_ALL), bf16),
        ],
        8, 30,
    )
    if near:
        dn_sum = wide(dn_kept) + wide(after(swap(dn_sent, CORES), gsec))
        dn_far = dn_sum[NEAR // 2 :].astype(bf16)
        up_sum = wide(up_kept) + wide(swap(up_sent, CORES))
        up_far = up_sum[NEAR // 2 :].astype(bf16)
        gsec, up_far, dn_far = lax.optimization_barrier((gsec, up_far, dn_far))
    out, gres, gout, gmix, sums = call(
        finish_kernel, [keep, cot, mixed, resid, branch, gsec, wout, vec],
        [
            ((OWN_ALL, D), bf16), ((ROWS, D), f32), ((D, D), bf16), ((ROWS, D), bf16), ((8, D), f32),
        ],
        [((ROWS, D), bf16)],
        0.1, 16,
    )
    (gproj,) = call(
        back_kernel, [gmix, proj, probs], [((ROWS, 3 * D), bf16)],
        [((HALF, HALF), bf16), ((CLIPS * BANDS, 2, BAND, HALF), bf16)],
        0.1, 16,
    )
    if near:
        up_arrived, gproj = lax.optimization_barrier((swap(up_far, ALONG_X, ALONG_Y), gproj))
        up_sum = up_sum[: NEAR // 2] + wide(up_arrived)
        up_near, gproj = lax.optimization_barrier((up_sum[PIECE:].astype(bf16), gproj))
    at_kept, at_sent = call(
        project_kernel, [own_near, gproj, gout, scaled, wqkv, vec, sums, colsum],
        [((NEAR * G_ROWS + V_ROWS, D), bf16)] * 2,
        [((3 * D, D), bf16), ((128, D), f32)],
        0.1, 16,
    )
    if near:
        dn_arrived, at_sent = lax.optimization_barrier((swap(dn_far, ALONG_Z[1], ALONG_Z[0]), at_sent))
        up_arrived, at_arrived, gproj = lax.optimization_barrier(
            (swap(up_near, ALONG_Y, ALONG_X), swap(at_sent, CORES), gproj)
        )
    (gtok,) = call(
        token_kernel, [gproj, x, gres, wqkv, vec], [((OWN_ALL, D), f32)], [], 0.1, 12,
    )
    if near:
        at_sum, *at_rest = call(
            share_kernel, [at_kept, at_arrived],
            [((PIECE * G_ROWS + V_ROWS, D), t) for t in (f32, bf16, bf16, bf16)], [], 0.1, 8,
        )
        dn_sum = dn_sum[: NEAR // 2] + wide(dn_arrived)
        up_sum = up_sum[:PIECE] + wide(up_arrived)
        at_arrived = [swap(piece, mask) for piece, mask in zip(at_rest, ALONG_XY)]
        ff_arrived = jnp.concatenate([dn_sum[PIECE:], up_sum[2:]], axis=0).astype(bf16)
        ff_arrived = swap(ff_arrived, ALONG_Z[0], ALONG_Z[1])
        ff_arrived, gtok = lax.optimization_barrier((ff_arrived, gtok))
        dn_sum, up_sum = dn_sum[:PIECE] + wide(ff_arrived[:PIECE]), up_sum[:2] + wide(ff_arrived[PIECE:])
        up_arrived = swap(up_sum[1:].astype(bf16), ALONG_Z[1], ALONG_Z[0])
        dn_rest = dn_sum.astype(bf16)
        dn_arrived = [
            swap(dn_rest[1:2], ALONG_Y, ALONG_X), swap(dn_rest[2:3], ALONG_X, ALONG_Y), swap(dn_rest[3:], ALONG_XY[2]),
        ]
        at_arrived, up_arrived = lax.optimization_barrier((at_arrived, up_arrived))
        at_sum, *at_rest = call(
            share_kernel, [at_sum, *at_arrived],
            [((G_ROWS + V_ROWS, D), t) for t in (f32, bf16, bf16, bf16)], [], 0.1, 8,
        )
        up_sum = up_sum[0] + wide(up_arrived)[0]
        dn_sum = add_all(dn_sum[:1], dn_arrived)[0]
        at_arrived = [swap(piece, mask) for piece, mask in zip(at_rest, ALONG_Z)]
        g_qkv, g_out, g_vec = call(
            total_kernel, [device.astype(jnp.int32)[None], at_sum, *at_arrived],
            [((QKV_ROWS, D), f32), ((OUT_ROWS, D), f32), (vectors.shape, f32)], [], 0.1, 4,
        )
    if near:
        g_up, g_down = up_sum, dn_sum.T
        g_qkv, g_out = g_qkv.T, g_out.T
    else:
        at_grads = jnp.concatenate([a[: NEAR * G_ROWS].reshape(NEAR, G_ROWS, D) for a in (at_kept, at_sent)], axis=0)

        def whole(array):
            blocks = array.reshape(SLOTS // CHUNKS, CHUNKS, UP_ROWS, D).transpose(0, 2, 1, 3)
            return blocks.reshape(D, FF)

        g_up = lax.psum_scatter(whole(jnp.concatenate([up_kept, up_sent], axis=0)), "dp", scatter_dimension=0, tiled=True)
        g_up = lax.psum_scatter(g_up, "tensor", scatter_dimension=1, tiled=True).astype(f32)
        g_down = lax.psum_scatter(whole(jnp.concatenate([dn_kept, dn_sent], axis=0)).T, "dp", scatter_dimension=1, tiled=True)
        g_down = lax.psum_scatter(g_down, "tensor", scatter_dimension=0, tiled=True).astype(f32)

        def owned(array):
            return lax.psum_scatter(array.astype(f32), BOTH, scatter_dimension=1, tiled=True)

        g_qkv = owned(at_grads[:, :QKV_ROWS].reshape(-1, D).T)
        g_out = owned(at_grads[:, QKV_ROWS:].reshape(-1, D).T)
        g_vec = owned(at_kept[NEAR * G_ROWS :][: vectors.shape[0]])
    shape = tokens.shape
    return (out.reshape(shape), gtok.reshape(shape), g_qkv, g_out, g_vec, g_up, g_down)


def solution(mesh):
    placed = (
        P("dp", "tensor", None),
        P("dp"),
        P(None, BOTH),
        P(None, BOTH),
        P(None, BOTH),
        P("dp", "tensor"),
        P("tensor", "dp"),
        P("dp", "tensor", None),
    )
    return jax.shard_map(
        shards,
        mesh=mesh,
        in_specs=placed,
        out_specs=(
            P("dp", "tensor", None),
            P("dp", "tensor", None),
            P(None, BOTH),
            P(None, BOTH),
            P(None, BOTH),
            P("dp", "tensor"),
            P("tensor", "dp"),
        ),
        check_vma=False,
    )
```

```python
import functools

import jax
import jax.numpy as jnp
from jax import lax
from jax.experimental import pallas as pl
from jax.experimental.pallas import tpu as pltpu
from jax.sharding import PartitionSpec as P

D = 512
FF = 2048
HEADS = 16
HEAD = D // HEADS
FREQ = 8
WINDOW = 4
SHIFT = 2
ROW_UNIT = 8

EPS = 1e-06
MASKED = -1000000000.0
SCALE = HEAD ** (-0.5)
INV_ROOT_TWO = 0.7071067811865476
INV_ROOT_TAU = 0.3989422804014327

BOTH = ("dp", "tensor")
SLOTS = 32
NEAR = SLOTS // 2
PIECE = 4
QKV_ROWS = 3 * D // SLOTS
OUT_ROWS = D // SLOTS
A_ROWS = QKV_ROWS + OUT_ROWS
CHUNKS = FF // D
UP_ROWS = D * CHUNKS // SLOTS
B_ROWS = OUT_ROWS + UP_ROWS
G_ROWS = QKV_ROWS + OUT_ROWS
V_ROWS = 16
AT_ROWS = SLOTS // 2 * G_ROWS + V_ROWS
PARTS = 5

CLIPS = 4
OWN = 128
EDGE = 16
OWN_ALL = CLIPS * OWN
ROWS = OWN_ALL + CLIPS * 2 * EDGE
BAND = 2 * EDGE
BANDS = OWN // BAND + 1
HALF = D // 2
HALF_HEADS = HALF // HEAD
STEP = 128
SUB = 32

bf16 = jnp.bfloat16
f32 = jnp.float32


def nn(a, b):
    return lax.dot_general(a, b, (((1,), (0,)), ((), ())), preferred_element_type=f32)


def nt(a, b):
    return lax.dot_general(a, b, (((1,), (1,)), ((), ())), preferred_element_type=f32)


def tn(a, b):
    return lax.dot_general(a, b, (((0,), (0,)), ((), ())), preferred_element_type=f32)


def rows_at(start, size):
    return pl.ds(pl.multiple_of(start, size), size)


def norm_parts(values):
    mean = jnp.mean(values, axis=-1, keepdims=True)
    centred = values - mean
    variance = jnp.mean(centred * centred, axis=-1, keepdims=True)
    inverse = lax.rsqrt(variance + EPS)
    return centred * inverse, inverse


def norm_back(grad, scaled, inverse, gain):
    grad_hat = grad * gain
    centre = jnp.mean(grad_hat, axis=-1, keepdims=True)
    slope = jnp.mean(grad_hat * scaled, axis=-1, keepdims=True)
    return inverse * (grad_hat - centre - scaled * slope)


def band_places(band):
    clip, place = divmod(band, BANDS)
    first = OWN_ALL + clip * BAND if place == 0 else clip * OWN + place * BAND - EDGE
    last = OWN_ALL + clip * BAND + EDGE if place == BANDS - 1 else clip * OWN + place * BAND
    return slice(first, first + EDGE), slice(last, last + EDGE)


def load_band(ref, places, columns):
    return jnp.concatenate([ref[places[0], columns], ref[places[1], columns]], axis=0)


def find(pieces, slot):
    size = pieces[0].shape[0]
    return pieces[slot // size], slot % size


def weight_block(owner):
    return rows_at(owner // CHUNKS * UP_ROWS, UP_ROWS), rows_at(owner % CHUNKS * D, D)


def pack_kernel(qkv_ref, vec_ref, out_ref, up_ref, block_ref, rows_ref, sems):
    here = (
        rows_ref, block_ref.at[:QKV_ROWS], block_ref.at[A_ROWS : A_ROWS + OUT_ROWS], block_ref.at[A_ROWS + OUT_ROWS :],
    )
    copies = [
        pltpu.make_async_copy(there, place, sems.at[i])
        for i, (there, place) in enumerate(zip((vec_ref, qkv_ref, out_ref, up_ref), here))
    ]
    for copy in copies:
        copy.start()
    block_ref[QKV_ROWS:A_ROWS, :] = jnp.zeros((OUT_ROWS, D), bf16)
    row = lax.broadcasted_iota(jnp.int32, (OUT_ROWS, OUT_ROWS), 0)
    lane = lax.broadcasted_iota(jnp.int32, (OUT_ROWS, OUT_ROWS), 1)
    copies[0].wait()
    turned = nt(jnp.where(row == lane, 1.0, 0.0).astype(bf16), rows_ref[...])
    block_ref[QKV_ROWS:A_ROWS, : vec_ref.shape[0]] = turned.astype(bf16)
    for copy in copies[1:]:
        copy.wait()


def head_lanes():
    row = lax.broadcasted_iota(jnp.int32, (HALF, HALF), 0) // HEAD
    lane = lax.broadcasted_iota(jnp.int32, (HALF, HALF), 1) // HEAD
    return jnp.where(row == lane, 1.0, 0.0)


def by_head(rows, lanes):
    return jnp.concatenate([rows] * HALF_HEADS, axis=0) * lanes


def flip_heads(wide):
    turned = wide.T
    return jnp.concatenate([turned[head * BAND : (head + 1) * BAND] for head in range(HALF_HEADS)], axis=1)


def attend_kernel(
    own_ref, keep_ref, x_ref, *refs,
):
    a_refs, refs = refs[:-10], refs[-10:]
    proj_ref, prob_ref, mixed_ref, scaled_ref, wqkv_ref, vec_ref, column_vec, lanes_ref, pair_ref, normed_ref = refs
    for slot in range(SLOTS):
        owner = own_ref[slot]
        a_ref, held = find(a_refs, slot)
        wqkv_ref[rows_at(owner * QKV_ROWS, QKV_ROWS), :] = a_ref[held, :QKV_ROWS, :]
        column_vec[rows_at(owner * OUT_ROWS, OUT_ROWS), :] = a_ref[held, QKV_ROWS:A_ROWS, :128].astype(f32)
    vec_ref[...] = column_vec[...].T[:16, :]
    lanes_ref[...] = head_lanes().astype(bf16)
    key_group = (lax.broadcasted_iota(jnp.int32, (BAND, HALF), 0) % FREQ + SHIFT) // WINDOW
    query_group = (lax.broadcasted_iota(jnp.int32, (BAND, HALF), 1) % FREQ + SHIFT) // WINDOW
    pair_ref[...] = jnp.where(key_group == query_group, 1.0, 0.0)

    for step in range(ROWS // SUB):
        here = slice(step * SUB, (step + 1) * SUB)
        scaled, _ = norm_parts(x_ref[here, :].astype(f32))
        scaled_ref[here, :] = scaled.astype(bf16)
        normed_ref[here, :] = (scaled * vec_ref[0:1, :] + vec_ref[1:2, :]).astype(bf16)
    for part in range(3):
        columns = slice(part * D, (part + 1) * D)
        part_out = nt(normed_ref[...], wqkv_ref[columns, :])
        if part != 1:
            bias = 2 if part == 0 else 3
            part_out = part_out + vec_ref[bias : bias + 1, :]
        proj_ref[:, columns] = part_out.astype(bf16)

    for band in range(CLIPS * BANDS):
        places = band_places(band)
        key_ok = load_band(keep_ref, places, slice(None))
        key_ok = jnp.concatenate([key_ok, key_ok], axis=1) * pair_ref[...] > 0.5
        for half in range(2):
            low = half * HALF
            query = load_band(proj_ref, places, slice(low, low + HALF))
            key = load_band(proj_ref, places, slice(D + low, D + low + HALF))
            scores = nt(key, by_head(query, lanes_ref[...])) * SCALE
            scores = jnp.where(key_ok, scores, MASKED)
            exponent = jnp.exp(scores - jnp.max(scores, axis=0, keepdims=True))
            prob_ref[band, half] = exponent / jnp.sum(exponent, axis=0, keepdims=True)
    for band in range(CLIPS * BANDS):
        places = band_places(band)
        for half in range(2):
            low = half * HALF
            value = load_band(proj_ref, places, slice(2 * D + low, 2 * D + low + HALF))
            probs = flip_heads(prob_ref[band, half].astype(bf16))
            mixed = nn(probs, by_head(value, lanes_ref[...])).astype(bf16)
            mixed_ref[places[0], low : low + HALF] = mixed[:EDGE]
            mixed_ref[places[1], low : low + HALF] = mixed[EDGE:]


def together(*works):
    for _ in range(4):
        for work in works:
            next(work)


def write_grads(own_ref, pieces, block_ref):
    for slot in range(SLOTS):
        grads_ref, held = find(pieces, slot)
        owner = own_ref[slot]
        grads_ref[held] = block_ref[owner % CHUNKS, rows_at(owner // CHUNKS * UP_ROWS, UP_ROWS), :]


def up_kernel(
    own_ref, own_down_ref, keep_ref, cot_ref, x_ref, mixed_ref, vec_ref, *refs,
):
    b_refs, refs = refs[:-14], refs[-14:]
    (
        kept_ref, sent_ref, resid_ref, hid_ref, slope_ref, second_ref, branch_low, up_ref, wout_ref,
        gdown_ref, pre_ref, branch_t, attended_ref, normed_ref,
    ) = refs
    for slot in range(SLOTS):
        owner = own_ref[slot]
        b_ref, held = find(b_refs, slot)
        low = b_ref.shape[1] - B_ROWS
        wout_ref[rows_at(owner * OUT_ROWS, OUT_ROWS), :] = b_ref[held, low : low + OUT_ROWS, :]
        up_ref[weight_block(owner)] = b_ref[held, low + OUT_ROWS :, :]

    attended_ref[...] = nt(mixed_ref[...], wout_ref[...])

    for step in range(ROWS // SUB):
        here = slice(step * SUB, (step + 1) * SUB)
        residual = x_ref[here, :].astype(f32) + (attended_ref[here, :] + vec_ref[4:5, :])
        resid_ref[here, :] = residual
        scaled, _ = norm_parts(residual)
        second = (scaled * vec_ref[5:6, :] + vec_ref[6:7, :]).astype(bf16)
        second_ref[here, :] = second
        normed_ref[here, :] = second
        wide = jnp.concatenate([keep_ref[here, :]] * (D // 128), axis=1)
        branch_low[here, :] = (cot_ref[here, :].astype(f32) * wide).astype(bf16)
    branch_t[...] = branch_low[:OWN_ALL, :].T

    def products(chunk):
        for half in range(2):
            columns = slice(chunk * D + half * HALF, chunk * D + (half + 1) * HALF)
            ring = slice(chunk % 2 * D + half * HALF, chunk % 2 * D + (half + 1) * HALF)
            pre_ref[:, ring] = nn(normed_ref[...], up_ref[:, columns])
            yield
            yield

    def slopes(chunk):
        columns = slice(chunk * D, (chunk + 1) * D)
        ring = slice(chunk % 2 * D, chunk % 2 * D + D)
        for step in range(ROWS // 16):
            here = slice(step * 16, step * 16 + 16)
            pre = pre_ref[here, ring] + vec_ref[8 + chunk : 9 + chunk, :]
            phi = 0.5 + 0.5 * lax.erf(pre * INV_ROOT_TWO)
            slope_ref[here, columns] = (phi + pre * (jnp.exp(-0.5 * pre * pre) * INV_ROOT_TAU)).astype(bf16)
            hid_ref[here, columns] = (pre * phi).astype(bf16)
            if step % 10 == 9:
                yield

    def weights(chunk):
        for half in range(2):
            columns = slice(chunk * D + half * HALF, chunk * D + (half + 1) * HALF)
            gdown = nn(branch_t[...], hid_ref[:OWN_ALL, columns])
            gdown_ref[chunk, :, half * HALF : (half + 1) * HALF] = gdown.astype(bf16)
            yield
            yield

    together(products(0))
    together(products(1), slopes(0))
    for chunk in range(2, CHUNKS):
        together(products(chunk), slopes(chunk - 1), weights(chunk - 2))
    together(slopes(CHUNKS - 1), weights(CHUNKS - 2))
    together(weights(CHUNKS - 1))
    write_grads(own_down_ref, (kept_ref, sent_ref), gdown_ref)


def down_kernel(
    own_ref, own_down_ref, slope_ref, second_ref, branch_low, *refs,
):
    c_refs, refs = refs[:-8], refs[-8:]
    (
        kept_ref, sent_ref, gpre_ref, down_ref, colsum_ref,
        gup_ref, ghid_ref, second_t,
    ) = refs
    for slot in range(SLOTS):
        c_ref, held = find(c_refs, slot)
        down_ref[weight_block(own_down_ref[slot])] = c_ref[held]
    second_t[:D, :] = second_ref[:OWN_ALL, :].T
    second_t[D:, :] = jnp.ones((16, OWN_ALL), bf16)

    def products(chunk):
        for half in range(2):
            columns = slice(chunk * D + half * HALF, chunk * D + (half + 1) * HALF)
            ring = slice(chunk % 2 * D + half * HALF, chunk % 2 * D + (half + 1) * HALF)
            ghid_ref[:, ring] = nn(branch_low[...], down_ref[:, columns])
            yield
            yield

    def slopes(chunk):
        columns = slice(chunk * D, (chunk + 1) * D)
        ring = slice(chunk % 2 * D, chunk % 2 * D + D)
        for step in range(ROWS // 16):
            here = slice(step * 16, step * 16 + 16)
            gpre_ref[here, columns] = (ghid_ref[here, ring] * slope_ref[here, columns].astype(f32)).astype(bf16)
            if step % 10 == 9:
                yield

    def weights(chunk):
        for half in range(2):
            columns = slice(chunk * D + half * HALF, chunk * D + (half + 1) * HALF)
            gup = nn(second_t[...], gpre_ref[:OWN_ALL, columns])
            gup_ref[chunk, :, half * HALF : (half + 1) * HALF] = gup[:D].astype(bf16)
            colsum_ref[chunk : chunk + 1, half * HALF : (half + 1) * HALF] = gup[D : D + 1]
            yield
            yield

    together(products(0))
    together(products(1), slopes(0))
    for chunk in range(2, CHUNKS):
        together(products(chunk), slopes(chunk - 1), weights(chunk - 2))
    together(slopes(CHUNKS - 1), weights(CHUNKS - 2))
    together(weights(CHUNKS - 1))
    write_grads(own_ref, (kept_ref, sent_ref), gup_ref)


def sum_kernel(hid_ref, gpre_ref, up_ref, down_ref, branch_ref, gsec_ref):
    branch_ref[...] = nt(hid_ref[:OWN_ALL, :], down_ref[...])
    gsec_ref[...] = nt(gpre_ref[...], up_ref[...])


def finish_kernel(
    keep_ref, cot_ref, mixed_ref, resid_ref, branch_ref, gsec_ref, wout_ref, vec_ref,
    out_ref, gres_ref, gout_ref, gmix_ref, sums_ref,
    gatt_ref,
):
    totals = [jnp.zeros((8, D), f32)] * 4
    for step in range(ROWS // SUB):
        here = slice(step * SUB, (step + 1) * SUB)
        wide = jnp.concatenate([keep_ref[here, :]] * (D // 128), axis=1)
        scaled, inverse = norm_parts(resid_ref[here, :])
        grad_out = cot_ref[here, :].astype(f32) * wide
        gsec = gsec_ref[here, :]
        gres = grad_out + norm_back(gsec, scaled, inverse, vec_ref[5:6, :])
        gres_ref[here, :] = gres
        gatt = gres.astype(bf16)
        gatt_ref[here, :] = gatt
        if step < OWN_ALL // SUB:
            parts = (gatt.astype(f32), gsec * scaled, gsec, grad_out.astype(bf16).astype(f32))
            totals = [t + p.reshape(SUB // 8, 8, D).sum(axis=0) for t, p in zip(totals, parts)]
            branch = branch_ref[here, :] + vec_ref[7:8, :]
            out_ref[here, :] = (wide * (resid_ref[here, :] + branch)).astype(bf16)
    for place, total in enumerate(totals):
        sums_ref[place : place + 1, :] = jnp.sum(total, axis=0, keepdims=True)
    gmix_ref[...] = nn(gatt_ref[...], wout_ref[...]).astype(bf16)
    gout_ref[...] = nn(gatt_ref[:OWN_ALL, :].T, mixed_ref[:OWN_ALL, :]).astype(bf16)


def back_kernel(clips, gmix_ref, proj_ref, prob_ref, gproj_ref, lanes_ref, gscore_ref):
    lanes_ref[...] = head_lanes().astype(bf16)
    bands = range(clips[0] * BANDS, (clips[-1] + 1) * BANDS)
    for band in bands:
        places = band_places(band)
        for half in range(2):
            low = half * HALF
            value = load_band(proj_ref, places, slice(2 * D + low, 2 * D + low + HALF))
            grad = load_band(gmix_ref, places, slice(low, low + HALF))
            probs = prob_ref[band, half]
            grad_probs = nt(value, by_head(grad, lanes_ref[...]))
            row_dot = jnp.sum(probs * grad_probs, axis=0, keepdims=True)
            gscore_ref[band - bands[0], half] = (probs * (grad_probs - row_dot)).astype(bf16)
    for band in bands:
        places = band_places(band)
        for half in range(2):
            low = half * HALF
            query = load_band(proj_ref, places, slice(low, low + HALF))
            key = load_band(proj_ref, places, slice(D + low, D + low + HALF))
            grad = load_band(gmix_ref, places, slice(low, low + HALF))
            grad_scores = gscore_ref[band - bands[0], half]
            grad_key = nn(grad_scores, by_head(query, lanes_ref[...])) * SCALE
            grad_value = nn(prob_ref[band, half].astype(bf16), by_head(grad, lanes_ref[...]))
            grad_query = nn(flip_heads(grad_scores), by_head(key, lanes_ref[...])) * SCALE
            for part, values in enumerate((grad_query, grad_key, grad_value)):
                values = values.astype(bf16)
                for rows, place in ((values[:EDGE], places[0]), (values[EDGE:], places[1])):
                    if place.start < OWN_ALL:
                        start = place.start - clips[0] * OWN
                        gproj_ref[start : start + EDGE, part * D + low : part * D + low + HALF] = rows


def project_kernel(
    own_ref, gproj_a, gproj_b, gout_ref, scaled_ref, wqkv_ref, vec_ref, sums_ref, colsum_ref,
    kept_ref, *refs,
):
    *sent_refs, gqkv_ref, gvec_ref = refs
    totals = jnp.zeros((8, 3 * D), f32)
    for step in range(OWN_ALL // 2 // SUB):
        here = slice(step * SUB, (step + 1) * SUB)
        for gproj_ref in (gproj_a, gproj_b):
            totals = totals + gproj_ref[here, :].astype(f32).reshape(SUB // 8, 8, 3 * D).sum(axis=0)
    totals = jnp.sum(totals, axis=0, keepdims=True)
    gvec_ref[...] = jnp.zeros_like(gvec_ref)
    gain_grad = jnp.zeros((8, D), f32)
    shift_grad = jnp.zeros((1, D), f32)
    for part in range(3):
        columns = slice(part * D, (part + 1) * D)
        gproj_t = jnp.concatenate([gproj_a[:, columns].T, gproj_b[:, columns].T], axis=1)
        product = nn(gproj_t, scaled_ref[:OWN_ALL, :])
        total = totals[:, part * D : (part + 1) * D]
        weight = wqkv_ref[part * D : (part + 1) * D, :]
        both = product * weight.astype(f32)
        gain_grad = gain_grad + both.reshape(D // 8, 8, D).sum(axis=0)
        high = total.astype(bf16)
        rest = (total - high.astype(f32)).astype(bf16)
        shift_grad = shift_grad + nn(high, weight) + nn(rest, weight)
        column = jnp.broadcast_to(total, (8, D)).T[:, 0:1]
        gqkv = product * vec_ref[0:1, :] + column * vec_ref[1:2, :]
        gqkv_ref[part * D : (part + 1) * D, :] = gqkv.astype(bf16)
    gvec_ref[0:1, :] = jnp.sum(gain_grad, axis=0, keepdims=True)
    gvec_ref[1:2, :] = shift_grad
    gvec_ref[2:3, :] = totals[:, :D]
    gvec_ref[3:4, :] = totals[:, 2 * D :]
    gvec_ref[4:8, :] = sums_ref[0:4, :]
    gvec_ref[8:12, :] = colsum_ref[0:4, :]
    for slot in range(SLOTS):
        owner = own_ref[slot]
        held = slot % NEAR * G_ROWS
        for low in range(0, G_ROWS, 16):
            if low < QKV_ROWS:
                rows = gqkv_ref[rows_at(owner * QKV_ROWS + low, 16), :]
            else:
                rows = gout_ref[rows_at(owner * OUT_ROWS + low - QKV_ROWS, 16), :]
            grads_ref, place = find_row([kept_ref] if slot < NEAR else sent_refs, held + low)
            grads_ref[place : place + 16, :] = rows
    for refs in ([kept_ref], sent_refs):
        grads_ref, place = find_row(refs, NEAR * G_ROWS)
        grads_ref[place : place + V_ROWS, :] = gvec_ref[:V_ROWS, :].astype(bf16)


def find_row(pieces, row):
    for piece in pieces:
        if row < piece.shape[0]:
            return piece, row
        row -= piece.shape[0]


def share_kernel(first_ref, *refs, end_to_end=False):
    pieces, outs = refs[:-4], refs[-4:]
    size = outs[0].shape[0] - V_ROWS

    def total(start):
        result = first_ref[start : start + 16, :].astype(f32)
        for found, row in [find_row(pieces, start)] if end_to_end else [(piece, start) for piece in pieces]:
            result = result + found[row : row + 16, :].astype(f32)
        return result

    vectors = total(4 * size)
    for part, out_ref in enumerate(outs):
        for low in range(0, size, 16):
            out_ref[low : low + 16, :] = total(part * size + low).astype(out_ref.dtype)
        out_ref[size:, :] = vectors.astype(out_ref.dtype)


def token_kernel(gproj_a, gproj_b, x_ref, gres_ref, wqkv_ref, vec_ref, gtok_ref):
    for step in range(OWN_ALL // STEP):
        here = slice(step * STEP, (step + 1) * STEP)
        gproj_ref, steps = (gproj_a, gproj_b)[step * STEP * 2 // OWN_ALL], OWN_ALL // 2 // STEP
        rows = slice(step % steps * STEP, (step % steps + 1) * STEP)
        gnormed = nn(gproj_ref[rows, :], wqkv_ref[...])
        scaled, inverse = norm_parts(x_ref[here, :].astype(f32))
        gtok_ref[here, :] = gres_ref[here, :] + norm_back(gnormed, scaled, inverse, vec_ref[0:1, :])


def total_kernel(device_ref, *refs):
    *pieces, gqkv_ref, gout_ref, gvec_ref = refs
    total = pieces[0][...]
    for piece in pieces[1:]:
        total = total + piece[...].astype(f32)
    gqkv_ref[...] = total[:QKV_ROWS]
    gout_ref[...] = total[QKV_ROWS:G_ROWS]
    own = pltpu.roll(total[G_ROWS:], lax.rem(D - device_ref[0] * OUT_ROWS, D), 1)
    gvec_ref[...] = own[: gvec_ref.shape[0], : gvec_ref.shape[1]]


def call(kernel, args, outs, scratch, micros, mib):
    smem, vmem = pl.BlockSpec(memory_space=pltpu.SMEM), pl.BlockSpec(memory_space=pltpu.VMEM)
    return pl.pallas_call(
        kernel,
        out_shape=[jax.ShapeDtypeStruct(s, t) for s, t in outs],
        in_specs=[smem if a.dtype == jnp.int32 else vmem for a in args],
        out_specs=[vmem] * len(outs),
        scratch_shapes=[pltpu.VMEM(s, t) for s, t in scratch],
        compiler_params=pltpu.CompilerParams(vmem_limit_bytes=mib * 1024 * 1024),
        cost_estimate=pl.CostEstimate(flops=int(micros * 1.1e9), bytes_accessed=2**20, transcendentals=0),
    )(*args)


def swap(array, mask, other=None):
    count = lax.axis_size("dp") * lax.axis_size("tensor")
    masks = (mask, mask if other is None else other)
    return lax.ppermute(array, BOTH, [(device, device ^ masks[device % 2]) for device in range(count)])


ALONG_Z, ALONG_Y, ALONG_X, CORES = (8, 16, 24), 2, 4, 1
ALONG_XY = (ALONG_Y, ALONG_X, ALONG_Y ^ ALONG_X)


def owners(device, swapped, line_first=True, turn=None):
    def one(second_core):
        first = ALONG_X if second_core and swapped else ALONG_Y
        plane = [0, first, first ^ ALONG_XY[2], ALONG_XY[2]]
        line = [0, *ALONG_Z]
        if turn is not None and second_core != turn:
            line = [line[0], line[2], line[1], line[3]]
        return [m ^ o for o in plane for m in line] if line_first else [m ^ o for o in line for m in plane]

    core = device % 2
    first = jnp.where(core == 0, jnp.array(one(0)), jnp.array(one(1)))
    second = jnp.where(core == 0, jnp.array(one(1)), jnp.array(one(0))) ^ CORES
    return (device ^ jnp.concatenate([first, second])).astype(jnp.int32)


def gather(held, phase):
    return [held] + [swap(held, mask) for mask in phase]


def both_cores(pieces):
    return pieces + [swap(piece, CORES) for piece in pieces]


def wide(array):
    return array.astype(f32)


def add_all(total, others):
    for other in others:
        total = total + wide(other)
    return total


def after(array, *others):
    return lax.optimization_barrier((array,) + others)[0]


def neighbours(array, axis_name, width):
    count = lax.axis_size(axis_name)
    up = [(i, i + 1) for i in range(count - 1)]
    low = lax.ppermute(array[..., -width:, :], axis_name, up)
    high = lax.ppermute(array[..., :width, :], axis_name, [(b, a) for a, b in up])
    return low, high


def shards(tokens, valid, w_qkv, w_out, vectors, w_up, w_down, cotangent):
    devices_dp, devices_t = lax.axis_size("dp"), lax.axis_size("tensor")
    near = devices_dp == 8 and devices_t == 4
    rank = lax.axis_index("tensor")

    own_time = jnp.broadcast_to((jnp.arange(OWN) // FREQ)[None], (CLIPS, OWN)).reshape(-1)
    edge_time = jnp.arange(BAND) // FREQ + jnp.where(jnp.arange(BAND) < EDGE, -SHIFT, OWN // FREQ - SHIFT)
    edge_time = jnp.broadcast_to(edge_time[None], (CLIPS, BAND)).reshape(-1)
    time = jnp.concatenate([own_time, edge_time]) + rank * (OWN // FREQ)
    limit = valid * ROW_UNIT
    limit = jnp.concatenate([jnp.repeat(limit, OWN), jnp.repeat(limit, BAND)])
    keep = jnp.where((time >= 0) & (time < limit), 1.0, 0.0).astype(f32)
    keep = jnp.broadcast_to(keep[:, None], (ROWS, 128))

    if near:
        device = lax.axis_index("dp") * devices_t + rank
        own_near, own_far = owners(device, False), owners(device, True)
        own_down, own_up = owners(device, True, False, 0), owners(device, True, True, 1)
        block = pl.pallas_call(
            pack_kernel,
            out_shape=jax.ShapeDtypeStruct((A_ROWS + B_ROWS, D), bf16),
            in_specs=[pl.BlockSpec(memory_space=pl.ANY)] * 4,
            out_specs=pl.BlockSpec(memory_space=pltpu.VMEM),
            scratch_shapes=[pltpu.VMEM(vectors.shape, bf16), pltpu.SemaphoreType.DMA((4,))],
            compiler_params=pltpu.CompilerParams(vmem_limit_bytes=60 * 1024 * 1024),
        )(w_qkv.T, vectors, w_out.T, w_up)
        edges = neighbours(jnp.stack([tokens, cotangent]), "tensor", EDGE)
        line = gather(block[None], ALONG_Z)
        down = w_down.T[None]
        down = jnp.concatenate([down, swap(down, ALONG_Y, ALONG_X)], axis=0)
        down = [down, swap(down, ALONG_X, ALONG_Y)]
        line, down, keep, own_near, own_far, own_down, own_up = lax.optimization_barrier(
            (line, down, keep, own_near, own_far, own_down, own_up)
        )
        line, down = jnp.concatenate(line, axis=0), jnp.concatenate(down, axis=0)
        near_pieces = swap(line, ALONG_Y, ALONG_X)
        down = [down, swap(down, ALONG_Z[0], ALONG_Z[1])]
        near_pieces, down, edges = lax.optimization_barrier((near_pieces, down, edges))
        down = jnp.concatenate(down, axis=0)
        near_pieces = jnp.concatenate([line, near_pieces], axis=0)
        a_far = swap(near_pieces[:, :A_ROWS], ALONG_X, ALONG_Y)
        b_far = swap(near_pieces[:, A_ROWS:], ALONG_X, ALONG_Y)
        pieces = both_cores([near_pieces])
        a_pieces = [pieces[0], a_far, pieces[1], swap(a_far, CORES)]
        c_pieces = [down, swap(down, ALONG_Z[1], ALONG_Z[0])]
    else:
        own_near = own_far = own_down = own_up = jnp.arange(SLOTS, dtype=jnp.int32)
        edges = neighbours(jnp.stack([tokens, cotangent]), "tensor", EDGE)
        qkv, out, vec = (lax.all_gather(a, BOTH, axis=1, tiled=True).T for a in (w_qkv, w_out, vectors))
        vec = jnp.pad(vec, ((0, 0), (0, D - vec.shape[1])))
        up = lax.all_gather(lax.all_gather(w_up, "dp", axis=0, tiled=True), "tensor", axis=1, tiled=True)
        down = lax.all_gather(lax.all_gather(w_down, "dp", axis=1, tiled=True), "tensor", axis=0, tiled=True).T
        up, down = (
            a.reshape(SLOTS // CHUNKS, UP_ROWS, CHUNKS, D).transpose(0, 2, 1, 3).reshape(SLOTS, UP_ROWS, D)
            for a in (up, down)
        )
        a_slots = jnp.concatenate([a.reshape(SLOTS, -1, D) for a in (qkv, vec)], axis=1)
        b_slots = jnp.concatenate([out.reshape(SLOTS, -1, D), up], axis=1)
        a_pieces, b_pieces, c_pieces = (
            [a[i : i + PIECE] for i in range(0, SLOTS, PIECE)] for a in (a_slots, b_slots, down)
        )

    edges = jnp.concatenate(edges, axis=2).reshape(2, CLIPS * BAND, D)
    x = jnp.concatenate([tokens.reshape(OWN_ALL, D), edges[0]], axis=0)
    cot = jnp.concatenate([cotangent.reshape(OWN_ALL, D), edges[1]], axis=0)
    proj, probs, mixed, scaled, wqkv, vec = call(
        attend_kernel, [own_far, keep, x, *a_pieces],
        [
            ((ROWS, 3 * D), bf16), ((CLIPS * BANDS, 2, BAND, HALF), f32), ((ROWS, D), bf16), ((ROWS, D), bf16),
            ((3 * D, D), bf16), ((16, D), f32),
        ],
        [((D, 128), f32), ((HALF, HALF), bf16), ((BAND, HALF), f32), ((ROWS, D), bf16)],
        0.1, 16,
    )
    if near:
        b_far, c_pieces, proj = lax.optimization_barrier((b_far, c_pieces, proj))
        b_pieces = [pieces[0], b_far, pieces[1], swap(b_far, CORES)]
        c_pieces = both_cores(c_pieces)
    dn_kept, dn_sent, resid, hid, slope, second, branch_low, up_all, wout = call(
        up_kernel, [own_far, own_down, keep, cot, x, mixed, vec, *b_pieces],
        [
            ((NEAR, UP_ROWS, D), bf16), ((NEAR, UP_ROWS, D), bf16), ((ROWS, D), f32), ((ROWS, FF), bf16),
            ((ROWS, FF), bf16), ((ROWS, D), bf16), ((ROWS, D), bf16), ((D, FF), bf16), ((D, D), bf16),
        ],
        [
            ((CHUNKS, D, D), bf16), ((ROWS, 2 * D), f32), ((D, OWN_ALL), bf16), ((ROWS, D), f32), ((ROWS, D), bf16),
        ],
        8, 25,
    )
    up_kept, up_sent, gpre, down_all, colsum = call(
        down_kernel, [own_up, own_down, slope, second, branch_low, *c_pieces],
        [
            ((NEAR, UP_ROWS, D), bf16), ((NEAR, UP_ROWS, D), bf16), ((ROWS, FF), bf16), ((D, FF), bf16), ((8, D), f32),
        ],
        [((CHUNKS, D, D), bf16), ((ROWS, 2 * D), f32), ((D + 16, OWN_ALL), bf16)],
        8, 20,
    )
    if near:
        dn_sum = wide(dn_kept) + wide(after(swap(dn_sent, CORES), gpre))
        gpre, dn_far = lax.optimization_barrier((gpre, dn_sum[NEAR // 2 :].astype(bf16)))
    branch, gsec = call(
        sum_kernel, [hid, gpre, up_all, down_all], [((OWN_ALL, D), f32), ((ROWS, D), f32)], [], 0.1, 13,
    )
    if near:
        up_sum = wide(up_kept) + wide(after(swap(up_sent, CORES), gsec))
        up_far = up_sum[NEAR // 2 :].astype(bf16)
        gsec, up_far, dn_far = lax.optimization_barrier((gsec, up_far, dn_far))
    out, gres, gout, gmix, sums = call(
        finish_kernel, [keep, cot, mixed, resid, branch, gsec, wout, vec],
        [
            ((OWN_ALL, D), bf16), ((ROWS, D), f32), ((D, D), bf16), ((ROWS, D), bf16), ((8, D), f32),
        ],
        [((ROWS, D), bf16)],
        0.1, 16,
    )
    def attend_back(*clips):
        rows = len(clips) * OWN
        return call(
            functools.partial(back_kernel, clips), [gmix, proj, probs], [((rows, 3 * D), bf16)],
            [((HALF, HALF), bf16), ((len(clips) * BANDS, 2, BAND, HALF), bf16)], 0.1, 12,
        )[0]

    gproj_a, gproj_b = attend_back(0, 1), attend_back(2, 3)
    if near:
        up_arrived, gproj_a, gproj_b = lax.optimization_barrier((swap(up_far, ALONG_X, ALONG_Y), gproj_a, gproj_b))
        up_sum = up_sum[: NEAR // 2] + wide(up_arrived)
        up_near, gproj_a, gproj_b = lax.optimization_barrier((up_sum[PIECE:].astype(bf16), gproj_a, gproj_b))
    at_kept, *at_sent = call(
        project_kernel, [own_near, gproj_a, gproj_b, gout, scaled, wqkv, vec, sums, colsum],
        [((NEAR * G_ROWS + V_ROWS, D), bf16)] + [((AT_ROWS // PARTS, D), bf16)] * PARTS,
        [((3 * D, D), bf16), ((128, D), f32)],
        0.1, 16,
    )
    if near:
        up_arrived, at_sent[-1] = lax.optimization_barrier((swap(up_near, ALONG_Y, ALONG_X), at_sent[-1]))
        at_arrived = [swap(piece, CORES) for piece in at_sent]
        up_arrived, dn_arrived, at_arrived, gproj_a = lax.optimization_barrier(
            (up_arrived, swap(dn_far, ALONG_Z[1], ALONG_Z[0]), at_arrived, gproj_a)
        )
    (gtok,) = call(
        token_kernel, [gproj_a, gproj_b, x, gres, wqkv, vec], [((OWN_ALL, D), f32)], [], 0.1, 12,
    )
    if near:
        at_sum, *at_rest = call(
            functools.partial(share_kernel, end_to_end=True), [at_kept, *at_arrived],
            [((PIECE * G_ROWS + V_ROWS, D), t) for t in (f32, bf16, bf16, bf16)], [], 0.1, 8,
        )
        dn_sum = dn_sum[: NEAR // 2] + wide(dn_arrived)
        up_sum = up_sum[:PIECE] + wide(up_arrived)
        at_arrived = [swap(piece, mask) for piece, mask in zip(at_rest, ALONG_XY)]
        ff_arrived = jnp.concatenate([dn_sum[PIECE:], up_sum[2:]], axis=0).astype(bf16)
        ff_arrived = swap(ff_arrived, ALONG_Z[0], ALONG_Z[1])
        ff_arrived, gtok = lax.optimization_barrier((ff_arrived, gtok))
        dn_sum, up_sum = dn_sum[:PIECE] + wide(ff_arrived[:PIECE]), up_sum[:2] + wide(ff_arrived[PIECE:])
        up_arrived = swap(up_sum[1:].astype(bf16), ALONG_Z[1], ALONG_Z[0])
        dn_rest = dn_sum.astype(bf16)
        dn_arrived = [
            swap(dn_rest[1:2], ALONG_Y, ALONG_X), swap(dn_rest[2:3], ALONG_X, ALONG_Y), swap(dn_rest[3:], ALONG_XY[2]),
        ]
        at_arrived, up_arrived = lax.optimization_barrier((at_arrived, up_arrived))
        at_sum, *at_rest = call(
            share_kernel, [at_sum, *at_arrived],
            [((G_ROWS + V_ROWS, D), t) for t in (f32, bf16, bf16, bf16)], [], 0.1, 8,
        )
        up_sum = up_sum[0] + wide(up_arrived)[0]
        dn_sum = add_all(dn_sum[:1], dn_arrived)[0]
        at_arrived = [swap(piece, mask) for piece, mask in zip(at_rest, ALONG_Z)]
        g_qkv, g_out, g_vec = call(
            total_kernel, [device.astype(jnp.int32)[None], at_sum, *at_arrived],
            [((QKV_ROWS, D), f32), ((OUT_ROWS, D), f32), (vectors.shape, f32)], [], 0.1, 4,
        )
    if near:
        g_up, g_down = up_sum, dn_sum.T
        g_qkv, g_out = g_qkv.T, g_out.T
    else:
        at_grads = jnp.concatenate([at_kept[: NEAR * G_ROWS], *at_sent], axis=0)
        at_grads = at_grads[: SLOTS * G_ROWS].reshape(SLOTS, G_ROWS, D)

        def whole(array):
            blocks = array.reshape(SLOTS // CHUNKS, CHUNKS, UP_ROWS, D).transpose(0, 2, 1, 3)
            return blocks.reshape(D, FF)

        g_up = lax.psum_scatter(whole(jnp.concatenate([up_kept, up_sent], axis=0)), "dp", scatter_dimension=0, tiled=True)
        g_up = lax.psum_scatter(g_up, "tensor", scatter_dimension=1, tiled=True).astype(f32)
        g_down = lax.psum_scatter(whole(jnp.concatenate([dn_kept, dn_sent], axis=0)).T, "dp", scatter_dimension=1, tiled=True)
        g_down = lax.psum_scatter(g_down, "tensor", scatter_dimension=0, tiled=True).astype(f32)

        def owned(array):
            return lax.psum_scatter(array.astype(f32), BOTH, scatter_dimension=1, tiled=True)

        g_qkv = owned(at_grads[:, :QKV_ROWS].reshape(-1, D).T)
        g_out = owned(at_grads[:, QKV_ROWS:].reshape(-1, D).T)
        g_vec = owned(at_kept[NEAR * G_ROWS :][: vectors.shape[0]])
    shape = tokens.shape
    return (out.reshape(shape), gtok.reshape(shape), g_qkv, g_out, g_vec, g_up, g_down)


def solution(mesh):
    placed = (
        P("dp", "tensor", None),
        P("dp"),
        P(None, BOTH),
        P(None, BOTH),
        P(None, BOTH),
        P("dp", "tensor"),
        P("tensor", "dp"),
        P("dp", "tensor", None),
    )
    return jax.shard_map(
        shards,
        mesh=mesh,
        in_specs=placed,
        out_specs=(
            P("dp", "tensor", None),
            P("dp", "tensor", None),
            P(None, BOTH),
            P(None, BOTH),
            P(None, BOTH),
            P("dp", "tensor"),
            P("tensor", "dp"),
        ),
        check_vma=False,
    )
```

```python
import functools

import jax
import jax.numpy as jnp
from jax import lax
from jax.experimental import pallas as pl
from jax.experimental.pallas import tpu as pltpu
from jax.sharding import PartitionSpec as P

D = 512
FF = 2048
HEADS = 16
HEAD = D // HEADS
FREQ = 8
WINDOW = 4
SHIFT = 2
ROW_UNIT = 8

EPS = 1e-06
MASKED = -1000000000.0
SCALE = HEAD ** (-0.5)
INV_ROOT_TWO = 0.7071067811865476
INV_ROOT_TAU = 0.3989422804014327

BOTH = ("dp", "tensor")
SLOTS = 32
NEAR = SLOTS // 2
PIECE = 4
QKV_ROWS = 3 * D // SLOTS
OUT_ROWS = D // SLOTS
A_ROWS = QKV_ROWS + OUT_ROWS
CHUNKS = FF // D
UP_ROWS = D * CHUNKS // SLOTS
B_ROWS = OUT_ROWS + UP_ROWS
G_ROWS = QKV_ROWS + OUT_ROWS
V_ROWS = 16
AT_ROWS = SLOTS // 2 * G_ROWS + V_ROWS
PARTS = 5

CLIPS = 4
OWN = 128
EDGE = 16
OWN_ALL = CLIPS * OWN
ROWS = OWN_ALL + CLIPS * 2 * EDGE
BAND = 2 * EDGE
BANDS = OWN // BAND + 1
HALF = D // 2
HALF_HEADS = HALF // HEAD
STEP = 128
SUB = 32

bf16 = jnp.bfloat16
f32 = jnp.float32


def nn(a, b):
    return lax.dot_general(a, b, (((1,), (0,)), ((), ())), preferred_element_type=f32)


def nt(a, b):
    return lax.dot_general(a, b, (((1,), (1,)), ((), ())), preferred_element_type=f32)


def tn(a, b):
    return lax.dot_general(a, b, (((0,), (0,)), ((), ())), preferred_element_type=f32)


def rows_at(start, size):
    return pl.ds(pl.multiple_of(start, size), size)


def norm_parts(values):
    mean = jnp.mean(values, axis=-1, keepdims=True)
    centred = values - mean
    variance = jnp.mean(centred * centred, axis=-1, keepdims=True)
    inverse = lax.rsqrt(variance + EPS)
    return centred * inverse, inverse


def norm_back(grad, scaled, inverse, gain):
    grad_hat = grad * gain
    centre = jnp.mean(grad_hat, axis=-1, keepdims=True)
    slope = jnp.mean(grad_hat * scaled, axis=-1, keepdims=True)
    return inverse * (grad_hat - centre - scaled * slope)


def band_places(band):
    clip, place = divmod(band, BANDS)
    first = OWN_ALL + clip * BAND if place == 0 else clip * OWN + place * BAND - EDGE
    last = OWN_ALL + clip * BAND + EDGE if place == BANDS - 1 else clip * OWN + place * BAND
    return slice(first, first + EDGE), slice(last, last + EDGE)


def load_band(ref, places, columns):
    return jnp.concatenate([ref[places[0], columns], ref[places[1], columns]], axis=0)


def find(pieces, slot):
    size = pieces[0].shape[0]
    return pieces[slot // size], slot % size


def weight_block(owner):
    return rows_at(owner // CHUNKS * UP_ROWS, UP_ROWS), rows_at(owner % CHUNKS * D, D)


def pack_kernel(qkv_ref, vec_ref, out_ref, up_ref, block_ref, rows_ref, sems):
    here = (
        rows_ref, block_ref.at[:QKV_ROWS], block_ref.at[A_ROWS : A_ROWS + OUT_ROWS], block_ref.at[A_ROWS + OUT_ROWS :],
    )
    copies = [
        pltpu.make_async_copy(there, place, sems.at[i])
        for i, (there, place) in enumerate(zip((vec_ref, qkv_ref, out_ref, up_ref), here))
    ]
    for copy in copies:
        copy.start()
    block_ref[QKV_ROWS:A_ROWS, :] = jnp.zeros((OUT_ROWS, D), bf16)
    row = lax.broadcasted_iota(jnp.int32, (OUT_ROWS, OUT_ROWS), 0)
    lane = lax.broadcasted_iota(jnp.int32, (OUT_ROWS, OUT_ROWS), 1)
    copies[0].wait()
    turned = nt(jnp.where(row == lane, 1.0, 0.0).astype(bf16), rows_ref[...])
    block_ref[QKV_ROWS:A_ROWS, : vec_ref.shape[0]] = turned.astype(bf16)
    for copy in copies[1:]:
        copy.wait()


def head_lanes():
    row = lax.broadcasted_iota(jnp.int32, (HALF, HALF), 0) // HEAD
    lane = lax.broadcasted_iota(jnp.int32, (HALF, HALF), 1) // HEAD
    return jnp.where(row == lane, 1.0, 0.0)


def by_head(rows, lanes):
    return jnp.concatenate([rows] * HALF_HEADS, axis=0) * lanes


def flip_heads(wide):
    turned = wide.T
    return jnp.concatenate([turned[head * BAND : (head + 1) * BAND] for head in range(HALF_HEADS)], axis=1)


def attend_kernel(
    own_ref, keep_ref, x_ref, *refs,
):
    a_refs, refs = refs[:-10], refs[-10:]
    proj_ref, prob_ref, mixed_ref, scaled_ref, wqkv_ref, vec_ref, column_vec, lanes_ref, pair_ref, normed_ref = refs
    for slot in range(SLOTS):
        owner = own_ref[slot]
        a_ref, held = find(a_refs, slot)
        wqkv_ref[rows_at(owner * QKV_ROWS, QKV_ROWS), :] = a_ref[held, :QKV_ROWS, :]
        column_vec[rows_at(owner * OUT_ROWS, OUT_ROWS), :] = a_ref[held, QKV_ROWS:A_ROWS, :128].astype(f32)
    vec_ref[...] = column_vec[...].T[:16, :]
    lanes_ref[...] = head_lanes().astype(bf16)
    key_group = (lax.broadcasted_iota(jnp.int32, (BAND, HALF), 0) % FREQ + SHIFT) // WINDOW
    query_group = (lax.broadcasted_iota(jnp.int32, (BAND, HALF), 1) % FREQ + SHIFT) // WINDOW
    pair_ref[...] = jnp.where(key_group == query_group, 1.0, 0.0)

    for step in range(ROWS // SUB):
        here = slice(step * SUB, (step + 1) * SUB)
        scaled, _ = norm_parts(x_ref[here, :].astype(f32))
        scaled_ref[here, :] = scaled.astype(bf16)
        normed_ref[here, :] = (scaled * vec_ref[0:1, :] + vec_ref[1:2, :]).astype(bf16)
    for part in range(3):
        columns = slice(part * D, (part + 1) * D)
        part_out = nt(normed_ref[...], wqkv_ref[columns, :])
        if part != 1:
            bias = 2 if part == 0 else 3
            part_out = part_out + vec_ref[bias : bias + 1, :]
        proj_ref[:, columns] = part_out.astype(bf16)

    for band in range(CLIPS * BANDS):
        places = band_places(band)
        key_ok = load_band(keep_ref, places, slice(None))
        key_ok = jnp.concatenate([key_ok, key_ok], axis=1) * pair_ref[...] > 0.5
        for half in range(2):
            low = half * HALF
            query = load_band(proj_ref, places, slice(low, low + HALF))
            key = load_band(proj_ref, places, slice(D + low, D + low + HALF))
            scores = nt(key, by_head(query, lanes_ref[...])) * SCALE
            scores = jnp.where(key_ok, scores, MASKED)
            exponent = jnp.exp(scores - jnp.max(scores, axis=0, keepdims=True))
            prob_ref[band, half] = exponent / jnp.sum(exponent, axis=0, keepdims=True)
    for band in range(CLIPS * BANDS):
        places = band_places(band)
        for half in range(2):
            low = half * HALF
            value = load_band(proj_ref, places, slice(2 * D + low, 2 * D + low + HALF))
            probs = flip_heads(prob_ref[band, half].astype(bf16))
            mixed = nn(probs, by_head(value, lanes_ref[...])).astype(bf16)
            mixed_ref[places[0], low : low + HALF] = mixed[:EDGE]
            mixed_ref[places[1], low : low + HALF] = mixed[EDGE:]


def together(*works):
    for _ in range(4):
        for work in works:
            next(work)


def write_grads(own_ref, pieces, block_ref):
    for slot in range(SLOTS):
        grads_ref, held = find(pieces, slot)
        owner = own_ref[slot]
        grads_ref[held] = block_ref[owner % CHUNKS, rows_at(owner // CHUNKS * UP_ROWS, UP_ROWS), :]


def up_kernel(
    own_ref, own_down_ref, keep_ref, cot_ref, x_ref, mixed_ref, vec_ref, *refs,
):
    b_refs, refs = refs[:-14], refs[-14:]
    (
        kept_ref, sent_ref, resid_ref, hid_ref, slope_ref, second_ref, branch_low, up_ref, wout_ref,
        gdown_ref, pre_ref, branch_t, attended_ref, normed_ref,
    ) = refs
    for slot in range(SLOTS):
        owner = own_ref[slot]
        b_ref, held = find(b_refs, slot)
        low = b_ref.shape[1] - B_ROWS
        wout_ref[rows_at(owner * OUT_ROWS, OUT_ROWS), :] = b_ref[held, low : low + OUT_ROWS, :]
        up_ref[weight_block(owner)] = b_ref[held, low + OUT_ROWS :, :]

    attended_ref[...] = nt(mixed_ref[...], wout_ref[...])

    for step in range(ROWS // SUB):
        here = slice(step * SUB, (step + 1) * SUB)
        residual = x_ref[here, :].astype(f32) + (attended_ref[here, :] + vec_ref[4:5, :])
        resid_ref[here, :] = residual
        scaled, _ = norm_parts(residual)
        second = (scaled * vec_ref[5:6, :] + vec_ref[6:7, :]).astype(bf16)
        second_ref[here, :] = second
        normed_ref[here, :] = second
        wide = jnp.concatenate([keep_ref[here, :]] * (D // 128), axis=1)
        branch_low[here, :] = (cot_ref[here, :].astype(f32) * wide).astype(bf16)
    branch_t[...] = branch_low[:OWN_ALL, :].T

    def products(chunk):
        for half in range(2):
            columns = slice(chunk * D + half * HALF, chunk * D + (half + 1) * HALF)
            ring = slice(chunk % 2 * D + half * HALF, chunk % 2 * D + (half + 1) * HALF)
            pre_ref[:, ring] = nn(normed_ref[...], up_ref[:, columns])
            yield
            yield

    def slopes(chunk):
        columns = slice(chunk * D, (chunk + 1) * D)
        ring = slice(chunk % 2 * D, chunk % 2 * D + D)
        for step in range(ROWS // 16):
            here = slice(step * 16, step * 16 + 16)
            pre = pre_ref[here, ring] + vec_ref[8 + chunk : 9 + chunk, :]
            phi = 0.5 + 0.5 * lax.erf(pre * INV_ROOT_TWO)
            slope_ref[here, columns] = (phi + pre * (jnp.exp(-0.5 * pre * pre) * INV_ROOT_TAU)).astype(bf16)
            hid_ref[here, columns] = (pre * phi).astype(bf16)
            if step % 10 == 9:
                yield

    def weights(chunk):
        for half in range(2):
            columns = slice(chunk * D + half * HALF, chunk * D + (half + 1) * HALF)
            gdown = nn(branch_t[...], hid_ref[:OWN_ALL, columns])
            gdown_ref[chunk, :, half * HALF : (half + 1) * HALF] = gdown.astype(bf16)
            yield
            yield

    together(products(0))
    together(products(1), slopes(0))
    for chunk in range(2, CHUNKS):
        together(products(chunk), slopes(chunk - 1), weights(chunk - 2))
    together(slopes(CHUNKS - 1), weights(CHUNKS - 2))
    together(weights(CHUNKS - 1))
    write_grads(own_down_ref, (kept_ref, sent_ref), gdown_ref)


def down_kernel(
    own_ref, own_down_ref, slope_ref, second_ref, branch_low, *refs,
):
    c_refs, refs = refs[:-8], refs[-8:]
    (
        kept_ref, sent_ref, gpre_ref, down_ref, colsum_ref,
        gup_ref, ghid_ref, second_t,
    ) = refs
    for slot in range(SLOTS):
        c_ref, held = find(c_refs, slot)
        down_ref[weight_block(own_down_ref[slot])] = c_ref[held]
    second_t[:D, :] = second_ref[:OWN_ALL, :].T
    second_t[D:, :] = jnp.ones((16, OWN_ALL), bf16)

    def products(chunk):
        for half in range(2):
            columns = slice(chunk * D + half * HALF, chunk * D + (half + 1) * HALF)
            ring = slice(chunk % 2 * D + half * HALF, chunk % 2 * D + (half + 1) * HALF)
            ghid_ref[:, ring] = nn(branch_low[...], down_ref[:, columns])
            yield
            yield

    def slopes(chunk):
        columns = slice(chunk * D, (chunk + 1) * D)
        ring = slice(chunk % 2 * D, chunk % 2 * D + D)
        for step in range(ROWS // 16):
            here = slice(step * 16, step * 16 + 16)
            gpre_ref[here, columns] = (ghid_ref[here, ring] * slope_ref[here, columns].astype(f32)).astype(bf16)
            if step % 10 == 9:
                yield

    def weights(chunk):
        for half in range(2):
            columns = slice(chunk * D + half * HALF, chunk * D + (half + 1) * HALF)
            gup = nn(second_t[...], gpre_ref[:OWN_ALL, columns])
            gup_ref[chunk, :, half * HALF : (half + 1) * HALF] = gup[:D].astype(bf16)
            colsum_ref[chunk : chunk + 1, half * HALF : (half + 1) * HALF] = gup[D : D + 1]
            yield
            yield

    together(products(0))
    together(products(1), slopes(0))
    for chunk in range(2, CHUNKS):
        together(products(chunk), slopes(chunk - 1), weights(chunk - 2))
    together(slopes(CHUNKS - 1), weights(CHUNKS - 2))
    together(weights(CHUNKS - 1))
    write_grads(own_ref, (kept_ref, sent_ref), gup_ref)


def sum_kernel(hid_ref, gpre_ref, up_ref, down_ref, branch_ref, gsec_ref):
    branch_ref[...] = nt(hid_ref[:OWN_ALL, :], down_ref[...])
    gsec_ref[...] = nt(gpre_ref[...], up_ref[...])


def finish_kernel(
    keep_ref, cot_ref, mixed_ref, resid_ref, branch_ref, gsec_ref, wout_ref, vec_ref,
    out_ref, gres_ref, gout_ref, gmix_ref, sums_ref,
    gatt_ref,
):
    totals = [jnp.zeros((8, D), f32)] * 4
    for step in range(ROWS // SUB):
        here = slice(step * SUB, (step + 1) * SUB)
        wide = jnp.concatenate([keep_ref[here, :]] * (D // 128), axis=1)
        scaled, inverse = norm_parts(resid_ref[here, :])
        grad_out = cot_ref[here, :].astype(f32) * wide
        gsec = gsec_ref[here, :]
        gres = grad_out + norm_back(gsec, scaled, inverse, vec_ref[5:6, :])
        gres_ref[here, :] = gres
        gatt = gres.astype(bf16)
        gatt_ref[here, :] = gatt
        if step < OWN_ALL // SUB:
            parts = (gatt.astype(f32), gsec * scaled, gsec, grad_out.astype(bf16).astype(f32))
            totals = [t + p.reshape(SUB // 8, 8, D).sum(axis=0) for t, p in zip(totals, parts)]
            branch = branch_ref[here, :] + vec_ref[7:8, :]
            out_ref[here, :] = (wide * (resid_ref[here, :] + branch)).astype(bf16)
    for place, total in enumerate(totals):
        sums_ref[place : place + 1, :] = jnp.sum(total, axis=0, keepdims=True)
    gmix_ref[...] = nn(gatt_ref[...], wout_ref[...]).astype(bf16)
    gout_ref[...] = nn(gatt_ref[:OWN_ALL, :].T, mixed_ref[:OWN_ALL, :]).astype(bf16)


def back_kernel(clips, gmix_ref, proj_ref, prob_ref, gproj_ref, lanes_ref, gscore_ref):
    lanes_ref[...] = head_lanes().astype(bf16)
    bands = range(clips[0] * BANDS, (clips[-1] + 1) * BANDS)
    for band in bands:
        places = band_places(band)
        for half in range(2):
            low = half * HALF
            value = load_band(proj_ref, places, slice(2 * D + low, 2 * D + low + HALF))
            grad = load_band(gmix_ref, places, slice(low, low + HALF))
            probs = prob_ref[band, half]
            grad_probs = nt(value, by_head(grad, lanes_ref[...]))
            row_dot = jnp.sum(probs * grad_probs, axis=0, keepdims=True)
            gscore_ref[band - bands[0], half] = (probs * (grad_probs - row_dot)).astype(bf16)
    for band in bands:
        places = band_places(band)
        for half in range(2):
            low = half * HALF
            query = load_band(proj_ref, places, slice(low, low + HALF))
            key = load_band(proj_ref, places, slice(D + low, D + low + HALF))
            grad = load_band(gmix_ref, places, slice(low, low + HALF))
            grad_scores = gscore_ref[band - bands[0], half]
            grad_key = nn(grad_scores, by_head(query, lanes_ref[...])) * SCALE
            grad_value = nn(prob_ref[band, half].astype(bf16), by_head(grad, lanes_ref[...]))
            grad_query = nn(flip_heads(grad_scores), by_head(key, lanes_ref[...])) * SCALE
            for part, values in enumerate((grad_query, grad_key, grad_value)):
                values = values.astype(bf16)
                for rows, place in ((values[:EDGE], places[0]), (values[EDGE:], places[1])):
                    if place.start < OWN_ALL:
                        start = place.start - clips[0] * OWN
                        gproj_ref[start : start + EDGE, part * D + low : part * D + low + HALF] = rows


def project_kernel(
    own_ref, gproj_a, gproj_b, gout_ref, scaled_ref, wqkv_ref, vec_ref, sums_ref, colsum_ref,
    kept_ref, *refs,
):
    *sent_refs, gqkv_ref, gvec_ref = refs
    totals = jnp.zeros((8, 3 * D), f32)
    for step in range(OWN_ALL // 2 // SUB):
        here = slice(step * SUB, (step + 1) * SUB)
        for gproj_ref in (gproj_a, gproj_b):
            totals = totals + gproj_ref[here, :].astype(f32).reshape(SUB // 8, 8, 3 * D).sum(axis=0)
    totals = jnp.sum(totals, axis=0, keepdims=True)
    gvec_ref[...] = jnp.zeros_like(gvec_ref)
    gain_grad = jnp.zeros((8, D), f32)
    shift_grad = jnp.zeros((1, D), f32)
    for part in range(3):
        columns = slice(part * D, (part + 1) * D)
        gproj_t = jnp.concatenate([gproj_a[:, columns].T, gproj_b[:, columns].T], axis=1)
        product = nn(gproj_t, scaled_ref[:OWN_ALL, :])
        total = totals[:, part * D : (part + 1) * D]
        weight = wqkv_ref[part * D : (part + 1) * D, :]
        both = product * weight.astype(f32)
        gain_grad = gain_grad + both.reshape(D // 8, 8, D).sum(axis=0)
        high = total.astype(bf16)
        rest = (total - high.astype(f32)).astype(bf16)
        shift_grad = shift_grad + nn(high, weight) + nn(rest, weight)
        column = jnp.broadcast_to(total, (8, D)).T[:, 0:1]
        gqkv = product * vec_ref[0:1, :] + column * vec_ref[1:2, :]
        gqkv_ref[part * D : (part + 1) * D, :] = gqkv.astype(bf16)
    gvec_ref[0:1, :] = jnp.sum(gain_grad, axis=0, keepdims=True)
    gvec_ref[1:2, :] = shift_grad
    gvec_ref[2:3, :] = totals[:, :D]
    gvec_ref[3:4, :] = totals[:, 2 * D :]
    gvec_ref[4:8, :] = sums_ref[0:4, :]
    gvec_ref[8:12, :] = colsum_ref[0:4, :]
    for slot in range(SLOTS):
        owner = own_ref[slot]
        held = slot % NEAR * G_ROWS
        for low in range(0, G_ROWS, 16):
            if low < QKV_ROWS:
                rows = gqkv_ref[rows_at(owner * QKV_ROWS + low, 16), :]
            else:
                rows = gout_ref[rows_at(owner * OUT_ROWS + low - QKV_ROWS, 16), :]
            grads_ref, place = find_row([kept_ref] if slot < NEAR else sent_refs, held + low)
            grads_ref[place : place + 16, :] = rows
    for refs in ([kept_ref], sent_refs):
        grads_ref, place = find_row(refs, NEAR * G_ROWS)
        grads_ref[place : place + V_ROWS, :] = gvec_ref[:V_ROWS, :].astype(bf16)


def find_row(pieces, row):
    for piece in pieces:
        if row < piece.shape[0]:
            return piece, row
        row -= piece.shape[0]


def share_kernel(first_ref, *refs, end_to_end=False):
    pieces, outs = refs[:-4], refs[-4:]
    size = outs[0].shape[0] - V_ROWS

    def total(start):
        result = first_ref[start : start + 16, :].astype(f32)
        for found, row in [find_row(pieces, start)] if end_to_end else [(piece, start) for piece in pieces]:
            result = result + found[row : row + 16, :].astype(f32)
        return result

    vectors = total(4 * size)
    for part, out_ref in enumerate(outs):
        for low in range(0, size, 16):
            out_ref[low : low + 16, :] = total(part * size + low).astype(out_ref.dtype)
        out_ref[size:, :] = vectors.astype(out_ref.dtype)


def token_kernel(gproj_a, gproj_b, x_ref, gres_ref, wqkv_ref, vec_ref, gtok_ref):
    for step in range(OWN_ALL // STEP):
        here = slice(step * STEP, (step + 1) * STEP)
        gproj_ref, steps = (gproj_a, gproj_b)[step * STEP * 2 // OWN_ALL], OWN_ALL // 2 // STEP
        rows = slice(step % steps * STEP, (step % steps + 1) * STEP)
        gnormed = nn(gproj_ref[rows, :], wqkv_ref[...])
        scaled, inverse = norm_parts(x_ref[here, :].astype(f32))
        gtok_ref[here, :] = gres_ref[here, :] + norm_back(gnormed, scaled, inverse, vec_ref[0:1, :])


def total_kernel(device_ref, *refs):
    *pieces, gqkv_ref, gout_ref, gvec_ref = refs
    total = pieces[0][...]
    for piece in pieces[1:]:
        total = total + piece[...].astype(f32)
    gqkv_ref[...] = total[:QKV_ROWS]
    gout_ref[...] = total[QKV_ROWS:G_ROWS]
    own = pltpu.roll(total[G_ROWS:], lax.rem(D - device_ref[0] * OUT_ROWS, D), 1)
    gvec_ref[...] = own[: gvec_ref.shape[0], : gvec_ref.shape[1]]


def call(kernel, args, outs, scratch, micros, mib):
    smem, vmem = pl.BlockSpec(memory_space=pltpu.SMEM), pl.BlockSpec(memory_space=pltpu.VMEM)
    return pl.pallas_call(
        kernel,
        out_shape=[jax.ShapeDtypeStruct(s, t) for s, t in outs],
        in_specs=[smem if a.dtype == jnp.int32 else vmem for a in args],
        out_specs=[vmem] * len(outs),
        scratch_shapes=[pltpu.VMEM(s, t) for s, t in scratch],
        compiler_params=pltpu.CompilerParams(vmem_limit_bytes=mib * 1024 * 1024),
        cost_estimate=pl.CostEstimate(flops=int(micros * 1.1e9), bytes_accessed=2**20, transcendentals=0),
    )(*args)


def swap(array, mask, other=None):
    count = lax.axis_size("dp") * lax.axis_size("tensor")
    masks = (mask, mask if other is None else other)
    return lax.ppermute(array, BOTH, [(device, device ^ masks[device % 2]) for device in range(count)])


ALONG_Z, ALONG_Y, ALONG_X, CORES = (16, 8, 24), 2, 4, 1
ALONG_XY = (ALONG_Y, ALONG_X, ALONG_Y ^ ALONG_X)


def owners(device, swapped, line_first=True, turn=None, second_first=True):
    def one(second_core):
        first = ALONG_X if swapped and bool(second_core) == second_first else ALONG_Y
        plane = [0, first, first ^ ALONG_XY[2], ALONG_XY[2]]
        line = [0, *ALONG_Z]
        if turn is not None and second_core != turn:
            line = [line[0], line[2], line[1], line[3]]
        return [m ^ o for o in plane for m in line] if line_first else [m ^ o for o in line for m in plane]

    core = device % 2
    first = jnp.where(core == 0, jnp.array(one(0)), jnp.array(one(1)))
    second = jnp.where(core == 0, jnp.array(one(1)), jnp.array(one(0))) ^ CORES
    return (device ^ jnp.concatenate([first, second])).astype(jnp.int32)


def gather(held, phase):
    return [held] + [swap(held, mask) for mask in phase]


def both_cores(pieces):
    return pieces + [swap(piece, CORES) for piece in pieces]


def wide(array):
    return array.astype(f32)


def add_all(total, others):
    for other in others:
        total = total + wide(other)
    return total


def after(array, *others):
    return lax.optimization_barrier((array,) + others)[0]


def neighbours(array, axis_name, width):
    count = lax.axis_size(axis_name)
    up = [(i, i + 1) for i in range(count - 1)]
    low = lax.ppermute(array[..., -width:, :], axis_name, up)
    high = lax.ppermute(array[..., :width, :], axis_name, [(b, a) for a, b in up])
    return low, high


def shards(tokens, valid, w_qkv, w_out, vectors, w_up, w_down, cotangent):
    devices_dp, devices_t = lax.axis_size("dp"), lax.axis_size("tensor")
    near = devices_dp == 8 and devices_t == 4
    rank = lax.axis_index("tensor")

    own_time = jnp.broadcast_to((jnp.arange(OWN) // FREQ)[None], (CLIPS, OWN)).reshape(-1)
    edge_time = jnp.arange(BAND) // FREQ + jnp.where(jnp.arange(BAND) < EDGE, -SHIFT, OWN // FREQ - SHIFT)
    edge_time = jnp.broadcast_to(edge_time[None], (CLIPS, BAND)).reshape(-1)
    time = jnp.concatenate([own_time, edge_time]) + rank * (OWN // FREQ)
    limit = valid * ROW_UNIT
    limit = jnp.concatenate([jnp.repeat(limit, OWN), jnp.repeat(limit, BAND)])
    keep = jnp.where((time >= 0) & (time < limit), 1.0, 0.0).astype(f32)
    keep = jnp.broadcast_to(keep[:, None], (ROWS, 128))

    if near:
        device = lax.axis_index("dp") * devices_t + rank
        own_near, own_far = owners(device, False), owners(device, True, second_first=False)
        own_down, own_up = owners(device, True, False, 0), owners(device, True, True, 1)
        block = pl.pallas_call(
            pack_kernel,
            out_shape=jax.ShapeDtypeStruct((A_ROWS + B_ROWS, D), bf16),
            in_specs=[pl.BlockSpec(memory_space=pl.ANY)] * 4,
            out_specs=pl.BlockSpec(memory_space=pltpu.VMEM),
            scratch_shapes=[pltpu.VMEM(vectors.shape, bf16), pltpu.SemaphoreType.DMA((4,))],
            compiler_params=pltpu.CompilerParams(vmem_limit_bytes=60 * 1024 * 1024),
        )(w_qkv.T, vectors, w_out.T, w_up)
        edges = neighbours(jnp.stack([tokens, cotangent]), "tensor", EDGE)
        line = gather(block[None], ALONG_Z)
        down = w_down.T[None]
        down = jnp.concatenate([down, swap(down, ALONG_Y, ALONG_X)], axis=0)
        down = [down, swap(down, ALONG_X, ALONG_Y)]
        line, down, keep, own_near, own_far, own_down, own_up = lax.optimization_barrier(
            (line, down, keep, own_near, own_far, own_down, own_up)
        )
        line, down = jnp.concatenate(line, axis=0), jnp.concatenate(down, axis=0)
        near_pieces = swap(line, ALONG_X, ALONG_Y)
        down = [down, swap(down, ALONG_Z[0], ALONG_Z[1])]
        near_pieces, down, edges = lax.optimization_barrier((near_pieces, down, edges))
        down = jnp.concatenate(down, axis=0)
        near_pieces = jnp.concatenate([line, near_pieces], axis=0)
        a_far = swap(near_pieces[:, :A_ROWS], ALONG_Y, ALONG_X)
        b_far = swap(near_pieces[:, A_ROWS:], ALONG_Y, ALONG_X)
        pieces = both_cores([near_pieces])
        a_pieces = [pieces[0], a_far, pieces[1], swap(a_far, CORES)]
        c_pieces = [down, swap(down, ALONG_Z[1], ALONG_Z[0])]
    else:
        own_near = own_far = own_down = own_up = jnp.arange(SLOTS, dtype=jnp.int32)
        edges = neighbours(jnp.stack([tokens, cotangent]), "tensor", EDGE)
        qkv, out, vec = (lax.all_gather(a, BOTH, axis=1, tiled=True).T for a in (w_qkv, w_out, vectors))
        vec = jnp.pad(vec, ((0, 0), (0, D - vec.shape[1])))
        up = lax.all_gather(lax.all_gather(w_up, "dp", axis=0, tiled=True), "tensor", axis=1, tiled=True)
        down = lax.all_gather(lax.all_gather(w_down, "dp", axis=1, tiled=True), "tensor", axis=0, tiled=True).T
        up, down = (
            a.reshape(SLOTS // CHUNKS, UP_ROWS, CHUNKS, D).transpose(0, 2, 1, 3).reshape(SLOTS, UP_ROWS, D)
            for a in (up, down)
        )
        a_slots = jnp.concatenate([a.reshape(SLOTS, -1, D) for a in (qkv, vec)], axis=1)
        b_slots = jnp.concatenate([out.reshape(SLOTS, -1, D), up], axis=1)
        a_pieces, b_pieces, c_pieces = (
            [a[i : i + PIECE] for i in range(0, SLOTS, PIECE)] for a in (a_slots, b_slots, down)
        )

    edges = jnp.concatenate(edges, axis=2).reshape(2, CLIPS * BAND, D)
    x = jnp.concatenate([tokens.reshape(OWN_ALL, D), edges[0]], axis=0)
    cot = jnp.concatenate([cotangent.reshape(OWN_ALL, D), edges[1]], axis=0)
    proj, probs, mixed, scaled, wqkv, vec = call(
        attend_kernel, [own_far, keep, x, *a_pieces],
        [
            ((ROWS, 3 * D), bf16), ((CLIPS * BANDS, 2, BAND, HALF), f32), ((ROWS, D), bf16), ((ROWS, D), bf16),
            ((3 * D, D), bf16), ((16, D), f32),
        ],
        [((D, 128), f32), ((HALF, HALF), bf16), ((BAND, HALF), f32), ((ROWS, D), bf16)],
        0.1, 16,
    )
    if near:
        b_far, c_pieces, proj = lax.optimization_barrier((b_far, c_pieces, proj))
        b_pieces = [pieces[0], b_far, pieces[1], swap(b_far, CORES)]
        c_pieces = both_cores(c_pieces)
    dn_kept, dn_sent, resid, hid, slope, second, branch_low, up_all, wout = call(
        up_kernel, [own_far, own_down, keep, cot, x, mixed, vec, *b_pieces],
        [
            ((NEAR, UP_ROWS, D), bf16), ((NEAR, UP_ROWS, D), bf16), ((ROWS, D), f32), ((ROWS, FF), bf16),
            ((ROWS, FF), bf16), ((ROWS, D), bf16), ((ROWS, D), bf16), ((D, FF), bf16), ((D, D), bf16),
        ],
        [
            ((CHUNKS, D, D), bf16), ((ROWS, 2 * D), f32), ((D, OWN_ALL), bf16), ((ROWS, D), f32), ((ROWS, D), bf16),
        ],
        8, 25,
    )
    up_kept, up_sent, gpre, down_all, colsum = call(
        down_kernel, [own_up, own_down, slope, second, branch_low, *c_pieces],
        [
            ((NEAR, UP_ROWS, D), bf16), ((NEAR, UP_ROWS, D), bf16), ((ROWS, FF), bf16), ((D, FF), bf16), ((8, D), f32),
        ],
        [((CHUNKS, D, D), bf16), ((ROWS, 2 * D), f32), ((D + 16, OWN_ALL), bf16)],
        8, 20,
    )
    if near:
        dn_sum = wide(dn_kept) + wide(after(swap(dn_sent, CORES), gpre))
        gpre, dn_far = lax.optimization_barrier((gpre, dn_sum[NEAR // 2 :].astype(bf16)))
    branch, gsec = call(
        sum_kernel, [hid, gpre, up_all, down_all], [((OWN_ALL, D), f32), ((ROWS, D), f32)], [], 0.1, 13,
    )
    if near:
        up_sum = wide(up_kept) + wide(after(swap(up_sent, CORES), gsec))
        up_far = up_sum[NEAR // 2 :].astype(bf16)
        gsec, up_far, dn_far = lax.optimization_barrier((gsec, up_far, dn_far))
    out, gres, gout, gmix, sums = call(
        finish_kernel, [keep, cot, mixed, resid, branch, gsec, wout, vec],
        [
            ((OWN_ALL, D), bf16), ((ROWS, D), f32), ((D, D), bf16), ((ROWS, D), bf16), ((8, D), f32),
        ],
        [((ROWS, D), bf16)],
        0.1, 16,
    )
    def attend_back(*clips):
        rows = len(clips) * OWN
        return call(
            functools.partial(back_kernel, clips), [gmix, proj, probs], [((rows, 3 * D), bf16)],
            [((HALF, HALF), bf16), ((len(clips) * BANDS, 2, BAND, HALF), bf16)], 0.1, 12,
        )[0]

    gproj_a, gproj_b = attend_back(0, 1), attend_back(2, 3)
    if near:
        up_arrived, gproj_a, gproj_b = lax.optimization_barrier((swap(up_far, ALONG_X, ALONG_Y), gproj_a, gproj_b))
        up_sum = up_sum[: NEAR // 2] + wide(up_arrived)
        up_near, gproj_a, gproj_b = lax.optimization_barrier((up_sum[PIECE:].astype(bf16), gproj_a, gproj_b))
    at_kept, *at_sent = call(
        project_kernel, [own_near, gproj_a, gproj_b, gout, scaled, wqkv, vec, sums, colsum],
        [((NEAR * G_ROWS + V_ROWS, D), bf16)] + [((AT_ROWS // PARTS, D), bf16)] * PARTS,
        [((3 * D, D), bf16), ((128, D), f32)],
        0.1, 16,
    )
    if near:
        up_arrived, at_sent[-1] = lax.optimization_barrier((swap(up_near, ALONG_Y, ALONG_X), at_sent[-1]))
        at_arrived = [swap(piece, CORES) for piece in at_sent]
        up_arrived, dn_arrived, at_arrived, gproj_a = lax.optimization_barrier(
            (up_arrived, swap(dn_far, ALONG_Z[1], ALONG_Z[0]), at_arrived, gproj_a)
        )
    (gtok,) = call(
        token_kernel, [gproj_a, gproj_b, x, gres, wqkv, vec], [((OWN_ALL, D), f32)], [], 0.1, 12,
    )
    if near:
        at_sum, *at_rest = call(
            functools.partial(share_kernel, end_to_end=True), [at_kept, *at_arrived],
            [((PIECE * G_ROWS + V_ROWS, D), t) for t in (f32, bf16, bf16, bf16)], [], 0.1, 8,
        )
        dn_sum = dn_sum[: NEAR // 2] + wide(dn_arrived)
        up_sum = up_sum[:PIECE] + wide(up_arrived)
        at_arrived = [swap(piece, mask) for piece, mask in zip(at_rest, ALONG_XY)]
        ff_arrived = jnp.concatenate([dn_sum[PIECE:], up_sum[2:]], axis=0).astype(bf16)
        ff_arrived = swap(ff_arrived, ALONG_Z[0], ALONG_Z[1])
        ff_arrived, gtok = lax.optimization_barrier((ff_arrived, gtok))
        dn_sum, up_sum = dn_sum[:PIECE] + wide(ff_arrived[:PIECE]), up_sum[:2] + wide(ff_arrived[PIECE:])
        up_arrived = swap(up_sum[1:].astype(bf16), ALONG_Z[1], ALONG_Z[0])
        dn_rest = dn_sum.astype(bf16)
        dn_arrived = [
            swap(dn_rest[1:2], ALONG_Y, ALONG_X), swap(dn_rest[2:3], ALONG_X, ALONG_Y), swap(dn_rest[3:], ALONG_XY[2]),
        ]
        at_arrived, up_arrived = lax.optimization_barrier((at_arrived, up_arrived))
        at_sum, *at_rest = call(
            share_kernel, [at_sum, *at_arrived],
            [((G_ROWS + V_ROWS, D), t) for t in (f32, bf16, bf16, bf16)], [], 0.1, 8,
        )
        up_sum = up_sum[0] + wide(up_arrived)[0]
        dn_sum = add_all(dn_sum[:1], dn_arrived)[0]
        at_arrived = [swap(piece, mask) for piece, mask in zip(at_rest, ALONG_Z)]
        g_qkv, g_out, g_vec = call(
            total_kernel, [device.astype(jnp.int32)[None], at_sum, *at_arrived],
            [((QKV_ROWS, D), f32), ((OUT_ROWS, D), f32), (vectors.shape, f32)], [], 0.1, 4,
        )
    if near:
        g_up, g_down = up_sum, dn_sum.T
        g_qkv, g_out = g_qkv.T, g_out.T
    else:
        at_grads = jnp.concatenate([at_kept[: NEAR * G_ROWS], *at_sent], axis=0)
        at_grads = at_grads[: SLOTS * G_ROWS].reshape(SLOTS, G_ROWS, D)

        def whole(array):
            blocks = array.reshape(SLOTS // CHUNKS, CHUNKS, UP_ROWS, D).transpose(0, 2, 1, 3)
            return blocks.reshape(D, FF)

        g_up = lax.psum_scatter(whole(jnp.concatenate([up_kept, up_sent], axis=0)), "dp", scatter_dimension=0, tiled=True)
        g_up = lax.psum_scatter(g_up, "tensor", scatter_dimension=1, tiled=True).astype(f32)
        g_down = lax.psum_scatter(whole(jnp.concatenate([dn_kept, dn_sent], axis=0)).T, "dp", scatter_dimension=1, tiled=True)
        g_down = lax.psum_scatter(g_down, "tensor", scatter_dimension=0, tiled=True).astype(f32)

        def owned(array):
            return lax.psum_scatter(array.astype(f32), BOTH, scatter_dimension=1, tiled=True)

        g_qkv = owned(at_grads[:, :QKV_ROWS].reshape(-1, D).T)
        g_out = owned(at_grads[:, QKV_ROWS:].reshape(-1, D).T)
        g_vec = owned(at_kept[NEAR * G_ROWS :][: vectors.shape[0]])
    shape = tokens.shape
    return (out.reshape(shape), gtok.reshape(shape), g_qkv, g_out, g_vec, g_up, g_down)


def solution(mesh):
    placed = (
        P("dp", "tensor", None),
        P("dp"),
        P(None, BOTH),
        P(None, BOTH),
        P(None, BOTH),
        P("dp", "tensor"),
        P("tensor", "dp"),
        P("dp", "tensor", None),
    )
    return jax.shard_map(
        shards,
        mesh=mesh,
        in_specs=placed,
        out_specs=(
            P("dp", "tensor", None),
            P("dp", "tensor", None),
            P(None, BOTH),
            P(None, BOTH),
            P(None, BOTH),
            P("dp", "tensor"),
            P("tensor", "dp"),
        ),
        check_vma=False,
    )
```

```python
import functools

import jax
import jax.numpy as jnp
from jax import lax
from jax.experimental import pallas as pl
from jax.experimental.pallas import tpu as pltpu
from jax.sharding import PartitionSpec as P

D = 512
FF = 2048
HEADS = 16
HEAD = D // HEADS
FREQ = 8
WINDOW = 4
SHIFT = 2
ROW_UNIT = 8

EPS = 1e-06
MASKED = -1000000000.0
SCALE = HEAD ** (-0.5)
INV_ROOT_TWO = 0.7071067811865476
INV_ROOT_TAU = 0.3989422804014327
HALF_LOG2_E = -0.7213475204444817

BOTH = ("dp", "tensor")
SLOTS = 32
NEAR = SLOTS // 2
PIECE = 4
QKV_ROWS = 3 * D // SLOTS
OUT_ROWS = D // SLOTS
A_ROWS = QKV_ROWS + OUT_ROWS
CHUNKS = FF // D
UP_ROWS = D * CHUNKS // SLOTS
B_ROWS = OUT_ROWS + UP_ROWS
G_ROWS = QKV_ROWS + OUT_ROWS
V_ROWS = 16
AT_ROWS = SLOTS // 2 * G_ROWS + V_ROWS
PARTS = 5

CLIPS = 4
OWN = 128
EDGE = 16
OWN_ALL = CLIPS * OWN
ROWS = OWN_ALL + CLIPS * 2 * EDGE
BAND = 2 * EDGE
BANDS = OWN // BAND + 1
HALF = D // 2
HALF_HEADS = HALF // HEAD
STEP = 128
SUB = 32

bf16 = jnp.bfloat16
f32 = jnp.float32


def nn(a, b):
    return lax.dot_general(a, b, (((1,), (0,)), ((), ())), preferred_element_type=f32)


def nt(a, b):
    return lax.dot_general(a, b, (((1,), (1,)), ((), ())), preferred_element_type=f32)


def tn(a, b):
    return lax.dot_general(a, b, (((0,), (0,)), ((), ())), preferred_element_type=f32)


def rows_at(start, size):
    return pl.ds(pl.multiple_of(start, size), size)


def norm_parts(values):
    mean = jnp.mean(values, axis=-1, keepdims=True)
    centred = values - mean
    variance = jnp.mean(centred * centred, axis=-1, keepdims=True)
    inverse = lax.rsqrt(variance + EPS)
    return centred * inverse, inverse


def norm_back(grad, scaled, inverse, gain):
    grad_hat = grad * gain
    centre = jnp.mean(grad_hat, axis=-1, keepdims=True)
    slope = jnp.mean(grad_hat * scaled, axis=-1, keepdims=True)
    return inverse * (grad_hat - centre - scaled * slope)


def band_places(band):
    clip, place = divmod(band, BANDS)
    first = OWN_ALL + clip * BAND if place == 0 else clip * OWN + place * BAND - EDGE
    last = OWN_ALL + clip * BAND + EDGE if place == BANDS - 1 else clip * OWN + place * BAND
    return slice(first, first + EDGE), slice(last, last + EDGE)


def load_band(ref, places, columns):
    return jnp.concatenate([ref[places[0], columns], ref[places[1], columns]], axis=0)


def find(pieces, slot):
    size = pieces[0].shape[0]
    return pieces[slot // size], slot % size


def weight_block(owner):
    return rows_at(owner // CHUNKS * UP_ROWS, UP_ROWS), rows_at(owner % CHUNKS * D, D)


def pack_kernel(qkv_ref, vec_ref, out_ref, up_ref, block_ref, rows_ref, sems):
    here = (
        rows_ref, block_ref.at[:QKV_ROWS], block_ref.at[A_ROWS : A_ROWS + OUT_ROWS], block_ref.at[A_ROWS + OUT_ROWS :],
    )
    copies = [
        pltpu.make_async_copy(there, place, sems.at[i])
        for i, (there, place) in enumerate(zip((vec_ref, qkv_ref, out_ref, up_ref), here))
    ]
    for copy in copies:
        copy.start()
    block_ref[QKV_ROWS:A_ROWS, :] = jnp.zeros((OUT_ROWS, D), bf16)
    row = lax.broadcasted_iota(jnp.int32, (OUT_ROWS, OUT_ROWS), 0)
    lane = lax.broadcasted_iota(jnp.int32, (OUT_ROWS, OUT_ROWS), 1)
    copies[0].wait()
    turned = nt(jnp.where(row == lane, 1.0, 0.0).astype(bf16), rows_ref[...])
    block_ref[QKV_ROWS:A_ROWS, : vec_ref.shape[0]] = turned.astype(bf16)
    for copy in copies[1:]:
        copy.wait()


def head_lanes():
    row = lax.broadcasted_iota(jnp.int32, (HALF, HALF), 0) // HEAD
    lane = lax.broadcasted_iota(jnp.int32, (HALF, HALF), 1) // HEAD
    return jnp.where(row == lane, 1.0, 0.0)


def by_head(rows, lanes):
    return jnp.concatenate([rows] * HALF_HEADS, axis=0) * lanes


def flip_heads(wide):
    turned = wide.T
    return jnp.concatenate([turned[head * BAND : (head + 1) * BAND] for head in range(HALF_HEADS)], axis=1)


def attend_kernel(
    own_ref, keep_ref, x_ref, *refs,
):
    a_refs, refs = refs[:-10], refs[-10:]
    proj_ref, prob_ref, mixed_ref, scaled_ref, wqkv_ref, vec_ref, column_vec, lanes_ref, pair_ref, normed_ref = refs
    for slot in range(SLOTS):
        owner = own_ref[slot]
        a_ref, held = find(a_refs, slot)
        wqkv_ref[rows_at(owner * QKV_ROWS, QKV_ROWS), :] = a_ref[held, :QKV_ROWS, :]
        column_vec[rows_at(owner * OUT_ROWS, OUT_ROWS), :] = a_ref[held, QKV_ROWS:A_ROWS, :128].astype(f32)
    vec_ref[...] = column_vec[...].T[:16, :]
    lanes_ref[...] = head_lanes().astype(bf16)
    key_group = (lax.broadcasted_iota(jnp.int32, (BAND, HALF), 0) % FREQ + SHIFT) // WINDOW
    query_group = (lax.broadcasted_iota(jnp.int32, (BAND, HALF), 1) % FREQ + SHIFT) // WINDOW
    pair_ref[...] = jnp.where(key_group == query_group, 1.0, 0.0)

    for step in range(ROWS // SUB):
        here = slice(step * SUB, (step + 1) * SUB)
        scaled, _ = norm_parts(x_ref[here, :].astype(f32))
        scaled_ref[here, :] = scaled.astype(bf16)
        normed_ref[here, :] = (scaled * vec_ref[0:1, :] + vec_ref[1:2, :]).astype(bf16)
    for part in range(3):
        columns = slice(part * D, (part + 1) * D)
        part_out = nt(normed_ref[...], wqkv_ref[columns, :])
        if part != 1:
            bias = 2 if part == 0 else 3
            part_out = part_out + vec_ref[bias : bias + 1, :]
        proj_ref[:, columns] = part_out.astype(bf16)

    for band in range(CLIPS * BANDS):
        places = band_places(band)
        key_ok = load_band(keep_ref, places, slice(None))
        key_ok = jnp.concatenate([key_ok, key_ok], axis=1) * pair_ref[...] > 0.5
        for half in range(2):
            low = half * HALF
            query = load_band(proj_ref, places, slice(low, low + HALF))
            key = load_band(proj_ref, places, slice(D + low, D + low + HALF))
            scores = nt(key, by_head(query, lanes_ref[...])) * SCALE
            scores = jnp.where(key_ok, scores, MASKED)
            exponent = jnp.exp(scores - jnp.max(scores, axis=0, keepdims=True))
            prob_ref[band, half] = exponent / jnp.sum(exponent, axis=0, keepdims=True)
    for band in range(CLIPS * BANDS):
        places = band_places(band)
        for half in range(2):
            low = half * HALF
            value = load_band(proj_ref, places, slice(2 * D + low, 2 * D + low + HALF))
            probs = flip_heads(prob_ref[band, half].astype(bf16))
            mixed = nn(probs, by_head(value, lanes_ref[...])).astype(bf16)
            mixed_ref[places[0], low : low + HALF] = mixed[:EDGE]
            mixed_ref[places[1], low : low + HALF] = mixed[EDGE:]


def together(*works):
    for _ in range(4):
        for work in works:
            next(work)


def write_grads(own_ref, pieces, block_ref):
    for slot in range(SLOTS):
        grads_ref, held = find(pieces, slot)
        owner = own_ref[slot]
        grads_ref[held] = block_ref[owner % CHUNKS, rows_at(owner // CHUNKS * UP_ROWS, UP_ROWS), :]


def up_kernel(
    own_ref, own_down_ref, keep_ref, cot_ref, x_ref, mixed_ref, vec_ref, *refs,
):
    b_refs, refs = refs[:-14], refs[-14:]
    (
        kept_ref, sent_ref, resid_ref, hid_ref, slope_ref, second_ref, branch_low, up_ref, wout_ref,
        gdown_ref, pre_ref, branch_t, attended_ref, normed_ref,
    ) = refs
    for slot in range(SLOTS):
        owner = own_ref[slot]
        b_ref, held = find(b_refs, slot)
        low = b_ref.shape[1] - B_ROWS
        wout_ref[rows_at(owner * OUT_ROWS, OUT_ROWS), :] = b_ref[held, low : low + OUT_ROWS, :]
        up_ref[weight_block(owner)] = b_ref[held, low + OUT_ROWS :, :]

    attended_ref[...] = nt(mixed_ref[...], wout_ref[...])

    for step in range(ROWS // SUB):
        here = slice(step * SUB, (step + 1) * SUB)
        residual = x_ref[here, :].astype(f32) + (attended_ref[here, :] + vec_ref[4:5, :])
        resid_ref[here, :] = residual
        scaled, _ = norm_parts(residual)
        second = (scaled * vec_ref[5:6, :] + vec_ref[6:7, :]).astype(bf16)
        second_ref[here, :] = second
        normed_ref[here, :] = second
        wide = jnp.concatenate([keep_ref[here, :]] * (D // 128), axis=1)
        branch_low[here, :] = (cot_ref[here, :].astype(f32) * wide).astype(bf16)
    branch_t[...] = branch_low[:OWN_ALL, :].T

    def products(chunk):
        for half in range(2):
            columns = slice(chunk * D + half * HALF, chunk * D + (half + 1) * HALF)
            ring = slice(chunk % 2 * D + half * HALF, chunk % 2 * D + (half + 1) * HALF)
            pre_ref[:, ring] = nn(normed_ref[...], up_ref[:, columns])
            yield
            yield

    def slopes(chunk):
        columns = slice(chunk * D, (chunk + 1) * D)
        ring = slice(chunk % 2 * D, chunk % 2 * D + D)
        for step in range(ROWS // 16):
            here = slice(step * 16, step * 16 + 16)
            pre = pre_ref[here, ring] + vec_ref[8 + chunk : 9 + chunk, :]
            phi = 0.5 + 0.5 * lax.erf(pre * INV_ROOT_TWO)
            slope_ref[here, columns] = (phi + pre * (jnp.exp2((pre * HALF_LOG2_E) * pre) * INV_ROOT_TAU)).astype(bf16)
            hid_ref[here, columns] = (pre * phi).astype(bf16)
            if step % 10 == 9:
                yield

    def weights(chunk):
        for half in range(2):
            columns = slice(chunk * D + half * HALF, chunk * D + (half + 1) * HALF)
            gdown = nn(branch_t[...], hid_ref[:OWN_ALL, columns])
            gdown_ref[chunk, :, half * HALF : (half + 1) * HALF] = gdown.astype(bf16)
            yield
            yield

    together(products(0))
    together(products(1), slopes(0))
    for chunk in range(2, CHUNKS):
        together(products(chunk), slopes(chunk - 1), weights(chunk - 2))
    together(slopes(CHUNKS - 1), weights(CHUNKS - 2))
    together(weights(CHUNKS - 1))
    write_grads(own_down_ref, (kept_ref, sent_ref), gdown_ref)


def down_kernel(
    own_ref, own_down_ref, slope_ref, second_ref, branch_low, *refs,
):
    c_refs, refs = refs[:-8], refs[-8:]
    (
        kept_ref, sent_ref, gpre_ref, down_ref, colsum_ref,
        gup_ref, ghid_ref, second_t,
    ) = refs
    for slot in range(SLOTS):
        c_ref, held = find(c_refs, slot)
        down_ref[weight_block(own_down_ref[slot])] = c_ref[held]
    second_t[:D, :] = second_ref[:OWN_ALL, :].T
    second_t[D:, :] = jnp.ones((16, OWN_ALL), bf16)

    def products(chunk):
        for half in range(2):
            columns = slice(chunk * D + half * HALF, chunk * D + (half + 1) * HALF)
            ring = slice(chunk % 2 * D + half * HALF, chunk % 2 * D + (half + 1) * HALF)
            ghid_ref[:, ring] = nn(branch_low[...], down_ref[:, columns])
            yield
            yield

    def slopes(chunk):
        columns = slice(chunk * D, (chunk + 1) * D)
        ring = slice(chunk % 2 * D, chunk % 2 * D + D)
        for step in range(ROWS // 16):
            here = slice(step * 16, step * 16 + 16)
            gpre_ref[here, columns] = (ghid_ref[here, ring] * slope_ref[here, columns].astype(f32)).astype(bf16)
            if step % 10 == 9:
                yield

    def weights(chunk):
        for half in range(2):
            columns = slice(chunk * D + half * HALF, chunk * D + (half + 1) * HALF)
            gup = nn(second_t[...], gpre_ref[:OWN_ALL, columns])
            gup_ref[chunk, :, half * HALF : (half + 1) * HALF] = gup[:D].astype(bf16)
            colsum_ref[chunk : chunk + 1, half * HALF : (half + 1) * HALF] = gup[D : D + 1]
            yield
            yield

    together(products(0))
    together(products(1), slopes(0))
    for chunk in range(2, CHUNKS):
        together(products(chunk), slopes(chunk - 1), weights(chunk - 2))
    together(slopes(CHUNKS - 1), weights(CHUNKS - 2))
    together(weights(CHUNKS - 1))
    write_grads(own_ref, (kept_ref, sent_ref), gup_ref)


def sum_kernel(hid_ref, gpre_ref, up_ref, down_ref, branch_ref, gsec_ref):
    branch_ref[...] = nt(hid_ref[:OWN_ALL, :], down_ref[...])
    gsec_ref[...] = nt(gpre_ref[...], up_ref[...])


def finish_kernel(
    keep_ref, cot_ref, mixed_ref, resid_ref, branch_ref, gsec_ref, wout_ref, vec_ref,
    out_ref, gres_ref, gout_ref, gmix_ref, sums_ref,
    gatt_ref,
):
    totals = [jnp.zeros((8, D), f32)] * 4
    for step in range(ROWS // SUB):
        here = slice(step * SUB, (step + 1) * SUB)
        wide = jnp.concatenate([keep_ref[here, :]] * (D // 128), axis=1)
        scaled, inverse = norm_parts(resid_ref[here, :])
        grad_out = cot_ref[here, :].astype(f32) * wide
        gsec = gsec_ref[here, :]
        gres = grad_out + norm_back(gsec, scaled, inverse, vec_ref[5:6, :])
        gres_ref[here, :] = gres
        gatt = gres.astype(bf16)
        gatt_ref[here, :] = gatt
        if step < OWN_ALL // SUB:
            parts = (gatt.astype(f32), gsec * scaled, gsec, grad_out.astype(bf16).astype(f32))
            totals = [t + p.reshape(SUB // 8, 8, D).sum(axis=0) for t, p in zip(totals, parts)]
            branch = branch_ref[here, :] + vec_ref[7:8, :]
            out_ref[here, :] = (wide * (resid_ref[here, :] + branch)).astype(bf16)
    for place, total in enumerate(totals):
        sums_ref[place : place + 1, :] = jnp.sum(total, axis=0, keepdims=True)
    gmix_ref[...] = nn(gatt_ref[...], wout_ref[...]).astype(bf16)
    gout_ref[...] = nn(gatt_ref[:OWN_ALL, :].T, mixed_ref[:OWN_ALL, :]).astype(bf16)


def back_kernel(clips, gmix_ref, proj_ref, prob_ref, gproj_ref, lanes_ref, gscore_ref):
    lanes_ref[...] = head_lanes().astype(bf16)
    bands = range(clips[0] * BANDS, (clips[-1] + 1) * BANDS)
    for band in bands:
        places = band_places(band)
        for half in range(2):
            low = half * HALF
            value = load_band(proj_ref, places, slice(2 * D + low, 2 * D + low + HALF))
            grad = load_band(gmix_ref, places, slice(low, low + HALF))
            probs = prob_ref[band, half]
            grad_probs = nt(value, by_head(grad, lanes_ref[...]))
            row_dot = jnp.sum(probs * grad_probs, axis=0, keepdims=True)
            gscore_ref[band - bands[0], half] = (probs * (grad_probs - row_dot)).astype(bf16)
    for band in bands:
        places = band_places(band)
        for half in range(2):
            low = half * HALF
            query = load_band(proj_ref, places, slice(low, low + HALF))
            key = load_band(proj_ref, places, slice(D + low, D + low + HALF))
            grad = load_band(gmix_ref, places, slice(low, low + HALF))
            grad_scores = gscore_ref[band - bands[0], half]
            grad_key = nn(grad_scores, by_head(query, lanes_ref[...])) * SCALE
            grad_value = nn(prob_ref[band, half].astype(bf16), by_head(grad, lanes_ref[...]))
            grad_query = nn(flip_heads(grad_scores), by_head(key, lanes_ref[...])) * SCALE
            for part, values in enumerate((grad_query, grad_key, grad_value)):
                values = values.astype(bf16)
                for rows, place in ((values[:EDGE], places[0]), (values[EDGE:], places[1])):
                    if place.start < OWN_ALL:
                        start = place.start - clips[0] * OWN
                        gproj_ref[start : start + EDGE, part * D + low : part * D + low + HALF] = rows


def project_kernel(
    own_ref, gproj_a, gproj_b, gout_ref, scaled_ref, wqkv_ref, vec_ref, sums_ref, colsum_ref,
    kept_ref, *refs,
):
    *sent_refs, gqkv_ref, gvec_ref = refs
    totals = jnp.zeros((8, 3 * D), f32)
    for step in range(OWN_ALL // 2 // SUB):
        here = slice(step * SUB, (step + 1) * SUB)
        for gproj_ref in (gproj_a, gproj_b):
            totals = totals + gproj_ref[here, :].astype(f32).reshape(SUB // 8, 8, 3 * D).sum(axis=0)
    totals = jnp.sum(totals, axis=0, keepdims=True)
    gvec_ref[...] = jnp.zeros_like(gvec_ref)
    gain_grad = jnp.zeros((8, D), f32)
    shift_grad = jnp.zeros((1, D), f32)
    for part in range(3):
        columns = slice(part * D, (part + 1) * D)
        gproj_t = jnp.concatenate([gproj_a[:, columns].T, gproj_b[:, columns].T], axis=1)
        product = nn(gproj_t, scaled_ref[:OWN_ALL, :])
        total = totals[:, part * D : (part + 1) * D]
        weight = wqkv_ref[part * D : (part + 1) * D, :]
        both = product * weight.astype(f32)
        gain_grad = gain_grad + both.reshape(D // 8, 8, D).sum(axis=0)
        high = total.astype(bf16)
        rest = (total - high.astype(f32)).astype(bf16)
        shift_grad = shift_grad + nn(high, weight) + nn(rest, weight)
        column = jnp.broadcast_to(total, (8, D)).T[:, 0:1]
        gqkv = product * vec_ref[0:1, :] + column * vec_ref[1:2, :]
        gqkv_ref[part * D : (part + 1) * D, :] = gqkv.astype(bf16)
    gvec_ref[0:1, :] = jnp.sum(gain_grad, axis=0, keepdims=True)
    gvec_ref[1:2, :] = shift_grad
    gvec_ref[2:3, :] = totals[:, :D]
    gvec_ref[3:4, :] = totals[:, 2 * D :]
    gvec_ref[4:8, :] = sums_ref[0:4, :]
    gvec_ref[8:12, :] = colsum_ref[0:4, :]
    for slot in range(SLOTS):
        owner = own_ref[slot]
        held = slot % NEAR * G_ROWS
        for low in range(0, G_ROWS, 16):
            if low < QKV_ROWS:
                rows = gqkv_ref[rows_at(owner * QKV_ROWS + low, 16), :]
            else:
                rows = gout_ref[rows_at(owner * OUT_ROWS + low - QKV_ROWS, 16), :]
            grads_ref, place = find_row([kept_ref] if slot < NEAR else sent_refs, held + low)
            grads_ref[place : place + 16, :] = rows
    for refs in ([kept_ref], sent_refs):
        grads_ref, place = find_row(refs, NEAR * G_ROWS)
        grads_ref[place : place + V_ROWS, :] = gvec_ref[:V_ROWS, :].astype(bf16)


def find_row(pieces, row):
    for piece in pieces:
        if row < piece.shape[0]:
            return piece, row
        row -= piece.shape[0]


def share_kernel(first_ref, *refs, end_to_end=False):
    pieces, outs = refs[:-4], refs[-4:]
    size = outs[0].shape[0] - V_ROWS

    def total(start):
        result = first_ref[start : start + 16, :].astype(f32)
        for found, row in [find_row(pieces, start)] if end_to_end else [(piece, start) for piece in pieces]:
            result = result + found[row : row + 16, :].astype(f32)
        return result

    vectors = total(4 * size)
    for part, out_ref in enumerate(outs):
        for low in range(0, size, 16):
            out_ref[low : low + 16, :] = total(part * size + low).astype(out_ref.dtype)
        out_ref[size:, :] = vectors.astype(out_ref.dtype)


def token_kernel(gproj_a, gproj_b, x_ref, gres_ref, wqkv_ref, vec_ref, gtok_ref):
    for step in range(OWN_ALL // STEP):
        here = slice(step * STEP, (step + 1) * STEP)
        gproj_ref, steps = (gproj_a, gproj_b)[step * STEP * 2 // OWN_ALL], OWN_ALL // 2 // STEP
        rows = slice(step % steps * STEP, (step % steps + 1) * STEP)
        gnormed = nn(gproj_ref[rows, :], wqkv_ref[...])
        scaled, inverse = norm_parts(x_ref[here, :].astype(f32))
        gtok_ref[here, :] = gres_ref[here, :] + norm_back(gnormed, scaled, inverse, vec_ref[0:1, :])


def total_kernel(device_ref, *refs):
    *pieces, gqkv_ref, gout_ref, gvec_ref = refs
    total = pieces[0][...]
    for piece in pieces[1:]:
        total = total + piece[...].astype(f32)
    gqkv_ref[...] = total[:QKV_ROWS]
    gout_ref[...] = total[QKV_ROWS:G_ROWS]
    own = pltpu.roll(total[G_ROWS:], lax.rem(D - device_ref[0] * OUT_ROWS, D), 1)
    gvec_ref[...] = own[: gvec_ref.shape[0], : gvec_ref.shape[1]]


def call(kernel, args, outs, scratch, micros, mib):
    smem, vmem = pl.BlockSpec(memory_space=pltpu.SMEM), pl.BlockSpec(memory_space=pltpu.VMEM)
    return pl.pallas_call(
        kernel,
        out_shape=[jax.ShapeDtypeStruct(s, t) for s, t in outs],
        in_specs=[smem if a.dtype == jnp.int32 else vmem for a in args],
        out_specs=[vmem] * len(outs),
        scratch_shapes=[pltpu.VMEM(s, t) for s, t in scratch],
        compiler_params=pltpu.CompilerParams(vmem_limit_bytes=mib * 1024 * 1024),
        cost_estimate=pl.CostEstimate(flops=int(micros * 1.1e9), bytes_accessed=2**20, transcendentals=0),
    )(*args)


def swap(array, mask, other=None):
    count = lax.axis_size("dp") * lax.axis_size("tensor")
    masks = (mask, mask if other is None else other)
    return lax.ppermute(array, BOTH, [(device, device ^ masks[device % 2]) for device in range(count)])


ALONG_Z, ALONG_Y, ALONG_X, CORES = (16, 8, 24), 2, 4, 1
ALONG_XY = (ALONG_Y, ALONG_X, ALONG_Y ^ ALONG_X)


AT_XY = (ALONG_XY[2], ALONG_Y, ALONG_X)


def owners(device, swapped, line_first=True, turn=None, second_first=True):
    def one(second_core):
        first = ALONG_X if swapped and bool(second_core) == second_first else ALONG_Y
        plane = [0, first, first ^ ALONG_XY[2], ALONG_XY[2]]
        if not swapped:
            plane = [0, *AT_XY]
        line = [0, *ALONG_Z]
        if turn is not None and second_core != turn:
            line = [line[0], line[2], line[1], line[3]]
        return [m ^ o for o in plane for m in line] if line_first else [m ^ o for o in line for m in plane]

    core = device % 2
    first = jnp.where(core == 0, jnp.array(one(0)), jnp.array(one(1)))
    second = jnp.where(core == 0, jnp.array(one(1)), jnp.array(one(0))) ^ CORES
    return (device ^ jnp.concatenate([first, second])).astype(jnp.int32)


def gather(held, phase):
    return [held] + [swap(held, mask) for mask in phase]


def both_cores(pieces):
    return pieces + [swap(piece, CORES) for piece in pieces]


def wide(array):
    return array.astype(f32)


def add_all(total, others):
    for other in others:
        total = total + wide(other)
    return total


def after(array, *others):
    return lax.optimization_barrier((array,) + others)[0]


def neighbours(array, axis_name, width):
    count = lax.axis_size(axis_name)
    up = [(i, i + 1) for i in range(count - 1)]
    low = lax.ppermute(array[..., -width:, :], axis_name, up)
    high = lax.ppermute(array[..., :width, :], axis_name, [(b, a) for a, b in up])
    return low, high


def shards(tokens, valid, w_qkv, w_out, vectors, w_up, w_down, cotangent):
    devices_dp, devices_t = lax.axis_size("dp"), lax.axis_size("tensor")
    near = devices_dp == 8 and devices_t == 4
    rank = lax.axis_index("tensor")

    own_time = jnp.broadcast_to((jnp.arange(OWN) // FREQ)[None], (CLIPS, OWN)).reshape(-1)
    edge_time = jnp.arange(BAND) // FREQ + jnp.where(jnp.arange(BAND) < EDGE, -SHIFT, OWN // FREQ - SHIFT)
    edge_time = jnp.broadcast_to(edge_time[None], (CLIPS, BAND)).reshape(-1)
    time = jnp.concatenate([own_time, edge_time]) + rank * (OWN // FREQ)
    limit = valid * ROW_UNIT
    limit = jnp.concatenate([jnp.repeat(limit, OWN), jnp.repeat(limit, BAND)])
    keep = jnp.where((time >= 0) & (time < limit), 1.0, 0.0).astype(f32)
    keep = jnp.broadcast_to(keep[:, None], (ROWS, 128))

    if near:
        device = lax.axis_index("dp") * devices_t + rank
        own_near, own_far = owners(device, False), owners(device, True, second_first=False)
        own_down, own_up = owners(device, True, False, 0), owners(device, True, True, 1)
        block = pl.pallas_call(
            pack_kernel,
            out_shape=jax.ShapeDtypeStruct((A_ROWS + B_ROWS, D), bf16),
            in_specs=[pl.BlockSpec(memory_space=pl.ANY)] * 4,
            out_specs=pl.BlockSpec(memory_space=pltpu.VMEM),
            scratch_shapes=[pltpu.VMEM(vectors.shape, bf16), pltpu.SemaphoreType.DMA((4,))],
            compiler_params=pltpu.CompilerParams(vmem_limit_bytes=60 * 1024 * 1024),
        )(w_qkv.T, vectors, w_out.T, w_up)
        edges = neighbours(jnp.stack([tokens, cotangent]), "tensor", EDGE)
        line = gather(block[None], ALONG_Z)
        down = w_down.T[None]
        down = jnp.concatenate([down, swap(down, ALONG_Y, ALONG_X)], axis=0)
        down = [down, swap(down, ALONG_X, ALONG_Y)]
        line, down, keep, own_near, own_far, own_down, own_up = lax.optimization_barrier(
            (line, down, keep, own_near, own_far, own_down, own_up)
        )
        line, down = jnp.concatenate(line, axis=0), jnp.concatenate(down, axis=0)
        near_pieces = swap(line, ALONG_X, ALONG_Y)
        down = [down, swap(down, ALONG_Z[0], ALONG_Z[1])]
        near_pieces, down, edges = lax.optimization_barrier((near_pieces, down, edges))
        down = jnp.concatenate(down, axis=0)
        near_pieces = jnp.concatenate([line, near_pieces], axis=0)
        a_far = swap(near_pieces[:, :A_ROWS], ALONG_Y, ALONG_X)
        b_far = swap(near_pieces[:, A_ROWS:], ALONG_Y, ALONG_X)
        pieces = both_cores([near_pieces])
        a_pieces = [pieces[0], a_far, pieces[1], swap(a_far, CORES)]
        c_pieces = [down, swap(down, ALONG_Z[1], ALONG_Z[0])]
    else:
        own_near = own_far = own_down = own_up = jnp.arange(SLOTS, dtype=jnp.int32)
        edges = neighbours(jnp.stack([tokens, cotangent]), "tensor", EDGE)
        qkv, out, vec = (lax.all_gather(a, BOTH, axis=1, tiled=True).T for a in (w_qkv, w_out, vectors))
        vec = jnp.pad(vec, ((0, 0), (0, D - vec.shape[1])))
        up = lax.all_gather(lax.all_gather(w_up, "dp", axis=0, tiled=True), "tensor", axis=1, tiled=True)
        down = lax.all_gather(lax.all_gather(w_down, "dp", axis=1, tiled=True), "tensor", axis=0, tiled=True).T
        up, down = (
            a.reshape(SLOTS // CHUNKS, UP_ROWS, CHUNKS, D).transpose(0, 2, 1, 3).reshape(SLOTS, UP_ROWS, D)
            for a in (up, down)
        )
        a_slots = jnp.concatenate([a.reshape(SLOTS, -1, D) for a in (qkv, vec)], axis=1)
        b_slots = jnp.concatenate([out.reshape(SLOTS, -1, D), up], axis=1)
        a_pieces, b_pieces, c_pieces = (
            [a[i : i + PIECE] for i in range(0, SLOTS, PIECE)] for a in (a_slots, b_slots, down)
        )

    edges = jnp.concatenate(edges, axis=2).reshape(2, CLIPS * BAND, D)
    x = jnp.concatenate([tokens.reshape(OWN_ALL, D), edges[0]], axis=0)
    cot = jnp.concatenate([cotangent.reshape(OWN_ALL, D), edges[1]], axis=0)
    proj, probs, mixed, scaled, wqkv, vec = call(
        attend_kernel, [own_far, keep, x, *a_pieces],
        [
            ((ROWS, 3 * D), bf16), ((CLIPS * BANDS, 2, BAND, HALF), f32), ((ROWS, D), bf16), ((ROWS, D), bf16),
            ((3 * D, D), bf16), ((16, D), f32),
        ],
        [((D, 128), f32), ((HALF, HALF), bf16), ((BAND, HALF), f32), ((ROWS, D), bf16)],
        0.1, 16,
    )
    if near:
        b_far, c_pieces, proj = lax.optimization_barrier((b_far, c_pieces, proj))
        b_pieces = [pieces[0], b_far, pieces[1], swap(b_far, CORES)]
        c_pieces = both_cores(c_pieces)
    dn_kept, dn_sent, resid, hid, slope, second, branch_low, up_all, wout = call(
        up_kernel, [own_far, own_down, keep, cot, x, mixed, vec, *b_pieces],
        [
            ((NEAR, UP_ROWS, D), bf16), ((NEAR, UP_ROWS, D), bf16), ((ROWS, D), f32), ((ROWS, FF), bf16),
            ((ROWS, FF), bf16), ((ROWS, D), bf16), ((ROWS, D), bf16), ((D, FF), bf16), ((D, D), bf16),
        ],
        [
            ((CHUNKS, D, D), bf16), ((ROWS, 2 * D), f32), ((D, OWN_ALL), bf16), ((ROWS, D), f32), ((ROWS, D), bf16),
        ],
        8, 25,
    )
    up_kept, up_sent, gpre, down_all, colsum = call(
        down_kernel, [own_up, own_down, slope, second, branch_low, *c_pieces],
        [
            ((NEAR, UP_ROWS, D), bf16), ((NEAR, UP_ROWS, D), bf16), ((ROWS, FF), bf16), ((D, FF), bf16), ((8, D), f32),
        ],
        [((CHUNKS, D, D), bf16), ((ROWS, 2 * D), f32), ((D + 16, OWN_ALL), bf16)],
        8, 20,
    )
    if near:
        dn_sum = wide(dn_kept) + wide(after(swap(dn_sent, CORES), gpre))
        gpre, dn_far = lax.optimization_barrier((gpre, dn_sum[NEAR // 2 :].astype(bf16)))
    branch, gsec = call(
        sum_kernel, [hid, gpre, up_all, down_all], [((OWN_ALL, D), f32), ((ROWS, D), f32)], [], 0.1, 13,
    )
    if near:
        up_sum = wide(up_kept) + wide(after(swap(up_sent, CORES), gsec))
        up_far = up_sum[NEAR // 2 :].astype(bf16)
        gsec, up_far, dn_far = lax.optimization_barrier((gsec, up_far, dn_far))
    out, gres, gout, gmix, sums = call(
        finish_kernel, [keep, cot, mixed, resid, branch, gsec, wout, vec],
        [
            ((OWN_ALL, D), bf16), ((ROWS, D), f32), ((D, D), bf16), ((ROWS, D), bf16), ((8, D), f32),
        ],
        [((ROWS, D), bf16)],
        0.1, 16,
    )
    def attend_back(*clips):
        rows = len(clips) * OWN
        return call(
            functools.partial(back_kernel, clips), [gmix, proj, probs], [((rows, 3 * D), bf16)],
            [((HALF, HALF), bf16), ((len(clips) * BANDS, 2, BAND, HALF), bf16)], 0.1, 12,
        )[0]

    gproj_a, gproj_b = attend_back(0, 1), attend_back(2, 3)
    if near:
        up_arrived, gproj_a, gproj_b = lax.optimization_barrier((swap(up_far, ALONG_X, ALONG_Y), gproj_a, gproj_b))
        up_sum = up_sum[: NEAR // 2] + wide(up_arrived)
        up_near, gproj_a, gproj_b = lax.optimization_barrier((up_sum[PIECE:].astype(bf16), gproj_a, gproj_b))
    at_kept, *at_sent = call(
        project_kernel, [own_near, gproj_a, gproj_b, gout, scaled, wqkv, vec, sums, colsum],
        [((NEAR * G_ROWS + V_ROWS, D), bf16)] + [((AT_ROWS // PARTS, D), bf16)] * PARTS,
        [((3 * D, D), bf16), ((128, D), f32)],
        0.1, 16,
    )
    if near:
        up_arrived, at_sent[-1] = lax.optimization_barrier((swap(up_near, ALONG_Y, ALONG_X), at_sent[-1]))
        at_arrived = [swap(piece, CORES) for piece in at_sent]
        up_arrived, dn_arrived, at_arrived, gproj_a = lax.optimization_barrier(
            (up_arrived, swap(dn_far, ALONG_Z[1], ALONG_Z[0]), at_arrived, gproj_a)
        )
    (gtok,) = call(
        token_kernel, [gproj_a, gproj_b, x, gres, wqkv, vec], [((OWN_ALL, D), f32)], [], 0.1, 12,
    )
    if near:
        at_sum, *at_rest = call(
            functools.partial(share_kernel, end_to_end=True), [at_kept, *at_arrived],
            [((PIECE * G_ROWS + V_ROWS, D), t) for t in (f32, bf16, bf16, bf16)], [], 0.1, 8,
        )
        dn_sum = dn_sum[: NEAR // 2] + wide(dn_arrived)
        up_sum = up_sum[:PIECE] + wide(up_arrived)
        at_arrived = [swap(piece, mask) for piece, mask in zip(at_rest, AT_XY)]
        ff_arrived = jnp.concatenate([dn_sum[PIECE:], up_sum[2:]], axis=0).astype(bf16)
        ff_arrived = swap(ff_arrived, ALONG_Z[0], ALONG_Z[1])
        ff_arrived, gtok = lax.optimization_barrier((ff_arrived, gtok))
        dn_sum, up_sum = dn_sum[:PIECE] + wide(ff_arrived[:PIECE]), up_sum[:2] + wide(ff_arrived[PIECE:])
        up_arrived = swap(up_sum[1:].astype(bf16), ALONG_Z[1], ALONG_Z[0])
        dn_rest = dn_sum.astype(bf16)
        dn_arrived = [
            swap(dn_rest[1:2], ALONG_Y, ALONG_X), swap(dn_rest[2:3], ALONG_X, ALONG_Y), swap(dn_rest[3:], ALONG_XY[2]),
        ]
        at_arrived, up_arrived = lax.optimization_barrier((at_arrived, up_arrived))
        at_sum, *at_rest = call(
            share_kernel, [at_sum, *at_arrived],
            [((G_ROWS + V_ROWS, D), t) for t in (f32, bf16, bf16, bf16)], [], 0.1, 8,
        )
        up_sum = up_sum[0] + wide(up_arrived)[0]
        dn_sum = add_all(dn_sum[:1], dn_arrived)[0]
        at_arrived = [swap(piece, mask) for piece, mask in zip(at_rest, ALONG_Z)]
        g_qkv, g_out, g_vec = call(
            total_kernel, [device.astype(jnp.int32)[None], at_sum, *at_arrived],
            [((QKV_ROWS, D), f32), ((OUT_ROWS, D), f32), (vectors.shape, f32)], [], 0.1, 4,
        )
    if near:
        g_up, g_down = up_sum, dn_sum.T
        g_qkv, g_out = g_qkv.T, g_out.T
    else:
        at_grads = jnp.concatenate([at_kept[: NEAR * G_ROWS], *at_sent], axis=0)
        at_grads = at_grads[: SLOTS * G_ROWS].reshape(SLOTS, G_ROWS, D)

        def whole(array):
            blocks = array.reshape(SLOTS // CHUNKS, CHUNKS, UP_ROWS, D).transpose(0, 2, 1, 3)
            return blocks.reshape(D, FF)

        g_up = lax.psum_scatter(whole(jnp.concatenate([up_kept, up_sent], axis=0)), "dp", scatter_dimension=0, tiled=True)
        g_up = lax.psum_scatter(g_up, "tensor", scatter_dimension=1, tiled=True).astype(f32)
        g_down = lax.psum_scatter(whole(jnp.concatenate([dn_kept, dn_sent], axis=0)).T, "dp", scatter_dimension=1, tiled=True)
        g_down = lax.psum_scatter(g_down, "tensor", scatter_dimension=0, tiled=True).astype(f32)

        def owned(array):
            return lax.psum_scatter(array.astype(f32), BOTH, scatter_dimension=1, tiled=True)

        g_qkv = owned(at_grads[:, :QKV_ROWS].reshape(-1, D).T)
        g_out = owned(at_grads[:, QKV_ROWS:].reshape(-1, D).T)
        g_vec = owned(at_kept[NEAR * G_ROWS :][: vectors.shape[0]])
    shape = tokens.shape
    return (out.reshape(shape), gtok.reshape(shape), g_qkv, g_out, g_vec, g_up, g_down)


def solution(mesh):
    placed = (
        P("dp", "tensor", None),
        P("dp"),
        P(None, BOTH),
        P(None, BOTH),
        P(None, BOTH),
        P("dp", "tensor"),
        P("tensor", "dp"),
        P("dp", "tensor", None),
    )
    return jax.shard_map(
        shards,
        mesh=mesh,
        in_specs=placed,
        out_specs=(
            P("dp", "tensor", None),
            P("dp", "tensor", None),
            P(None, BOTH),
            P(None, BOTH),
            P(None, BOTH),
            P("dp", "tensor"),
            P("tensor", "dp"),
        ),
        check_vma=False,
    )
```

```python
import functools

import jax
import jax.numpy as jnp
from jax import lax
from jax.experimental import pallas as pl
from jax.experimental.pallas import tpu as pltpu
from jax.sharding import PartitionSpec as P

D = 512
FF = 2048
HEADS = 16
HEAD = D // HEADS
FREQ = 8
WINDOW = 4
SHIFT = 2
ROW_UNIT = 8

EPS = 1e-06
MASKED = -1000000000.0
SCALE = HEAD ** (-0.5)
INV_ROOT_TWO = 0.7071067811865476
INV_ROOT_TAU = 0.3989422804014327
HALF_LOG2_E = -0.7213475204444817

BOTH = ("dp", "tensor")
SLOTS = 32
NEAR = SLOTS // 2
PIECE = 4
QKV_ROWS = 3 * D // SLOTS
OUT_ROWS = D // SLOTS
A_ROWS = QKV_ROWS + OUT_ROWS
CHUNKS = FF // D
UP_ROWS = D * CHUNKS // SLOTS
B_ROWS = OUT_ROWS + UP_ROWS
G_ROWS = QKV_ROWS + OUT_ROWS
V_ROWS = 16
AT_ROWS = SLOTS // 2 * G_ROWS + V_ROWS
PARTS = 5

CLIPS = 4
OWN = 128
EDGE = 16
OWN_ALL = CLIPS * OWN
ROWS = OWN_ALL + CLIPS * 2 * EDGE
BAND = 2 * EDGE
BANDS = OWN // BAND + 1
HALF = D // 2
HALF_HEADS = HALF // HEAD
STEP = 128
SUB = 32

bf16 = jnp.bfloat16
f32 = jnp.float32


def nn(a, b):
    return lax.dot_general(a, b, (((1,), (0,)), ((), ())), preferred_element_type=f32)


def nt(a, b):
    return lax.dot_general(a, b, (((1,), (1,)), ((), ())), preferred_element_type=f32)


def tn(a, b):
    return lax.dot_general(a, b, (((0,), (0,)), ((), ())), preferred_element_type=f32)


def rows_at(start, size):
    return pl.ds(pl.multiple_of(start, size), size)


def norm_parts(values):
    mean = jnp.mean(values, axis=-1, keepdims=True)
    centred = values - mean
    variance = jnp.mean(centred * centred, axis=-1, keepdims=True)
    inverse = lax.rsqrt(variance + EPS)
    return centred * inverse, inverse


def norm_back(grad, scaled, inverse, gain):
    grad_hat = grad * gain
    centre = jnp.mean(grad_hat, axis=-1, keepdims=True)
    slope = jnp.mean(grad_hat * scaled, axis=-1, keepdims=True)
    return inverse * (grad_hat - centre - scaled * slope)


def band_places(band):
    clip, place = divmod(band, BANDS)
    first = OWN_ALL + clip * BAND if place == 0 else clip * OWN + place * BAND - EDGE
    last = OWN_ALL + clip * BAND + EDGE if place == BANDS - 1 else clip * OWN + place * BAND
    return slice(first, first + EDGE), slice(last, last + EDGE)


def load_band(ref, places, columns):
    return jnp.concatenate([ref[places[0], columns], ref[places[1], columns]], axis=0)


def find(pieces, slot):
    size = pieces[0].shape[0]
    return pieces[slot // size], slot % size


def weight_block(owner):
    return rows_at(owner // CHUNKS * UP_ROWS, UP_ROWS), rows_at(owner % CHUNKS * D, D)


def pack_kernel(qkv_ref, vec_ref, out_ref, up_ref, block_ref, rows_ref, sems):
    here = (
        rows_ref, block_ref.at[:QKV_ROWS], block_ref.at[A_ROWS : A_ROWS + OUT_ROWS], block_ref.at[A_ROWS + OUT_ROWS :],
    )
    copies = [
        pltpu.make_async_copy(there, place, sems.at[i])
        for i, (there, place) in enumerate(zip((vec_ref, qkv_ref, out_ref, up_ref), here))
    ]
    for copy in copies:
        copy.start()
    block_ref[QKV_ROWS:A_ROWS, :] = jnp.zeros((OUT_ROWS, D), bf16)
    row = lax.broadcasted_iota(jnp.int32, (OUT_ROWS, OUT_ROWS), 0)
    lane = lax.broadcasted_iota(jnp.int32, (OUT_ROWS, OUT_ROWS), 1)
    copies[0].wait()
    turned = nt(jnp.where(row == lane, 1.0, 0.0).astype(bf16), rows_ref[...])
    block_ref[QKV_ROWS:A_ROWS, : vec_ref.shape[0]] = turned.astype(bf16)
    for copy in copies[1:]:
        copy.wait()


def head_lanes():
    row = lax.broadcasted_iota(jnp.int32, (HALF, HALF), 0) // HEAD
    lane = lax.broadcasted_iota(jnp.int32, (HALF, HALF), 1) // HEAD
    return jnp.where(row == lane, 1.0, 0.0)


def by_head(rows, lanes):
    return jnp.concatenate([rows] * HALF_HEADS, axis=0) * lanes


def flip_heads(wide):
    turned = wide.T
    return jnp.concatenate([turned[head * BAND : (head + 1) * BAND] for head in range(HALF_HEADS)], axis=1)


def attend_kernel(
    own_ref, keep_ref, x_ref, *refs,
):
    a_refs, refs = refs[:-10], refs[-10:]
    proj_ref, prob_ref, mixed_ref, scaled_ref, wqkv_ref, vec_ref, column_vec, lanes_ref, pair_ref, normed_ref = refs
    for slot in range(SLOTS):
        owner = own_ref[slot]
        a_ref, held = find(a_refs, slot)
        wqkv_ref[rows_at(owner * QKV_ROWS, QKV_ROWS), :] = a_ref[held, :QKV_ROWS, :]
        column_vec[rows_at(owner * OUT_ROWS, OUT_ROWS), :] = a_ref[held, QKV_ROWS:A_ROWS, :128].astype(f32)
    vec_ref[...] = column_vec[...].T[:16, :]
    lanes_ref[...] = head_lanes().astype(bf16)
    key_group = (lax.broadcasted_iota(jnp.int32, (BAND, HALF), 0) % FREQ + SHIFT) // WINDOW
    query_group = (lax.broadcasted_iota(jnp.int32, (BAND, HALF), 1) % FREQ + SHIFT) // WINDOW
    pair_ref[...] = jnp.where(key_group == query_group, 1.0, 0.0)

    for step in range(ROWS // SUB):
        here = slice(step * SUB, (step + 1) * SUB)
        scaled, _ = norm_parts(x_ref[here, :].astype(f32))
        scaled_ref[here, :] = scaled.astype(bf16)
        normed_ref[here, :] = (scaled * vec_ref[0:1, :] + vec_ref[1:2, :]).astype(bf16)
    for part in range(3):
        columns = slice(part * D, (part + 1) * D)
        part_out = nt(normed_ref[...], wqkv_ref[columns, :])
        if part != 1:
            bias = 2 if part == 0 else 3
            part_out = part_out + vec_ref[bias : bias + 1, :]
        proj_ref[:, columns] = part_out.astype(bf16)

    for band in range(CLIPS * BANDS):
        places = band_places(band)
        key_ok = load_band(keep_ref, places, slice(None))
        key_ok = jnp.concatenate([key_ok, key_ok], axis=1) * pair_ref[...] > 0.5
        for half in range(2):
            low = half * HALF
            query = load_band(proj_ref, places, slice(low, low + HALF))
            key = load_band(proj_ref, places, slice(D + low, D + low + HALF))
            scores = nt(key, by_head(query, lanes_ref[...])) * SCALE
            scores = jnp.where(key_ok, scores, MASKED)
            exponent = jnp.exp(scores - jnp.max(scores, axis=0, keepdims=True))
            prob_ref[band, half] = exponent / jnp.sum(exponent, axis=0, keepdims=True)
    for band in range(CLIPS * BANDS):
        places = band_places(band)
        for half in range(2):
            low = half * HALF
            value = load_band(proj_ref, places, slice(2 * D + low, 2 * D + low + HALF))
            probs = flip_heads(prob_ref[band, half].astype(bf16))
            mixed = nn(probs, by_head(value, lanes_ref[...])).astype(bf16)
            mixed_ref[places[0], low : low + HALF] = mixed[:EDGE]
            mixed_ref[places[1], low : low + HALF] = mixed[EDGE:]


def together(*works):
    for _ in range(4):
        for work in works:
            next(work)


def write_grads(own_ref, pieces, block_ref):
    for slot in range(SLOTS):
        grads_ref, held = find(pieces, slot)
        owner = own_ref[slot]
        grads_ref[held] = block_ref[owner % CHUNKS, rows_at(owner // CHUNKS * UP_ROWS, UP_ROWS), :]


def up_kernel(
    own_ref, own_down_ref, keep_ref, cot_ref, x_ref, mixed_ref, vec_ref, *refs,
):
    b_refs, refs = refs[:-14], refs[-14:]
    (
        kept_ref, sent_ref, resid_ref, hid_ref, slope_ref, second_ref, branch_low, up_ref, wout_ref,
        gdown_ref, pre_ref, branch_t, attended_ref, normed_ref,
    ) = refs
    for slot in range(SLOTS):
        owner = own_ref[slot]
        b_ref, held = find(b_refs, slot)
        low = b_ref.shape[1] - B_ROWS
        wout_ref[rows_at(owner * OUT_ROWS, OUT_ROWS), :] = b_ref[held, low : low + OUT_ROWS, :]
        up_ref[weight_block(owner)] = b_ref[held, low + OUT_ROWS :, :]

    attended_ref[...] = nt(mixed_ref[...], wout_ref[...])

    for step in range(ROWS // SUB):
        here = slice(step * SUB, (step + 1) * SUB)
        residual = x_ref[here, :].astype(f32) + (attended_ref[here, :] + vec_ref[4:5, :])
        resid_ref[here, :] = residual
        scaled, _ = norm_parts(residual)
        second = (scaled * vec_ref[5:6, :] + vec_ref[6:7, :]).astype(bf16)
        second_ref[here, :] = second
        normed_ref[here, :] = second
        wide = jnp.concatenate([keep_ref[here, :]] * (D // 128), axis=1)
        branch_low[here, :] = (cot_ref[here, :].astype(f32) * wide).astype(bf16)
    branch_t[...] = branch_low[:OWN_ALL, :].T

    def products(chunk):
        for half in range(2):
            columns = slice(chunk * D + half * HALF, chunk * D + (half + 1) * HALF)
            ring = slice(chunk % 2 * D + half * HALF, chunk % 2 * D + (half + 1) * HALF)
            pre_ref[:, ring] = nn(normed_ref[...], up_ref[:, columns])
            yield
            yield

    def slopes(chunk):
        columns = slice(chunk * D, (chunk + 1) * D)
        ring = slice(chunk % 2 * D, chunk % 2 * D + D)
        for step in range(ROWS // 16):
            here = slice(step * 16, step * 16 + 16)
            pre = pre_ref[here, ring] + vec_ref[8 + chunk : 9 + chunk, :]
            phi = 0.5 + 0.5 * lax.erf(pre * INV_ROOT_TWO)
            slope_ref[here, columns] = (phi + pre * (jnp.exp2((pre * HALF_LOG2_E) * pre) * INV_ROOT_TAU)).astype(bf16)
            hid_ref[here, columns] = (pre * phi).astype(bf16)
            if step % 10 == 9:
                yield

    def weights(chunk):
        for half in range(2):
            columns = slice(chunk * D + half * HALF, chunk * D + (half + 1) * HALF)
            gdown = nn(branch_t[...], hid_ref[:OWN_ALL, columns])
            gdown_ref[chunk, :, half * HALF : (half + 1) * HALF] = gdown.astype(bf16)
            yield
            yield

    together(products(0))
    together(products(1), slopes(0))
    for chunk in range(2, CHUNKS):
        together(products(chunk), slopes(chunk - 1), weights(chunk - 2))
    together(slopes(CHUNKS - 1), weights(CHUNKS - 2))
    together(weights(CHUNKS - 1))
    write_grads(own_down_ref, (kept_ref, sent_ref), gdown_ref)


def down_kernel(
    own_ref, own_down_ref, slope_ref, second_ref, branch_low, *refs,
):
    c_refs, refs = refs[:-8], refs[-8:]
    (
        kept_ref, sent_ref, gpre_ref, down_ref, colsum_ref,
        gup_ref, ghid_ref, second_t,
    ) = refs
    for slot in range(SLOTS):
        c_ref, held = find(c_refs, slot)
        down_ref[weight_block(own_down_ref[slot])] = c_ref[held]
    second_t[:D, :] = second_ref[:OWN_ALL, :].T
    second_t[D:, :] = jnp.ones((16, OWN_ALL), bf16)

    def products(chunk):
        for half in range(2):
            columns = slice(chunk * D + half * HALF, chunk * D + (half + 1) * HALF)
            ring = slice(chunk % 2 * D + half * HALF, chunk % 2 * D + (half + 1) * HALF)
            ghid_ref[:, ring] = nn(branch_low[...], down_ref[:, columns])
            yield
            yield

    def slopes(chunk):
        columns = slice(chunk * D, (chunk + 1) * D)
        ring = slice(chunk % 2 * D, chunk % 2 * D + D)
        for step in range(ROWS // 16):
            here = slice(step * 16, step * 16 + 16)
            gpre_ref[here, columns] = (ghid_ref[here, ring] * slope_ref[here, columns].astype(f32)).astype(bf16)
            if step % 10 == 9:
                yield

    def weights(chunk):
        for half in range(2):
            columns = slice(chunk * D + half * HALF, chunk * D + (half + 1) * HALF)
            gup = nn(second_t[...], gpre_ref[:OWN_ALL, columns])
            gup_ref[chunk, :, half * HALF : (half + 1) * HALF] = gup[:D].astype(bf16)
            colsum_ref[chunk : chunk + 1, half * HALF : (half + 1) * HALF] = gup[D : D + 1]
            yield
            yield

    together(products(0))
    together(products(1), slopes(0))
    for chunk in range(2, CHUNKS):
        together(products(chunk), slopes(chunk - 1), weights(chunk - 2))
    together(slopes(CHUNKS - 1), weights(CHUNKS - 2))
    together(weights(CHUNKS - 1))
    write_grads(own_ref, (kept_ref, sent_ref), gup_ref)


def sum_kernel(hid_ref, gpre_ref, up_ref, down_ref, branch_ref, gsec_ref):
    branch_ref[...] = nt(hid_ref[:OWN_ALL, :], down_ref[...])
    gsec_ref[...] = nt(gpre_ref[...], up_ref[...])


def finish_kernel(
    keep_ref, cot_ref, mixed_ref, resid_ref, branch_ref, gsec_ref, wout_ref, vec_ref,
    out_ref, gres_ref, gout_ref, gmix_ref, sums_ref,
    gatt_ref,
):
    totals = [jnp.zeros((8, D), f32)] * 4
    for step in range(ROWS // SUB):
        here = slice(step * SUB, (step + 1) * SUB)
        wide = jnp.concatenate([keep_ref[here, :]] * (D // 128), axis=1)
        scaled, inverse = norm_parts(resid_ref[here, :])
        grad_out = cot_ref[here, :].astype(f32) * wide
        gsec = gsec_ref[here, :]
        gres = grad_out + norm_back(gsec, scaled, inverse, vec_ref[5:6, :])
        gres_ref[here, :] = gres
        gatt = gres.astype(bf16)
        gatt_ref[here, :] = gatt
        if step < OWN_ALL // SUB:
            parts = (gatt.astype(f32), gsec * scaled, gsec, grad_out.astype(bf16).astype(f32))
            totals = [t + p.reshape(SUB // 8, 8, D).sum(axis=0) for t, p in zip(totals, parts)]
            branch = branch_ref[here, :] + vec_ref[7:8, :]
            out_ref[here, :] = (wide * (resid_ref[here, :] + branch)).astype(bf16)
    for place, total in enumerate(totals):
        sums_ref[place : place + 1, :] = jnp.sum(total, axis=0, keepdims=True)
    gmix_ref[...] = nn(gatt_ref[...], wout_ref[...]).astype(bf16)
    gout_ref[...] = nn(gatt_ref[:OWN_ALL, :].T, mixed_ref[:OWN_ALL, :]).astype(bf16)


def back_kernel(clips, gmix_ref, proj_ref, prob_ref, gproj_ref, lanes_ref, gscore_ref):
    lanes_ref[...] = head_lanes().astype(bf16)
    bands = range(clips[0] * BANDS, (clips[-1] + 1) * BANDS)
    for band in bands:
        places = band_places(band)
        for half in range(2):
            low = half * HALF
            value = load_band(proj_ref, places, slice(2 * D + low, 2 * D + low + HALF))
            grad = load_band(gmix_ref, places, slice(low, low + HALF))
            probs = prob_ref[band, half]
            grad_probs = nt(value, by_head(grad, lanes_ref[...]))
            row_dot = jnp.sum(probs * grad_probs, axis=0, keepdims=True)
            gscore_ref[band - bands[0], half] = (probs * (grad_probs - row_dot)).astype(bf16)
    for band in bands:
        places = band_places(band)
        for half in range(2):
            low = half * HALF
            query = load_band(proj_ref, places, slice(low, low + HALF))
            key = load_band(proj_ref, places, slice(D + low, D + low + HALF))
            grad = load_band(gmix_ref, places, slice(low, low + HALF))
            grad_scores = gscore_ref[band - bands[0], half]
            grad_key = nn(grad_scores, by_head(query, lanes_ref[...])) * SCALE
            grad_value = nn(prob_ref[band, half].astype(bf16), by_head(grad, lanes_ref[...]))
            grad_query = nn(flip_heads(grad_scores), by_head(key, lanes_ref[...])) * SCALE
            for part, values in enumerate((grad_query, grad_key, grad_value)):
                values = values.astype(bf16)
                for rows, place in ((values[:EDGE], places[0]), (values[EDGE:], places[1])):
                    if place.start < OWN_ALL:
                        start = place.start - clips[0] * OWN
                        gproj_ref[start : start + EDGE, part * D + low : part * D + low + HALF] = rows


def project_kernel(
    own_ref, gproj_a, gproj_b, gout_ref, scaled_ref, wqkv_ref, vec_ref, sums_ref, colsum_ref,
    kept_ref, *refs,
):
    *sent_refs, gqkv_ref, gvec_ref = refs
    totals = jnp.zeros((8, 3 * D), f32)
    for step in range(OWN_ALL // 2 // SUB):
        here = slice(step * SUB, (step + 1) * SUB)
        for gproj_ref in (gproj_a, gproj_b):
            totals = totals + gproj_ref[here, :].astype(f32).reshape(SUB // 8, 8, 3 * D).sum(axis=0)
    totals = jnp.sum(totals, axis=0, keepdims=True)
    gvec_ref[...] = jnp.zeros_like(gvec_ref)
    gain_grad = jnp.zeros((8, D), f32)
    shift_grad = jnp.zeros((1, D), f32)
    for part in range(3):
        columns = slice(part * D, (part + 1) * D)
        gproj_t = jnp.concatenate([gproj_a[:, columns].T, gproj_b[:, columns].T], axis=1)
        product = nn(gproj_t, scaled_ref[:OWN_ALL, :])
        total = totals[:, part * D : (part + 1) * D]
        weight = wqkv_ref[part * D : (part + 1) * D, :]
        both = product * weight.astype(f32)
        gain_grad = gain_grad + both.reshape(D // 8, 8, D).sum(axis=0)
        high = total.astype(bf16)
        rest = (total - high.astype(f32)).astype(bf16)
        shift_grad = shift_grad + nn(high, weight) + nn(rest, weight)
        column = jnp.broadcast_to(total, (8, D)).T[:, 0:1]
        gqkv = product * vec_ref[0:1, :] + column * vec_ref[1:2, :]
        gqkv_ref[part * D : (part + 1) * D, :] = gqkv.astype(bf16)
    gvec_ref[0:1, :] = jnp.sum(gain_grad, axis=0, keepdims=True)
    gvec_ref[1:2, :] = shift_grad
    gvec_ref[2:3, :] = totals[:, :D]
    gvec_ref[3:4, :] = totals[:, 2 * D :]
    gvec_ref[4:8, :] = sums_ref[0:4, :]
    gvec_ref[8:12, :] = colsum_ref[0:4, :]
    for slot in range(SLOTS):
        owner = own_ref[slot]
        held = slot % NEAR * G_ROWS
        for low in range(0, G_ROWS, 16):
            if low < QKV_ROWS:
                rows = gqkv_ref[rows_at(owner * QKV_ROWS + low, 16), :]
            else:
                rows = gout_ref[rows_at(owner * OUT_ROWS + low - QKV_ROWS, 16), :]
            grads_ref, place = find_row([kept_ref] if slot < NEAR else sent_refs, held + low)
            grads_ref[place : place + 16, :] = rows
    for refs in ([kept_ref], sent_refs):
        grads_ref, place = find_row(refs, NEAR * G_ROWS)
        grads_ref[place : place + V_ROWS, :] = gvec_ref[:V_ROWS, :].astype(bf16)


def find_row(pieces, row):
    for piece in pieces:
        if row < piece.shape[0]:
            return piece, row
        row -= piece.shape[0]


def share_kernel(first_ref, *refs, end_to_end=False):
    pieces, outs = refs[:-4], refs[-4:]
    size = outs[0].shape[0] - V_ROWS

    def total(start):
        result = first_ref[start : start + 16, :].astype(f32)
        for found, row in [find_row(pieces, start)] if end_to_end else [(piece, start) for piece in pieces]:
            result = result + found[row : row + 16, :].astype(f32)
        return result

    vectors = total(4 * size)
    for part, out_ref in enumerate(outs):
        for low in range(0, size, 16):
            out_ref[low : low + 16, :] = total(part * size + low).astype(out_ref.dtype)
        out_ref[size:, :] = vectors.astype(out_ref.dtype)


def token_kernel(gproj_a, gproj_b, x_ref, gres_ref, wqkv_ref, vec_ref, gtok_ref):
    for step in range(OWN_ALL // STEP):
        here = slice(step * STEP, (step + 1) * STEP)
        gproj_ref, steps = (gproj_a, gproj_b)[step * STEP * 2 // OWN_ALL], OWN_ALL // 2 // STEP
        rows = slice(step % steps * STEP, (step % steps + 1) * STEP)
        gnormed = nn(gproj_ref[rows, :], wqkv_ref[...])
        scaled, inverse = norm_parts(x_ref[here, :].astype(f32))
        gtok_ref[here, :] = gres_ref[here, :] + norm_back(gnormed, scaled, inverse, vec_ref[0:1, :])


def total_kernel(device_ref, *refs):
    *pieces, gqkv_ref, gout_ref, gvec_ref = refs
    total = pieces[0][...]
    for piece in pieces[1:]:
        total = total + piece[...].astype(f32)
    gqkv_ref[...] = total[:QKV_ROWS]
    gout_ref[...] = total[QKV_ROWS:G_ROWS]
    own = pltpu.roll(total[G_ROWS:], lax.rem(D - device_ref[0] * OUT_ROWS, D), 1)
    gvec_ref[...] = own[: gvec_ref.shape[0], : gvec_ref.shape[1]]


def call(kernel, args, outs, scratch, micros, mib):
    smem, vmem = pl.BlockSpec(memory_space=pltpu.SMEM), pl.BlockSpec(memory_space=pltpu.VMEM)
    return pl.pallas_call(
        kernel,
        out_shape=[jax.ShapeDtypeStruct(s, t) for s, t in outs],
        in_specs=[smem if a.dtype == jnp.int32 else vmem for a in args],
        out_specs=[vmem] * len(outs),
        scratch_shapes=[pltpu.VMEM(s, t) for s, t in scratch],
        compiler_params=pltpu.CompilerParams(vmem_limit_bytes=mib * 1024 * 1024),
        cost_estimate=pl.CostEstimate(flops=int(micros * 1.1e9), bytes_accessed=2**20, transcendentals=0),
    )(*args)


def swap(array, mask, other=None):
    count = lax.axis_size("dp") * lax.axis_size("tensor")
    masks = (mask, mask if other is None else other)
    return lax.ppermute(array, BOTH, [(device, device ^ masks[device % 2]) for device in range(count)])


ALONG_Z, ALONG_Y, ALONG_X, CORES = (16, 8, 24), 2, 4, 1
ALONG_XY = (ALONG_Y, ALONG_X, ALONG_Y ^ ALONG_X)


AT_XY = (ALONG_XY[2], ALONG_Y, ALONG_X)


def owners(device, swapped, line_first=True, turn=None, second_first=True):
    def one(second_core):
        first = ALONG_X if swapped and bool(second_core) == second_first else ALONG_Y
        plane = [0, first, first ^ ALONG_XY[2], ALONG_XY[2]]
        if not swapped:
            plane = [0, *AT_XY]
        line = [0, *ALONG_Z]
        if turn is not None and second_core != turn:
            line = [line[0], line[2], line[1], line[3]]
        return [m ^ o for o in plane for m in line] if line_first else [m ^ o for o in line for m in plane]

    core = device % 2
    first = jnp.where(core == 0, jnp.array(one(0)), jnp.array(one(1)))
    second = jnp.where(core == 0, jnp.array(one(1)), jnp.array(one(0))) ^ CORES
    return (device ^ jnp.concatenate([first, second])).astype(jnp.int32)


def gather(held, phase):
    return [held] + [swap(held, mask) for mask in phase]


def both_cores(pieces):
    return pieces + [swap(piece, CORES) for piece in pieces]


def wide(array):
    return array.astype(f32)


def add_all(total, others):
    for other in others:
        total = total + wide(other)
    return total


def after(array, *others):
    return lax.optimization_barrier((array,) + others)[0]


def neighbours(array, axis_name, width):
    count = lax.axis_size(axis_name)
    up = [(i, i + 1) for i in range(count - 1)]
    low = lax.ppermute(array[..., -width:, :], axis_name, up)
    high = lax.ppermute(array[..., :width, :], axis_name, [(b, a) for a, b in up])
    return low, high


def shards(tokens, valid, w_qkv, w_out, vectors, w_up, w_down, cotangent):
    devices_dp, devices_t = lax.axis_size("dp"), lax.axis_size("tensor")
    near = devices_dp == 8 and devices_t == 4
    rank = lax.axis_index("tensor")

    own_time = jnp.broadcast_to((jnp.arange(OWN) // FREQ)[None], (CLIPS, OWN)).reshape(-1)
    edge_time = jnp.arange(BAND) // FREQ + jnp.where(jnp.arange(BAND) < EDGE, -SHIFT, OWN // FREQ - SHIFT)
    edge_time = jnp.broadcast_to(edge_time[None], (CLIPS, BAND)).reshape(-1)
    time = jnp.concatenate([own_time, edge_time]) + rank * (OWN // FREQ)
    limit = valid * ROW_UNIT
    limit = jnp.concatenate([jnp.repeat(limit, OWN), jnp.repeat(limit, BAND)])
    keep = jnp.where((time >= 0) & (time < limit), 1.0, 0.0).astype(f32)
    keep = jnp.broadcast_to(keep[:, None], (ROWS, 128))

    if near:
        device = lax.axis_index("dp") * devices_t + rank
        own_near, own_far = owners(device, False), owners(device, True, second_first=False)
        own_down, own_up = owners(device, True, False, 0), owners(device, True, True, 1)
        block = pl.pallas_call(
            pack_kernel,
            out_shape=jax.ShapeDtypeStruct((A_ROWS + B_ROWS, D), bf16),
            in_specs=[pl.BlockSpec(memory_space=pl.ANY)] * 4,
            out_specs=pl.BlockSpec(memory_space=pltpu.VMEM),
            scratch_shapes=[pltpu.VMEM(vectors.shape, bf16), pltpu.SemaphoreType.DMA((4,))],
            compiler_params=pltpu.CompilerParams(vmem_limit_bytes=60 * 1024 * 1024),
        )(w_qkv.T, vectors, w_out.T, w_up)
        edges = neighbours(jnp.stack([tokens, cotangent]), "tensor", EDGE)
        line = gather(block[None], ALONG_Z)
        down = w_down.T[None]
        down = jnp.concatenate([down, swap(down, ALONG_Y, ALONG_X)], axis=0)
        down = [down, swap(down, ALONG_X, ALONG_Y)]
        line, down, keep, own_near, own_far, own_down, own_up = lax.optimization_barrier(
            (line, down, keep, own_near, own_far, own_down, own_up)
        )
        line, down = jnp.concatenate(line, axis=0), jnp.concatenate(down, axis=0)
        near_pieces = swap(line, ALONG_X, ALONG_Y)
        down = [down, swap(down, ALONG_Z[0], ALONG_Z[1])]
        near_pieces, down, edges = lax.optimization_barrier((near_pieces, down, edges))
        down = jnp.concatenate(down, axis=0)
        near_pieces = jnp.concatenate([line, near_pieces], axis=0)
        a_far = swap(near_pieces[:, :A_ROWS], ALONG_Y, ALONG_X)
        b_far = swap(near_pieces[:, A_ROWS:], ALONG_Y, ALONG_X)
        pieces = both_cores([near_pieces])
        a_pieces = [pieces[0], a_far, pieces[1], swap(a_far, CORES)]
        c_pieces = [down, swap(down, ALONG_Z[1], ALONG_Z[0])]
    else:
        own_near = own_far = own_down = own_up = jnp.arange(SLOTS, dtype=jnp.int32)
        edges = neighbours(jnp.stack([tokens, cotangent]), "tensor", EDGE)
        qkv, out, vec = (lax.all_gather(a, BOTH, axis=1, tiled=True).T for a in (w_qkv, w_out, vectors))
        vec = jnp.pad(vec, ((0, 0), (0, D - vec.shape[1])))
        up = lax.all_gather(lax.all_gather(w_up, "dp", axis=0, tiled=True), "tensor", axis=1, tiled=True)
        down = lax.all_gather(lax.all_gather(w_down, "dp", axis=1, tiled=True), "tensor", axis=0, tiled=True).T
        up, down = (
            a.reshape(SLOTS // CHUNKS, UP_ROWS, CHUNKS, D).transpose(0, 2, 1, 3).reshape(SLOTS, UP_ROWS, D)
            for a in (up, down)
        )
        a_slots = jnp.concatenate([a.reshape(SLOTS, -1, D) for a in (qkv, vec)], axis=1)
        b_slots = jnp.concatenate([out.reshape(SLOTS, -1, D), up], axis=1)
        a_pieces, b_pieces, c_pieces = (
            [a[i : i + PIECE] for i in range(0, SLOTS, PIECE)] for a in (a_slots, b_slots, down)
        )

    edges = jnp.concatenate(edges, axis=2).reshape(2, CLIPS * BAND, D)
    x = jnp.concatenate([tokens.reshape(OWN_ALL, D), edges[0]], axis=0)
    cot = jnp.concatenate([cotangent.reshape(OWN_ALL, D), edges[1]], axis=0)
    proj, probs, mixed, scaled, wqkv, vec = call(
        attend_kernel, [own_far, keep, x, *a_pieces],
        [
            ((ROWS, 3 * D), bf16), ((CLIPS * BANDS, 2, BAND, HALF), f32), ((ROWS, D), bf16), ((ROWS, D), bf16),
            ((3 * D, D), bf16), ((16, D), f32),
        ],
        [((D, 128), f32), ((HALF, HALF), bf16), ((BAND, HALF), f32), ((ROWS, D), bf16)],
        0.1, 16,
    )
    if near:
        b_far, c_pieces, proj = lax.optimization_barrier((b_far, c_pieces, proj))
        b_pieces = [pieces[0], b_far, pieces[1], swap(b_far, CORES)]
        c_pieces = both_cores(c_pieces)
    dn_kept, dn_sent, resid, hid, slope, second, branch_low, up_all, wout = call(
        up_kernel, [own_far, own_down, keep, cot, x, mixed, vec, *b_pieces],
        [
            ((NEAR, UP_ROWS, D), bf16), ((NEAR, UP_ROWS, D), bf16), ((ROWS, D), f32), ((ROWS, FF), bf16),
            ((ROWS, FF), bf16), ((ROWS, D), bf16), ((ROWS, D), bf16), ((D, FF), bf16), ((D, D), bf16),
        ],
        [
            ((CHUNKS, D, D), bf16), ((ROWS, 2 * D), f32), ((D, OWN_ALL), bf16), ((ROWS, D), f32), ((ROWS, D), bf16),
        ],
        8, 25,
    )
    up_kept, up_sent, gpre, down_all, colsum = call(
        down_kernel, [own_up, own_down, slope, second, branch_low, *c_pieces],
        [
            ((NEAR, UP_ROWS, D), bf16), ((NEAR, UP_ROWS, D), bf16), ((ROWS, FF), bf16), ((D, FF), bf16), ((8, D), f32),
        ],
        [((CHUNKS, D, D), bf16), ((ROWS, 2 * D), f32), ((D + 16, OWN_ALL), bf16)],
        8, 20,
    )
    if near:
        dn_sum = wide(dn_kept) + wide(after(swap(dn_sent, CORES), gpre))
        gpre, dn_far = lax.optimization_barrier((gpre, dn_sum[NEAR // 2 :].astype(bf16)))
    branch, gsec = call(
        sum_kernel, [hid, gpre, up_all, down_all], [((OWN_ALL, D), f32), ((ROWS, D), f32)], [], 0.1, 13,
    )
    if near:
        up_sum = wide(up_kept) + wide(after(swap(up_sent, CORES), gsec))
        up_far = up_sum[NEAR // 2 :].astype(bf16)
        gsec, up_far, dn_far = lax.optimization_barrier((gsec, up_far, dn_far))
    out, gres, gout, gmix, sums = call(
        finish_kernel, [keep, cot, mixed, resid, branch, gsec, wout, vec],
        [
            ((OWN_ALL, D), bf16), ((ROWS, D), f32), ((D, D), bf16), ((ROWS, D), bf16), ((8, D), f32),
        ],
        [((ROWS, D), bf16)],
        0.1, 16,
    )
    def attend_back(*clips):
        rows = len(clips) * OWN
        return call(
            functools.partial(back_kernel, clips), [gmix, proj, probs], [((rows, 3 * D), bf16)],
            [((HALF, HALF), bf16), ((len(clips) * BANDS, 2, BAND, HALF), bf16)], 0.1, 12,
        )[0]

    gproj_a, gproj_b = attend_back(0, 1), attend_back(2, 3)
    if near:
        up_arrived, gproj_a, gproj_b = lax.optimization_barrier((swap(up_far, ALONG_X, ALONG_Y), gproj_a, gproj_b))
        up_sum = up_sum[: NEAR // 2] + wide(up_arrived)
        up_near, gproj_a, gproj_b = lax.optimization_barrier((up_sum[PIECE:].astype(bf16), gproj_a, gproj_b))
    at_kept, *at_sent = call(
        project_kernel, [own_near, gproj_a, gproj_b, gout, scaled, wqkv, vec, sums, colsum],
        [((NEAR * G_ROWS + V_ROWS, D), bf16)] + [((AT_ROWS // PARTS, D), bf16)] * PARTS,
        [((3 * D, D), bf16), ((128, D), f32)],
        0.1, 16,
    )
    if near:
        up_arrived, at_sent[-1] = lax.optimization_barrier((swap(up_near, ALONG_Y, ALONG_X), at_sent[-1]))
        at_arrived = [swap(piece, CORES) for piece in at_sent]
        up_arrived, dn_arrived, at_arrived, gproj_a = lax.optimization_barrier(
            (up_arrived, swap(dn_far, ALONG_Z[1], ALONG_Z[0]), at_arrived, gproj_a)
        )
    (gtok,) = call(
        token_kernel, [gproj_a, gproj_b, x, gres, wqkv, vec], [((OWN_ALL, D), f32)], [], 0.1, 12,
    )
    if near:
        at_sum, *at_rest = call(
            functools.partial(share_kernel, end_to_end=True), [at_kept, *at_arrived],
            [((PIECE * G_ROWS + V_ROWS, D), t) for t in (f32, bf16, bf16, bf16)], [], 0.1, 8,
        )
        dn_sum = dn_sum[: NEAR // 2] + wide(dn_arrived)
        up_sum = up_sum[:PIECE] + wide(up_arrived)
        at_arrived = [swap(piece, mask) for piece, mask in zip(at_rest, AT_XY)]
        ff_arrived = jnp.concatenate([dn_sum[PIECE:], up_sum[2:]], axis=0).astype(bf16)
        ff_arrived = swap(ff_arrived, ALONG_Z[0], ALONG_Z[1])
        ff_arrived, gtok = lax.optimization_barrier((ff_arrived, gtok))
        dn_sum, up_sum = dn_sum[:PIECE] + wide(ff_arrived[:PIECE]), up_sum[:2] + wide(ff_arrived[PIECE:])
        up_arrived = swap(up_sum[1:].astype(bf16), ALONG_Z[1], ALONG_Z[0])
        dn_rest = dn_sum.astype(bf16)
        dn_arrived = [
            swap(dn_rest[3:], ALONG_XY[2]), swap(dn_rest[1:2], ALONG_Y, ALONG_X), swap(dn_rest[2:3], ALONG_X, ALONG_Y),
        ]
        at_arrived, up_arrived = lax.optimization_barrier((at_arrived, up_arrived))
        at_sum, *at_rest = call(
            share_kernel, [at_sum, *at_arrived],
            [((G_ROWS + V_ROWS, D), t) for t in (f32, bf16, bf16, bf16)], [], 0.1, 8,
        )
        up_sum = up_sum[0] + wide(up_arrived)[0]
        dn_sum = add_all(dn_sum[:1], dn_arrived)[0]
        at_arrived = [swap(piece, mask) for piece, mask in zip(at_rest, ALONG_Z)]
        g_qkv, g_out, g_vec = call(
            total_kernel, [device.astype(jnp.int32)[None], at_sum, *at_arrived],
            [((QKV_ROWS, D), f32), ((OUT_ROWS, D), f32), (vectors.shape, f32)], [], 0.1, 4,
        )
    if near:
        g_up, g_down = up_sum, dn_sum.T
        g_qkv, g_out = g_qkv.T, g_out.T
    else:
        at_grads = jnp.concatenate([at_kept[: NEAR * G_ROWS], *at_sent], axis=0)
        at_grads = at_grads[: SLOTS * G_ROWS].reshape(SLOTS, G_ROWS, D)

        def whole(array):
            blocks = array.reshape(SLOTS // CHUNKS, CHUNKS, UP_ROWS, D).transpose(0, 2, 1, 3)
            return blocks.reshape(D, FF)

        g_up = lax.psum_scatter(whole(jnp.concatenate([up_kept, up_sent], axis=0)), "dp", scatter_dimension=0, tiled=True)
        g_up = lax.psum_scatter(g_up, "tensor", scatter_dimension=1, tiled=True).astype(f32)
        g_down = lax.psum_scatter(whole(jnp.concatenate([dn_kept, dn_sent], axis=0)).T, "dp", scatter_dimension=1, tiled=True)
        g_down = lax.psum_scatter(g_down, "tensor", scatter_dimension=0, tiled=True).astype(f32)

        def owned(array):
            return lax.psum_scatter(array.astype(f32), BOTH, scatter_dimension=1, tiled=True)

        g_qkv = owned(at_grads[:, :QKV_ROWS].reshape(-1, D).T)
        g_out = owned(at_grads[:, QKV_ROWS:].reshape(-1, D).T)
        g_vec = owned(at_kept[NEAR * G_ROWS :][: vectors.shape[0]])
    shape = tokens.shape
    return (out.reshape(shape), gtok.reshape(shape), g_qkv, g_out, g_vec, g_up, g_down)


def solution(mesh):
    placed = (
        P("dp", "tensor", None),
        P("dp"),
        P(None, BOTH),
        P(None, BOTH),
        P(None, BOTH),
        P("dp", "tensor"),
        P("tensor", "dp"),
        P("dp", "tensor", None),
    )
    return jax.shard_map(
        shards,
        mesh=mesh,
        in_specs=placed,
        out_specs=(
            P("dp", "tensor", None),
            P("dp", "tensor", None),
            P(None, BOTH),
            P(None, BOTH),
            P(None, BOTH),
            P("dp", "tensor"),
            P("tensor", "dp"),
        ),
        check_vma=False,
    )
```
